32 devices in a mesh: row: 4 (over x, core), col: 8 (over z, y).
Axes of the slice: x: 2, y: 2, z: 4, core: 2. Of those that a mesh axis runs over, the one named last changes fastest.
Arguments:
- atom_feat: bfloat16 [8192, 128], P(('row', 'col')), may hold values from -6 to 6
- atom_token: int32 [8192], P(('row', 'col')), may hold values from 0 to 1023, as said below
- w_atom_qkv: bfloat16 [128, 384], replicated, may hold values from -0.5 to 0.5
- w_atom_out: bfloat16 [128, 128], replicated, may hold values from -0.5 to 0.5
- w_atom_up: bfloat16 [128, 768], replicated, may hold values from -0.5 to 0.5
- pair_repr: bfloat16 [1024, 4, 256, 128], P('row', None, 'col'), may hold values from -6 to 6
- w_bias: float32 [128, 16], replicated, may hold values from -16 to 16
- w_query: bfloat16 [768, 768], replicated, may hold values from -0.21875 to 0.21875
- w_kv: bfloat16 [768, 1536], replicated, may hold values from -0.21875 to 0.21875
- w_gate: bfloat16 [768, 768], replicated, may hold values from -0.21875 to 0.21875
- w_out: bfloat16 [768, 768], replicated, may hold values from -0.21875 to 0.21875
- w_down: bfloat16 [768, 128], replicated, may hold values from -0.21875 to 0.21875
Outputs:
- token_out: bfloat16 [1024, 768], P('row', 'col')
- atom_final: bfloat16 [8192, 128], P(('row', 'col'))
The draws below stay inside these ranges and needn't reach their ends.
Inputs may be any that keep to these rules, and one draw needn't show every extreme that they name: atom_token never falls along the atoms; the atoms held by the device with index r along row name only tokens r*256 to r*256 + 255, and every token is named by at least one atom.
All inputs are finite; a program needn't handle non-finite values.
Results may differ from the reference program's by a relative error of at most 0.017.
The reference program's roundings to bfloat16 on the way count: a program that leaves them out, or rounds other values in their place, can miss the bound.
Values may be sent and summed in bfloat16 or wider, within the bound.
No kernel may reach another device: no remote copies, remote signals or barrier semaphores. Data moves between devices by JAX's collectives and lax.ppermute only.
A program may use at most 192 MiB of HBM per device.

```python
import jax
import jax.numpy as jnp
from jax import lax

D = 768
HEADS = 16
DH = 48
CP = 128
CA = 128
AHEADS = 4
ADH = 32
QBLOCK = 32
KWIN = 128
HALO = 48
TOK_ROW = 256
NTOK = 1024
ATOM_ROW = 2048
ATOMS = 8192
N_ROW = 4


def draw_atom_token(key, part):
    key = jax.random.fold_in(key, 11)
    first_key, second_key = jax.random.split(key)
    groups = NTOK // TOK_ROW
    extra = ATOM_ROW - TOK_ROW
    first = jax.random.randint(first_key, (groups, extra), 0, TOK_ROW)
    second = jax.random.randint(second_key, (groups, extra), 0, TOK_ROW)
    chosen = jnp.minimum(first, second)
    every = jnp.broadcast_to(jnp.arange(TOK_ROW, dtype=jnp.int32)[None, :], (groups, TOK_ROW))
    joined = jnp.sort(jnp.concatenate([every, chosen.astype(jnp.int32)], axis=1), axis=1)
    offset = (jnp.arange(groups, dtype=jnp.int32) * TOK_ROW)[:, None]
    return (joined + offset).reshape(-1).astype(jnp.int32)


def draw_w_bias(key, part):
    key = jax.random.fold_in(key, 12)
    base_key, scale_key = jax.random.split(key)
    values = jnp.clip(jax.random.normal(base_key, (CP, HEADS), jnp.float32), -3.0, 3.0) / CP ** 0.5
    scales = jnp.exp(jax.random.uniform(scale_key, (1, HEADS), jnp.float32, -0.7, 1.1))
    return jnp.clip(values * scales, -16.0, 16.0).astype(jnp.float32)


def level_of(key, shape, pieces, smallest, largest):
    loudness = 1.0
    for dim, blocks in pieces:
        draws = jax.random.uniform(jax.random.fold_in(jax.random.fold_in(key, 6), dim), (blocks,), jnp.float32, smallest / len(pieces), largest / len(pieces))
        loudness = loudness * jnp.repeat(jnp.exp(draws), shape[dim] // blocks).reshape((-1,) + (1,) * (len(shape) - 1 - dim))
    return loudness


def normal_values(rng, shape, scale, reach, cuts=(), held_as=jnp.bfloat16):
    factor_of = level_of(rng, shape, cuts, -0.22, 0.18) if cuts else 1.0
    result = jax.random.normal(rng, shape, jnp.float32) * scale * factor_of
    return jnp.minimum(jnp.maximum(result, -reach), reach).astype(held_as)


def setup_inputs(seed: int = 0) -> dict:
    splits = jax.random.split(jax.random.key(seed), 13)
    return {
        "atom_feat": normal_values(splits[0], (ATOMS, CA), 1.0, 6.0, ((0, 32),)),
        "atom_token": draw_atom_token(jax.random.fold_in(splits[12], 71), 0),
        "w_atom_qkv": normal_values(splits[2], (CA, 3 * CA), CA ** -0.5, 0.5),
        "w_atom_out": normal_values(splits[3], (CA, CA), CA ** -0.5, 0.5),
        "w_atom_up": normal_values(splits[4], (CA, D), CA ** -0.5, 0.5),
        "pair_repr": normal_values(splits[5], (NTOK, N_ROW, TOK_ROW, CP), 1.0, 6.0, ((0, 4), (2, 8))),
        "w_bias": draw_w_bias(jax.random.fold_in(splits[12], 71), 0),
        "w_query": normal_values(splits[7], (D, D), D ** -0.5, 0.21875),
        "w_kv": normal_values(splits[8], (D, 2 * D), D ** -0.5, 0.21875),
        "w_gate": normal_values(splits[9], (D, D), D ** -0.5, 0.21875),
        "w_out": normal_values(splits[10], (D, D), D ** -0.5, 0.21875),
        "w_down": normal_values(splits[11], (D, CA), D ** -0.5, 0.21875),
    }


EPS = 1e-05

def layer_norm(values):
    center = lax.optimization_barrier(jnp.mean(values, axis=-1, keepdims=True))
    spread = lax.optimization_barrier(jnp.mean(values * values, axis=-1, keepdims=True)) - center * center
    return (values - center) / jnp.sqrt(spread + EPS)

def atom_layer(atom_feat, w_atom_qkv, w_atom_out):
    total = atom_feat.shape[0]
    atom_proj = jnp.dot(atom_feat, w_atom_qkv, preferred_element_type=jnp.float32).astype(jnp.bfloat16)
    queries = atom_proj[:, :CA]
    keyvals = jnp.pad(atom_proj[:, CA:], ((HALO, HALO), (0, 0)))
    blocks = total // QBLOCK
    window = (jnp.arange(blocks)[:, None] * QBLOCK + jnp.arange(KWIN)[None, :]).astype(jnp.int32)
    position = window - HALO
    valid = (position >= 0) & (position < total)
    near = keyvals[window]
    near_keys = near[..., :CA].reshape(blocks, KWIN, AHEADS, ADH).astype(jnp.float32)
    near_vals = near[..., CA:].reshape(blocks, KWIN, AHEADS, ADH).astype(jnp.float32)
    block_q = queries.reshape(blocks, QBLOCK, AHEADS, ADH).astype(jnp.float32)
    scores = jnp.einsum('bqhd,bkhd->bhqk', block_q, near_keys) / ADH ** 0.5
    scores = jnp.where(valid[:, None, None, :], scores, -1e+30)
    top = lax.optimization_barrier(jnp.max(scores, axis=-1, keepdims=True))
    expo = jnp.exp(scores - top)
    atom_weights = expo.astype(jnp.bfloat16)
    denom = lax.optimization_barrier(jnp.sum(expo, axis=-1))
    context = jnp.einsum('bhqk,bkhd->bqhd', atom_weights.astype(jnp.float32), near_vals)
    context = context / jnp.transpose(denom, (0, 2, 1))[..., None]
    atom_ctx = context.reshape(total, CA).astype(jnp.bfloat16)
    mixed = atom_feat.astype(jnp.float32) + jnp.dot(atom_ctx, w_atom_out, preferred_element_type=jnp.float32)
    return mixed.astype(jnp.bfloat16)

def reference(atom_feat, atom_token, w_atom_qkv, w_atom_out, w_atom_up, pair_repr, w_bias, w_query, w_kv, w_gate, w_out, w_down):
    atom_out = atom_layer(atom_feat, w_atom_qkv, w_atom_out)
    atom_up = jax.nn.relu(jnp.dot(atom_out, w_atom_up, preferred_element_type=jnp.float32)).astype(jnp.bfloat16)
    token_sum = jax.ops.segment_sum(atom_up.astype(jnp.float32), atom_token, num_segments=NTOK)
    counts = jax.ops.segment_sum(jnp.ones(atom_token.shape, jnp.float32), atom_token, num_segments=NTOK)
    token_act = token_sum / counts[:, None]
    normed = layer_norm(token_act).astype(jnp.bfloat16)
    queries = jnp.dot(normed, w_query, preferred_element_type=jnp.float32).astype(jnp.bfloat16)
    keyvals = jnp.dot(normed, w_kv, preferred_element_type=jnp.float32).astype(jnp.bfloat16)
    gating = jax.nn.sigmoid(jnp.dot(normed, w_gate, preferred_element_type=jnp.float32))
    all_keys = keyvals[:, :D].reshape(NTOK, HEADS, DH).astype(jnp.float32)
    all_vals = keyvals[:, D:].reshape(NTOK, HEADS, DH).astype(jnp.float32)
    tiles = pair_repr.reshape(N_ROW, TOK_ROW, NTOK, CP)

    def one_block(inputs):
        tile, block_q, block_gate, block_act = inputs
        pair_normed = layer_norm(tile.astype(jnp.float32)).astype(jnp.bfloat16)
        pair_bias = jnp.dot(pair_normed.reshape(-1, CP), w_bias.astype(jnp.bfloat16), preferred_element_type=jnp.float32).astype(jnp.bfloat16)
        pair_bias = pair_bias.reshape(TOK_ROW, NTOK, HEADS)
        query_heads = block_q.reshape(TOK_ROW, HEADS, DH).astype(jnp.float32)
        scores = jnp.einsum('qhd,khd->hqk', query_heads, all_keys) / DH ** 0.5
        scores = scores + jnp.transpose(pair_bias, (2, 0, 1)).astype(jnp.float32)
        top = lax.optimization_barrier(jnp.max(scores, axis=-1, keepdims=True))
        expo = jnp.exp(scores - top)
        token_weights = expo.astype(jnp.bfloat16)
        denom = lax.optimization_barrier(jnp.sum(expo, axis=-1))
        context = jnp.einsum('hqk,khd->qhd', token_weights.astype(jnp.float32), all_vals)
        context = context / jnp.transpose(denom)[:, :, None]
        gated = (context.reshape(TOK_ROW, D) * block_gate).astype(jnp.bfloat16)
        updated = block_act + jnp.dot(gated, w_out, preferred_element_type=jnp.float32)
        return updated.astype(jnp.bfloat16)
    token_out = lax.map(one_block, (tiles, queries.reshape(N_ROW, TOK_ROW, D), gating.reshape(N_ROW, TOK_ROW, D), token_act.reshape(N_ROW, TOK_ROW, D)))
    token_out = token_out.reshape(NTOK, D)
    token_down = jnp.dot(token_out, w_down, preferred_element_type=jnp.float32).astype(jnp.bfloat16)
    atom_final = atom_out.astype(jnp.float32) + token_down[atom_token].astype(jnp.float32)
    return (token_out, atom_final.astype(jnp.bfloat16))
```

```python
import functools

import jax
import jax.numpy as jnp
from jax import lax
from jax.experimental import pallas as pl
from jax.experimental.pallas import tpu as pltpu
from jax.sharding import PartitionSpec as P

AHEADS = 4
QBLOCK = 32
KWIN = 128
HALO = 48
LANES = 128
AHEAD = 4
PAD_ROWS = 16
EDGE_BLOCKS = 2
EPS = 1e-05
LOG2_E = 1.4426950408889634
F32 = jnp.float32
BF16 = jnp.bfloat16
MIB = 1024 * 1024

NT = (((1,), (1,)), ((), ()))
NN = (((1,), (0,)), ((), ()))
TN = (((0,), (0,)), ((), ()))


def mul(a, b, dims=NN):
    return lax.dot_general(a, b, dims, preferred_element_type=F32)


def call(kernel, out_shape, vmem_mib, **kwargs):
    return pl.pallas_call(
        kernel,
        out_shape=out_shape,
        compiler_params=pltpu.CompilerParams(vmem_limit_bytes=vmem_mib * MIB),
        **kwargs,
    )


def shape_of(shape, dtype):
    return jax.ShapeDtypeStruct(shape, dtype)


def lane_iota(shape):
    return lax.broadcasted_iota(jnp.int32, shape, len(shape) - 1)


def in_hbm(*arrays):
    return tuple(pltpu.with_memory_space_constraint(x, pltpu.HBM) for x in arrays)


def load_all(sources, targets, sems):
    copies = [
        pltpu.make_async_copy(source, target, sems.at[i])
        for i, (source, target) in enumerate(zip(sources, targets))
    ]
    for copy in copies:
        copy.start()
    return copies


def wait_all(copies):
    for copy in copies:
        copy.wait()


def pack_kernel(place_ref, own_ref, token_ref, far_ref, far_token_ref, after_ref, out_ref):
    del after_ref
    atom_count = own_ref.shape[0]
    token_rows = token_ref.shape[0]
    blank = jnp.zeros((PAD_ROWS - token_rows, LANES), F32)
    for k, (feat, token) in enumerate(((own_ref, token_ref), (far_ref, far_token_ref))):
        out_ref[k, :atom_count, :] = feat[...]
        names = (token[...] - place_ref[1]).astype(F32)
        out_ref[k, atom_count:, :] = jnp.concatenate([names, blank], axis=0).astype(BF16)


def edge_kernel(place_ref, bias_ref, *refs):
    packets, (sent_ref, atoms_ref, first_ref, second_ref) = refs[:-4], refs[-4:]
    sent_ref[...] = bias_ref[...].astype(BF16)
    col_count, packet_rows, _ = atoms_ref.shape
    atom_count = packet_rows - PAD_ROWS
    for k, packet in enumerate(packets):
        for j in range(2):
            atoms_ref[place_ref[10] ^ (k + j * (col_count // 2))] = packet[j]
    tail = atoms_ref[col_count - 1, atom_count - HALO : atom_count, :]
    head = atoms_ref[0, :HALO, :]
    even = place_ref[7] == 0
    first_ref[...] = jnp.where(even, tail, head)
    second_ref[...] = jnp.where(even, head, tail)


def attend(query_of, window_of, blocks, valid_of=None):
    channels = query_of(0).shape[1]
    head_size = channels // AHEADS
    head_of = lane_iota((QBLOCK, channels)) // head_size
    picks = [head_of == h for h in range(AHEADS)]
    scores = []
    for b in range(blocks):
        query = query_of(b)
        stacked = jnp.concatenate(
            [jnp.where(pick, query, jnp.zeros_like(query)) for pick in picks], axis=0
        )
        scores.append(mul(window_of(b, 1), stacked, NT))
    blank = jnp.zeros((KWIN, channels), BF16)
    row = lax.broadcasted_iota(jnp.int32, (PAD_ROWS, channels), 0)
    pair_rows = jnp.where(row < 2, 1.0, 0.0).astype(BF16)
    sum_rows = jnp.concatenate([blank[:PAD_ROWS], pair_rows], axis=1)
    contexts = []
    for b in range(blocks):
        score = scores[b]
        if valid_of is not None:
            score = jnp.where(valid_of(b, score.shape), score, -1e30)
        score = score - jnp.max(score, axis=0, keepdims=True)
        expo = jnp.exp2(score * (LOG2_E / head_size**0.5))
        denom = jnp.sum(expo, axis=0, keepdims=True)
        denom_high = denom.astype(BF16).astype(F32)
        sums = jnp.where(row == 0, denom_high, jnp.where(row == 1, denom - denom_high, 0.0))
        weights = jnp.concatenate([expo.astype(BF16), sums.astype(BF16)], axis=0)
        values = jnp.concatenate([window_of(b, 2), blank], axis=1)
        mixed = mul(weights, jnp.concatenate([values, sum_rows], axis=0), TN)
        context = mixed[:QBLOCK]
        for h in range(1, AHEADS):
            pick = jnp.concatenate([picks[h]] * 2, axis=1)
            context = jnp.where(pick, mixed[h * QBLOCK : (h + 1) * QBLOCK], context)
        contexts.append((context[:, :channels] / context[:, channels:]).astype(BF16))
    return contexts


def inner_kernel(
    place_ref,
    atoms_ref,
    w_qkv_ref,
    w_out_ref,
    w_up_ref,
    w_query_hbm,
    w_kv_hbm,
    total_ref,
    count_ref,
    my_ref,
    w_query_ref,
    w_kv_ref,
    proj_ref,
    ctx_ref,
    up_ref,
    hot_ref,
    sems,
):
    loads = load_all((w_query_hbm, w_kv_hbm), (w_query_ref, w_kv_ref), sems)
    col_count, packet_rows, channels = atoms_ref.shape
    atom_count = packet_rows - PAD_ROWS
    row_atoms = col_count * atom_count
    tok_rows = total_ref.shape[0]
    blocks = row_atoms // QBLOCK - 2 * EDGE_BLOCKS
    step_blocks = max(n for n in range(1, 21) if blocks % n == 0)
    edge = EDGE_BLOCKS * QBLOCK
    for c in range(col_count):
        proj = mul(atoms_ref[c, :atom_count, :], w_qkv_ref[...])
        proj_ref[c * atom_count : (c + 1) * atom_count, :] = proj.astype(BF16)
    ctx_ref[:edge, :] = jnp.zeros((edge, channels), BF16)
    ctx_ref[row_atoms - edge :, :] = jnp.zeros((edge, channels), BF16)

    def step(i, carry):
        first = i * (step_blocks * QBLOCK) + edge

        def query_of(b):
            start = pl.multiple_of(first + b * QBLOCK, QBLOCK)
            return proj_ref[pl.ds(start, QBLOCK), :channels]

        def window_of(b, part):
            start = pl.multiple_of(first + b * QBLOCK - HALO, PAD_ROWS)
            return proj_ref[pl.ds(start, KWIN), part * channels : (part + 1) * channels]

        for b, context in enumerate(attend(query_of, window_of, step_blocks)):
            ctx_ref[pl.ds(pl.multiple_of(first + b * QBLOCK, QBLOCK), QBLOCK), :] = context
        return carry

    lax.fori_loop(0, blocks // step_blocks, step, 0)
    counts = jnp.zeros((tok_rows, LANES), F32)
    token = lax.broadcasted_iota(jnp.int32, (tok_rows, LANES), 0).astype(F32)
    lane = lane_iota((1, LANES))
    chunks = row_atoms // LANES
    for c in range(col_count):
        rows = slice(c * atom_count, (c + 1) * atom_count)
        names = atoms_ref[c, atom_count:, :].astype(F32)
        for k in range(atom_count // LANES):
            name = names[k : k + 1, :]
            counts = counts + jnp.where(name == token, 1.0, 0.0)
            chunk = c * (atom_count // LANES) + k
            if chunk == 0:
                name = jnp.where(lane < edge, -1.0, name)
            if chunk == chunks - 1:
                name = jnp.where(lane >= LANES - edge, -1.0, name)
            hot = jnp.where(name == token, 1.0, 0.0)
            hot_ref[:, chunk * LANES : (chunk + 1) * LANES] = hot.astype(BF16)
        atom_out = atoms_ref[c, :atom_count, :].astype(F32) + mul(ctx_ref[rows, :], w_out_ref[...])
        atom_out = atom_out.astype(BF16)
        ctx_ref[rows, :] = atom_out
        up_ref[rows, :] = jnp.maximum(mul(atom_out, w_up_ref[...]), 0.0).astype(BF16)
    total_ref[...] = mul(hot_ref[...], up_ref[...])
    count_ref[...] = jnp.broadcast_to(jnp.sum(counts, axis=-1, keepdims=True), counts.shape)
    mine = place_ref[0]
    start = pl.multiple_of(mine * atom_count, atom_count)
    my_ref[:atom_count, :] = ctx_ref[pl.ds(start, atom_count), :]
    my_ref[atom_count:, :] = atoms_ref[mine, atom_count:, :]
    wait_all(loads)


def bias_kernel(place_ref, pair_ref, w_ref, after_ref, *refs, place, chunk, loads):
    del after_ref
    sources, out_ref, targets = refs[:loads], refs[loads], refs[loads + 1 : 2 * loads + 1]
    cells_ref, sems, load_sems = refs[2 * loads + 1 :]
    queries, rows, share, width = cells_ref.shape
    keys = rows * share
    heads = w_ref.shape[0]
    count = queries // chunk
    base = place_ref[place]

    def load(i):
        start = pl.multiple_of(i * chunk, chunk)
        return pltpu.make_async_copy(
            pair_ref.at[pl.ds(pl.multiple_of(base + start, chunk), chunk)],
            cells_ref.at[pl.ds(start, chunk)],
            sems.at[i],
        )

    for i in range(AHEAD):
        load(i).start()
    extra = load_all(sources, targets, load_sems)
    weights = w_ref[...].astype(BF16)
    weight_sum = jnp.sum(weights.astype(F32), axis=1, keepdims=True)
    mean_of = jnp.full((heads, width), 1.0 / width, BF16)
    left = jnp.concatenate([weights, mean_of], axis=0)
    left = jnp.concatenate([left, left], axis=1)
    row = lax.broadcasted_iota(jnp.int32, (keys, 2 * keys), 0)
    lane = lane_iota((keys, 2 * keys))
    diagonal = (lane == row) | (lane == row + keys)
    blank = jnp.zeros((keys, width), BF16)

    def step(i, carry):
        load(i).wait()

        @pl.when(i + AHEAD < count)
        def _():
            load(i + AHEAD).start()

        start = pl.multiple_of(i * chunk, chunk)
        for q in range(0, chunk, 2):
            one = cells_ref[start + q].reshape(keys, width)
            two = cells_ref[start + q + 1].reshape(keys, width)
            held = jnp.concatenate(
                [
                    jnp.concatenate([one, blank], axis=1),
                    jnp.concatenate([blank, two], axis=1),
                ],
                axis=0,
            )
            streamed = jnp.concatenate([left, jnp.concatenate([one, two], axis=1)], axis=0)
            found = mul(streamed, held, NT)
            dots, center = found[:heads], found[heads : 2 * heads]
            squares = jnp.where(diagonal, found[2 * heads :], 0.0)
            spread = jnp.sum(squares, axis=0, keepdims=True) * (1.0 / width)
            spread = spread - center * center
            bias = (dots - center * weight_sum) * lax.rsqrt(spread + EPS)
            bias = bias.astype(BF16).astype(F32)
            out_ref[:, start + q, :] = bias[:, :keys]
            out_ref[:, start + q + 1, :] = bias[:, keys:]
        return carry

    lax.fori_loop(0, count, step, 0)
    wait_all(extra)


def pool_kernel(
    place_ref,
    atoms_ref,
    total_ref,
    count_ref,
    inner_ref,
    first_ref,
    second_ref,
    w_qkv_ref,
    w_out_ref,
    w_up_ref,
    mine_ref,
    half_ref,
    normed_out_ref,
    act_out_ref,
    my_ref,
    act_ref,
    normed_ref,
    *,
    all_atoms,
):
    col_count, packet_rows, channels = atoms_ref.shape
    atom_count = packet_rows - PAD_ROWS
    row_atoms = col_count * atom_count
    tok_rows, width = total_ref.shape
    slices, share = mine_ref.shape[:2]
    edge = EDGE_BLOCKS * QBLOCK
    near = edge + HALO
    first = atoms_ref[0, :near, :]
    final = atoms_ref[col_count - 1, atom_count - near : atom_count, :]
    contexts = []
    even = place_ref[7] == 0
    before = jnp.where(even, second_ref[...], first_ref[...])
    after = jnp.where(even, first_ref[...], second_ref[...])
    for wide, base in (
        (jnp.concatenate([before, first], axis=0), -HALO),
        (jnp.concatenate([final, after], axis=0), row_atoms - near),
    ):
        proj = mul(wide, w_qkv_ref[...]).astype(BF16)

        def query_of(b):
            return proj[HALO + b * QBLOCK : HALO + (b + 1) * QBLOCK, :channels]

        def window_of(b, part):
            return proj[b * QBLOCK : b * QBLOCK + KWIN, part * channels : (part + 1) * channels]

        def valid_of(b, shape):
            position = place_ref[1] + (base + b * QBLOCK)
            position = position + lax.broadcasted_iota(jnp.int32, shape, 0)
            return (position >= 0) & (position < all_atoms)

        contexts += attend(query_of, window_of, EDGE_BLOCKS, valid_of)
    feat = jnp.concatenate([first[:edge], final[HALO:]], axis=0).astype(F32)
    atom_out = feat + mul(jnp.concatenate(contexts, axis=0), w_out_ref[...])
    atom_out = atom_out.astype(BF16)
    up = jnp.maximum(mul(atom_out, w_up_ref[...]), 0.0).astype(BF16)
    token = lax.broadcasted_iota(jnp.int32, (tok_rows, LANES), 0).astype(F32)
    name_first = atoms_ref[0, atom_count:, :].astype(F32)[:1]
    last_row = atom_count // LANES - 1
    name_final = atoms_ref[col_count - 1, atom_count:, :].astype(F32)[last_row : last_row + 1]
    name = jnp.where(lane_iota((1, LANES)) < edge, name_first, name_final)
    hot = jnp.where(name == token, 1.0, 0.0).astype(BF16)
    token_act = (total_ref[...] + mul(hot, up)) / count_ref[:, :1]
    center = jnp.sum(token_act, axis=-1, keepdims=True) * (1.0 / width)
    spread = jnp.sum(token_act * token_act, axis=-1, keepdims=True) * (1.0 / width)
    spread = spread - center * center
    normed = ((token_act - center) / jnp.sqrt(spread + EPS)).astype(BF16)
    normed_ref[...] = normed
    act_ref[...] = token_act
    for k in range(slices):
        mine_ref[k] = normed_ref[pl.ds(pl.multiple_of(place_ref[2 + k], share), share), :]
    out_share = act_out_ref.shape[0]
    start = pl.multiple_of(place_ref[6], out_share)
    normed_out_ref[...] = normed_ref[pl.ds(start, out_share), :]
    act_out_ref[...] = act_ref[pl.ds(start, out_share), :]
    inner = inner_ref[:atom_count, :]
    col = place_ref[0]
    my_ref[:edge, :] = jnp.where(col == 0, atom_out[:edge], inner[:edge])
    if atom_count > 2 * edge:
        my_ref[edge : atom_count - edge, :] = inner[edge : atom_count - edge]
    my_ref[atom_count - edge : atom_count, :] = jnp.where(
        col == col_count - 1, atom_out[edge:], inner[atom_count - edge :]
    )
    my_ref[atom_count:, :] = inner_ref[atom_count:, :]
    half = half_ref.shape[0]
    half_ref[...] = normed_ref[pl.ds(pl.multiple_of(place_ref[4], half), half), :]


def query_kernel(half_ref, normed_ref, w_query_ref, w_gate_hbm, query_ref, gate_ref, w_gate_ref, sem):
    load = pltpu.make_async_copy(w_gate_hbm, w_gate_ref, sem)
    load.start()
    query_ref[...] = mul(half_ref[...], w_query_ref[...]).astype(BF16)
    load.wait()
    gate_ref[...] = jax.nn.sigmoid(mul(normed_ref[...], w_gate_ref[...]))


def token_kernel(place_ref, query_ref, w_kv_ref, kept_ref, swapped_ref, *refs, row_count, groups):
    parts, refs = refs[:row_count], refs[row_count:]
    w_out_hbm, w_down_hbm, *refs = refs
    out_refs, refs = refs[:groups], refs[groups:]
    w_out_ref, w_down_ref, keys_ref, packet_ref, sems = refs
    loads = load_all((w_out_hbm, w_down_hbm), (w_out_ref, w_down_ref), sems)
    for k, part in enumerate(parts):
        for i in range(2):
            keys_ref[i, place_ref[8] ^ k] = part[i]
    heads, tok_rows, part_keys = kept_ref.shape
    key_count = 2 * part_keys
    width = query_ref.shape[1]
    head_size = width // heads
    share = out_refs[0].shape[0]
    keyvals = mul(keys_ref[...].reshape(key_count, width), w_kv_ref[...]).astype(BF16)
    stats = jnp.zeros((tok_rows, LANES), F32)
    lane = lane_iota((tok_rows, LANES))
    tiles = [jnp.zeros((tok_rows, LANES), F32)] * (width // LANES)
    tile_lane = lane_iota((tok_rows, LANES))
    windows = []
    scores = []
    for h in range(heads):
        low = h * head_size // LANES * LANES
        high = min(width, -(-(h + 1) * head_size // LANES) * LANES)
        windows.append((low, high))
        chan = lane_iota((tok_rows, high - low)) + low
        inside = (chan >= h * head_size) & (chan < (h + 1) * head_size)
        query = query_ref[:, low:high]
        query = jnp.where(inside, query, jnp.zeros_like(query))
        scores.append(mul(query, keyvals[:, low:high], NT))
    for h, (low, high) in enumerate(windows):
        score = scores[h] * (1.0 / head_size**0.5)
        score = score + jnp.concatenate([kept_ref[h], swapped_ref[h].astype(F32)], axis=1)
        top = jnp.max(score, axis=-1, keepdims=True)
        top_high = top.astype(BF16).astype(F32)
        top_low = (top - top_high).astype(BF16).astype(F32)
        expo = jnp.exp(score - (top_high + top_low))
        denom = jnp.sum(expo, axis=-1, keepdims=True)
        denom_high = denom.astype(BF16).astype(F32)
        stats = jnp.where(lane == h, top_high, stats)
        stats = jnp.where(lane == heads + h, top_low, stats)
        stats = jnp.where(lane == 2 * heads + h, denom_high, stats)
        stats = jnp.where(lane == 3 * heads + h, denom - denom_high, stats)
        mixed = mul(expo.astype(BF16), keyvals[:, width + low : width + high])
        for tile in range(low // LANES, high // LANES):
            chan = tile_lane + tile * LANES
            inside = (chan >= h * head_size) & (chan < (h + 1) * head_size)
            part = mixed[:, tile * LANES - low : (tile + 1) * LANES - low]
            tiles[tile] = jnp.where(inside, part, tiles[tile])
    for tile, values in enumerate(tiles):
        lanes = slice(tile * LANES, (tile + 1) * LANES)
        packet_ref[:, lanes] = values.astype(BF16)
    packet_ref[:, width:] = stats.astype(BF16)
    for k, out_ref in enumerate(out_refs):
        start = pl.multiple_of((place_ref[9] ^ k) * share, share)
        out_ref[...] = packet_ref[pl.ds(start, share), :]
    wait_all(loads)


def merge_kernel(*refs, heads, groups):
    part_refs = refs[:groups]
    gate_ref, act_ref, w_out_ref, w_down_ref, out_ref = refs[groups:]
    share = part_refs[0].shape[0]
    col_count = out_ref.shape[0]
    width = w_out_ref.shape[0]
    head_size = width // heads
    chan_share = width // col_count
    stats = jnp.stack([part[:, width:] for part in part_refs]).astype(F32)
    top = stats + pltpu.roll(stats, LANES - heads, 2)
    denom = pltpu.roll(stats, LANES - 2 * heads, 2) + pltpu.roll(stats, LANES - 3 * heads, 2)
    is_head = lane_iota(stats.shape) < heads
    highest = jnp.max(top, axis=0, keepdims=True)
    scale = jnp.where(is_head, jnp.exp(jnp.where(is_head, top - highest, 0.0)), 0.0)
    total = jnp.sum(scale * denom, axis=0, keepdims=True)
    factor = scale / jnp.where(is_head[:1], total, 1.0)
    factor = factor.reshape(groups * share, LANES)
    factor_high = factor.astype(BF16)
    factor_low = (factor - factor_high.astype(F32)).astype(BF16)
    chan_head = lane_iota((LANES, width)) // head_size
    spread = jnp.where(
        chan_head == lax.broadcasted_iota(jnp.int32, (LANES, width), 0), 1.0, 0.0
    ).astype(BF16)
    wide = mul(factor_high, spread) + mul(factor_low, spread)
    wide = wide.reshape(groups, share, width)
    context = sum(part[:, :width].astype(F32) * wide[k] for k, part in enumerate(part_refs))
    gated = (context * gate_ref[...]).astype(BF16)
    updated = act_ref[...] + mul(gated, w_out_ref[...])
    token_out = updated.astype(BF16)
    token_down = mul(token_out, w_down_ref[...]).astype(BF16)
    for c in range(col_count):
        out_ref[c, :, :LANES] = token_down
        out_ref[c, :, LANES : LANES + chan_share] = token_out[
            :, c * chan_share : (c + 1) * chan_share
        ]


def final_kernel(atoms_ref, last_ref, token_ref, atom_ref, *, chan_share):
    col_count, share, _ = last_ref.shape
    tok_rows = col_count * share
    atom_count = atom_ref.shape[0]
    order = sorted(range(col_count), key=lambda c: (c % 2, c // 2))
    last = jnp.concatenate([last_ref[c] for c in order], axis=0)
    token_ref[...] = last[:, LANES : LANES + chan_share].astype(F32).T.astype(BF16)
    names = atoms_ref[atom_count:, :].astype(F32)
    token = lane_iota((LANES, tok_rows)).astype(F32)
    for k in range(atom_count // LANES):
        name = jnp.broadcast_to(names[k : k + 1, :], (LANES, LANES)).T
        name = jnp.concatenate([name] * (tok_rows // LANES), axis=1)
        hot = jnp.where(name == token, 1.0, 0.0).astype(BF16)
        rows = slice(k * LANES, (k + 1) * LANES)
        moved = atoms_ref[rows, :].astype(F32) + mul(hot, last[:, :LANES])
        atom_ref[rows, :] = moved.astype(BF16)


def body(
    atom_feat,
    atom_token,
    w_atom_qkv,
    w_atom_out,
    w_atom_up,
    pair_repr,
    w_bias,
    w_query,
    w_kv,
    w_gate,
    w_out,
    w_down,
):
    row_count = lax.axis_size("row")
    col_count = lax.axis_size("col")
    row_index = lax.axis_index("row")
    col_index = lax.axis_index("col")
    atom_count, channels = atom_feat.shape
    tok_rows, _, share, pair_width = pair_repr.shape
    key_count = row_count * share
    heads = w_bias.shape[1]
    width = w_query.shape[0]
    chan_share = width // col_count
    all_atoms = atom_count * row_count * col_count
    half = tok_rows // 2
    col_groups = col_count // 2
    side, group = col_index & 1, col_index >> 1
    out_share = half // col_groups
    shares = [
        col_index * share,
        (col_index ^ 1) * share,
        side * half,
        (1 - side) * half,
        side * half + group * out_share,
        row_index & 1,
        row_index,
        group,
        col_index,
    ]
    place = jnp.stack([col_index, row_index * tok_rows] + shares).astype(jnp.int32)
    edge_place = jnp.stack([col_index, row_index * (atom_count * col_count)] + shares)
    edge_place = edge_place.astype(jnp.int32)
    smem = pl.BlockSpec(memory_space=pltpu.SMEM)
    vmem = pl.BlockSpec(memory_space=pltpu.VMEM)
    hbm = pl.BlockSpec(memory_space=pltpu.HBM)
    unread = pl.BlockSpec(memory_space=pl.ANY)

    def swap(x, axis, step):
        return lax.ppermute(x, axis, [(i, i ^ step) for i in range(lax.axis_size(axis))])

    top = col_count // 2
    far = swap(atom_feat, "col", top)
    far_tokens = swap(atom_token, "col", top)
    token_shape = (atom_count // LANES, LANES)
    tokens, far_tokens = atom_token.reshape(token_shape), far_tokens.reshape(token_shape)
    chunk = 16

    bias_shape = (heads, half, key_count)

    def pair_bias(place_of, after, weights):
        loads = len(weights)
        return call(
            functools.partial(bias_kernel, place=place_of, chunk=chunk, loads=loads),
            (shape_of(bias_shape, F32),) + tuple(shape_of(x.shape, x.dtype) for x in weights),
            12,
            in_specs=[smem, hbm, vmem, unread] + [hbm] * loads,
            out_specs=(vmem,) * (1 + loads),
            scratch_shapes=[
                pltpu.VMEM((half,) + pair_repr.shape[1:], BF16),
                pltpu.SemaphoreType.DMA((half // chunk,)),
                pltpu.SemaphoreType.DMA((loads,)),
            ],
        )(place, *in_hbm(pair_repr, w_bias.T), after, *in_hbm(*weights))

    kept, own, own_tokens = pair_bias(4, place, (atom_feat, tokens))
    packet = call(
        pack_kernel,
        shape_of((2, atom_count + PAD_ROWS, channels), BF16),
        2,
        in_specs=[smem] + [vmem] * 4 + [unread],
        out_specs=vmem,
    )(place, own, own_tokens, far, far_tokens, kept)
    packets = [packet] + [swap(packet, "col", k) for k in range(1, top)]
    other, *atom_weights = pair_bias(5, packet, (w_atom_qkv, w_atom_out, w_atom_up))
    sent, row_atoms, first, second = call(
        edge_kernel,
        (shape_of(bias_shape, BF16), shape_of((col_count, atom_count + PAD_ROWS, channels), BF16))
        + (shape_of((HALO, channels), BF16),) * 2,
        4,
        in_specs=[smem] + [vmem] * (1 + top),
        out_specs=(vmem,) * 4,
    )(place, other, *packets)
    swapped = swap(sent, "col", 1)
    first = swap(first, "row", 1)
    pairs = [(i, ((i + 1) ^ 1) - 1) for i in range(1, row_count - 1)]
    second = lax.ppermute(second, "row", pairs)
    total, counts, inner, w_query, w_kv = call(
        inner_kernel,
        (
            shape_of((tok_rows, width), F32),
            shape_of((tok_rows, LANES), F32),
            shape_of((atom_count + PAD_ROWS, channels), BF16),
            shape_of(w_query.shape, BF16),
            shape_of(w_kv.shape, BF16),
        ),
        16,
        in_specs=[smem] + [vmem] * 4 + [hbm] * 2,
        out_specs=(vmem,) * 5,
        scratch_shapes=[
            pltpu.VMEM((col_count * atom_count, 3 * channels), BF16),
            pltpu.VMEM((col_count * atom_count, channels), BF16),
            pltpu.VMEM((col_count * atom_count, width), BF16),
            pltpu.VMEM((tok_rows, col_count * atom_count), BF16),
            pltpu.SemaphoreType.DMA((2,)),
        ],
    )(place, row_atoms, *atom_weights, *in_hbm(w_query, w_kv))
    mine, half_normed, normed, act, my_atoms = call(
        functools.partial(pool_kernel, all_atoms=all_atoms),
        (
            shape_of((2, share, width), BF16),
            shape_of((half, width), BF16),
            shape_of((out_share, width), BF16),
            shape_of((out_share, width), F32),
            shape_of((atom_count + PAD_ROWS, channels), BF16),
        ),
        12,
        in_specs=[smem] + [vmem] * 9,
        out_specs=(vmem,) * 5,
        scratch_shapes=[
            pltpu.VMEM((tok_rows, width), F32),
            pltpu.VMEM((tok_rows, width), BF16),
        ],
    )(edge_place, row_atoms, total, counts, inner, first, second, *atom_weights)
    key_parts = [mine] + [
        lax.ppermute(mine, "row", [(i, i ^ k) for i in range(row_count)])
        for k in range(1, row_count)
    ]
    queries, gate = call(
        query_kernel,
        (shape_of((half, width), BF16), shape_of((out_share, width), F32)),
        6,
        in_specs=[vmem] * 3 + [hbm],
        out_specs=(vmem,) * 2,
        scratch_shapes=[pltpu.VMEM(w_gate.shape, BF16), pltpu.SemaphoreType.DMA],
    )(half_normed, normed, w_query, *in_hbm(w_gate))
    *parts, w_out, w_down = call(
        functools.partial(token_kernel, row_count=row_count, groups=col_groups),
        tuple(shape_of((out_share, width + LANES), BF16) for _ in range(col_groups))
        + (shape_of(w_out.shape, BF16), shape_of(w_down.shape, BF16)),
        14,
        in_specs=[smem] + [vmem] * (4 + row_count) + [hbm] * 2,
        out_specs=(vmem,) * (col_groups + 2),
        scratch_shapes=[
            pltpu.VMEM((2, row_count, share, width), BF16),
            pltpu.VMEM((half, width + LANES), BF16),
            pltpu.SemaphoreType.DMA((2,)),
        ],
    )(place, queries, w_kv, kept, swapped, *key_parts, *in_hbm(w_out, w_down))
    parts = parts[:1] + [
        lax.ppermute(part, "col", [(c, c ^ (2 * k)) for c in range(col_count)])
        for k, part in enumerate(parts)
        if k > 0
    ]
    last = call(
        functools.partial(merge_kernel, heads=heads, groups=col_groups),
        shape_of((col_count, out_share, 2 * LANES), BF16),
        8,
        in_specs=[vmem] * (col_groups + 4),
        out_specs=vmem,
    )(*parts, gate, act, w_out, w_down)
    last = lax.all_to_all(last, "col", 0, 0)
    token_share, atom_final = call(
        functools.partial(final_kernel, chan_share=chan_share),
        (shape_of((chan_share, tok_rows), BF16), shape_of((atom_count, channels), BF16)),
        4,
        in_specs=[vmem] * 2,
        out_specs=(vmem,) * 2,
    )(my_atoms, last)
    return (token_share.T, atom_final)


def solution(mesh):
    return jax.shard_map(
        body,
        mesh=mesh,
        in_specs=(
            P(("row", "col"), None),
            P(("row", "col")),
            P(),
            P(),
            P(),
            P("row", None, "col", None),
            P(),
            P(),
            P(),
            P(),
            P(),
            P(),
        ),
        out_specs=(P("row", "col"), P(("row", "col"), None)),
        check_vma=False,
    )
```

```python
import functools

import jax
import jax.numpy as jnp
from jax import lax
from jax.experimental import pallas as pl
from jax.experimental.pallas import tpu as pltpu
from jax.sharding import PartitionSpec as P

AHEADS = 4
QBLOCK = 32
KWIN = 128
HALO = 48
LANES = 128
AHEAD = 4
PAD_ROWS = 16
EDGE_BLOCKS = 2
EPS = 1e-05
LOG2_E = 1.4426950408889634
F32 = jnp.float32
BF16 = jnp.bfloat16
MIB = 1024 * 1024

NT = (((1,), (1,)), ((), ()))
NN = (((1,), (0,)), ((), ()))
TN = (((0,), (0,)), ((), ()))


def mul(a, b, dims=NN):
    return lax.dot_general(a, b, dims, preferred_element_type=F32)


def call(kernel, out_shape, vmem_mib, **kwargs):
    return pl.pallas_call(
        kernel,
        out_shape=out_shape,
        compiler_params=pltpu.CompilerParams(vmem_limit_bytes=vmem_mib * MIB),
        **kwargs,
    )


def shape_of(shape, dtype):
    return jax.ShapeDtypeStruct(shape, dtype)


def lane_iota(shape):
    return lax.broadcasted_iota(jnp.int32, shape, len(shape) - 1)


def in_hbm(*arrays):
    return tuple(pltpu.with_memory_space_constraint(x, pltpu.HBM) for x in arrays)


def load_all(sources, targets, sems):
    copies = [
        pltpu.make_async_copy(source, target, sems.at[i])
        for i, (source, target) in enumerate(zip(sources, targets))
    ]
    for copy in copies:
        copy.start()
    return copies


def wait_all(copies):
    for copy in copies:
        copy.wait()


def pack_kernel(place_ref, own_ref, token_ref, far_ref, far_token_ref, after_ref, out_ref):
    del after_ref
    atom_count = own_ref.shape[0]
    token_rows = token_ref.shape[0]
    blank = jnp.zeros((PAD_ROWS - token_rows, LANES), F32)
    for k, (feat, token) in enumerate(((own_ref, token_ref), (far_ref, far_token_ref))):
        out_ref[k, :atom_count, :] = feat[...]
        names = (token[...] - place_ref[1]).astype(F32)
        out_ref[k, atom_count:, :] = jnp.concatenate([names, blank], axis=0).astype(BF16)


def edge_kernel(place_ref, bias_ref, *refs):
    packets, (sent_ref, atoms_ref, first_ref, second_ref) = refs[:-4], refs[-4:]
    sent_ref[...] = bias_ref[...].astype(BF16)
    col_count, packet_rows, _ = atoms_ref.shape
    atom_count = packet_rows - PAD_ROWS
    for k, packet in enumerate(packets):
        for j in range(2):
            atoms_ref[place_ref[10] ^ (k + j * (col_count // 2))] = packet[j]
    tail = atoms_ref[col_count - 1, atom_count - HALO : atom_count, :]
    head = atoms_ref[0, :HALO, :]
    even = place_ref[7] == 0
    first_ref[...] = jnp.where(even, tail, head)
    second_ref[...] = jnp.where(even, head, tail)


def attend(query_of, window_of, blocks, valid_of=None):
    channels = query_of(0).shape[1]
    head_size = channels // AHEADS
    head_of = lane_iota((QBLOCK, channels)) // head_size
    picks = [head_of == h for h in range(AHEADS)]
    scores = []
    for b in range(blocks):
        query = query_of(b)
        stacked = jnp.concatenate(
            [jnp.where(pick, query, jnp.zeros_like(query)) for pick in picks], axis=0
        )
        scores.append(mul(window_of(b, 1), stacked, NT))
    blank = jnp.zeros((KWIN, channels), BF16)
    row = lax.broadcasted_iota(jnp.int32, (PAD_ROWS, channels), 0)
    pair_rows = jnp.where(row < 2, 1.0, 0.0).astype(BF16)
    sum_rows = jnp.concatenate([blank[:PAD_ROWS], pair_rows], axis=1)
    contexts = []
    for b in range(blocks):
        score = scores[b]
        if valid_of is not None:
            score = jnp.where(valid_of(b, score.shape), score, -1e30)
        score = score - jnp.max(score, axis=0, keepdims=True)
        expo = jnp.exp2(score * (LOG2_E / head_size**0.5))
        denom = jnp.sum(expo, axis=0, keepdims=True)
        denom_high = denom.astype(BF16).astype(F32)
        sums = jnp.where(row == 0, denom_high, jnp.where(row == 1, denom - denom_high, 0.0))
        weights = jnp.concatenate([expo.astype(BF16), sums.astype(BF16)], axis=0)
        values = jnp.concatenate([window_of(b, 2), blank], axis=1)
        mixed = mul(weights, jnp.concatenate([values, sum_rows], axis=0), TN)
        context = mixed[:QBLOCK]
        for h in range(1, AHEADS):
            pick = jnp.concatenate([picks[h]] * 2, axis=1)
            context = jnp.where(pick, mixed[h * QBLOCK : (h + 1) * QBLOCK], context)
        contexts.append((context[:, :channels] / context[:, channels:]).astype(BF16))
    return contexts


def inner_kernel(
    place_ref,
    atoms_ref,
    w_qkv_ref,
    w_out_ref,
    w_up_ref,
    w_query_hbm,
    w_kv_hbm,
    total_ref,
    count_ref,
    my_ref,
    w_query_ref,
    w_kv_ref,
    proj_ref,
    ctx_ref,
    up_ref,
    hot_ref,
    sems,
):
    loads = load_all((w_query_hbm, w_kv_hbm), (w_query_ref, w_kv_ref), sems)
    col_count, packet_rows, channels = atoms_ref.shape
    atom_count = packet_rows - PAD_ROWS
    row_atoms = col_count * atom_count
    tok_rows = total_ref.shape[0]
    blocks = row_atoms // QBLOCK - 2 * EDGE_BLOCKS
    step_blocks = max(n for n in range(1, 21) if blocks % n == 0)
    edge = EDGE_BLOCKS * QBLOCK
    for c in range(col_count):
        proj = mul(atoms_ref[c, :atom_count, :], w_qkv_ref[...])
        proj_ref[c * atom_count : (c + 1) * atom_count, :] = proj.astype(BF16)
    ctx_ref[:edge, :] = jnp.zeros((edge, channels), BF16)
    ctx_ref[row_atoms - edge :, :] = jnp.zeros((edge, channels), BF16)

    def step(i, carry):
        first = i * (step_blocks * QBLOCK) + edge

        def query_of(b):
            start = pl.multiple_of(first + b * QBLOCK, QBLOCK)
            return proj_ref[pl.ds(start, QBLOCK), :channels]

        def window_of(b, part):
            start = pl.multiple_of(first + b * QBLOCK - HALO, PAD_ROWS)
            return proj_ref[pl.ds(start, KWIN), part * channels : (part + 1) * channels]

        for b, context in enumerate(attend(query_of, window_of, step_blocks)):
            ctx_ref[pl.ds(pl.multiple_of(first + b * QBLOCK, QBLOCK), QBLOCK), :] = context
        return carry

    lax.fori_loop(0, blocks // step_blocks, step, 0)
    counts = jnp.zeros((tok_rows, LANES), F32)
    token = lax.broadcasted_iota(jnp.int32, (tok_rows, LANES), 0).astype(F32)
    lane = lane_iota((1, LANES))
    chunks = row_atoms // LANES
    for c in range(col_count):
        rows = slice(c * atom_count, (c + 1) * atom_count)
        names = atoms_ref[c, atom_count:, :].astype(F32)
        for k in range(atom_count // LANES):
            name = names[k : k + 1, :]
            counts = counts + jnp.where(name == token, 1.0, 0.0)
            chunk = c * (atom_count // LANES) + k
            if chunk == 0:
                name = jnp.where(lane < edge, -1.0, name)
            if chunk == chunks - 1:
                name = jnp.where(lane >= LANES - edge, -1.0, name)
            hot = jnp.where(name == token, 1.0, 0.0)
            hot_ref[:, chunk * LANES : (chunk + 1) * LANES] = hot.astype(BF16)
        atom_out = atoms_ref[c, :atom_count, :].astype(F32) + mul(ctx_ref[rows, :], w_out_ref[...])
        atom_out = atom_out.astype(BF16)
        ctx_ref[rows, :] = atom_out
        up_ref[rows, :] = jnp.maximum(mul(atom_out, w_up_ref[...]), 0.0).astype(BF16)
    total_ref[...] = mul(hot_ref[...], up_ref[...])
    count_ref[...] = jnp.broadcast_to(jnp.sum(counts, axis=-1, keepdims=True), counts.shape)
    mine = place_ref[0]
    start = pl.multiple_of(mine * atom_count, atom_count)
    my_ref[:atom_count, :] = ctx_ref[pl.ds(start, atom_count), :]
    my_ref[atom_count:, :] = atoms_ref[mine, atom_count:, :]
    wait_all(loads)


def bias_kernel(place_ref, pair_ref, w_ref, after_ref, *refs, place, chunk, loads):
    del after_ref
    sources, out_ref, targets = refs[:loads], refs[loads], refs[loads + 1 : 2 * loads + 1]
    cells_ref, sems, load_sems = refs[2 * loads + 1 :]
    queries, rows, share, width = cells_ref.shape
    keys = rows * share
    heads = w_ref.shape[0]
    count = queries // chunk
    base = place_ref[place]

    def load(i):
        start = pl.multiple_of(i * chunk, chunk)
        return pltpu.make_async_copy(
            pair_ref.at[pl.ds(pl.multiple_of(base + start, chunk), chunk)],
            cells_ref.at[pl.ds(start, chunk)],
            sems.at[i],
        )

    for i in range(AHEAD):
        load(i).start()
    extra = load_all(sources, targets, load_sems)
    weights = w_ref[...].astype(BF16)
    weight_sum = jnp.sum(weights.astype(F32), axis=1, keepdims=True)
    mean_of = jnp.full((heads, width), 1.0 / width, BF16)
    left = jnp.concatenate([weights, mean_of], axis=0)
    def step(i, carry):
        load(i).wait()

        @pl.when(i + AHEAD < count)
        def _():
            load(i + AHEAD).start()

        start = pl.multiple_of(i * chunk, chunk)
        for q in range(chunk):
            cells = cells_ref[start + q].reshape(keys, width).T
            values = cells.astype(F32)
            found = mul(left, cells)
            dots, center = found[:heads], found[heads:]
            spread = jnp.sum(values * values, axis=0, keepdims=True) * (1.0 / width)
            spread = spread - center * center
            bias = (dots - center * weight_sum) * lax.rsqrt(spread + EPS)
            out_ref[:, start + q, :] = bias.astype(BF16).astype(F32)
        return carry

    lax.fori_loop(0, count, step, 0)
    wait_all(extra)


def pool_kernel(
    place_ref,
    atoms_ref,
    total_ref,
    count_ref,
    inner_ref,
    first_ref,
    second_ref,
    w_qkv_ref,
    w_out_ref,
    w_up_ref,
    mine_ref,
    half_ref,
    normed_out_ref,
    act_out_ref,
    my_ref,
    act_ref,
    normed_ref,
    *,
    all_atoms,
):
    col_count, packet_rows, channels = atoms_ref.shape
    atom_count = packet_rows - PAD_ROWS
    row_atoms = col_count * atom_count
    tok_rows, width = total_ref.shape
    slices, share = mine_ref.shape[:2]
    edge = EDGE_BLOCKS * QBLOCK
    near = edge + HALO
    first = atoms_ref[0, :near, :]
    final = atoms_ref[col_count - 1, atom_count - near : atom_count, :]
    contexts = []
    even = place_ref[7] == 0
    before = jnp.where(even, second_ref[...], first_ref[...])
    after = jnp.where(even, first_ref[...], second_ref[...])
    for wide, base in (
        (jnp.concatenate([before, first], axis=0), -HALO),
        (jnp.concatenate([final, after], axis=0), row_atoms - near),
    ):
        proj = mul(wide, w_qkv_ref[...]).astype(BF16)

        def query_of(b):
            return proj[HALO + b * QBLOCK : HALO + (b + 1) * QBLOCK, :channels]

        def window_of(b, part):
            return proj[b * QBLOCK : b * QBLOCK + KWIN, part * channels : (part + 1) * channels]

        def valid_of(b, shape):
            position = place_ref[1] + (base + b * QBLOCK)
            position = position + lax.broadcasted_iota(jnp.int32, shape, 0)
            return (position >= 0) & (position < all_atoms)

        contexts += attend(query_of, window_of, EDGE_BLOCKS, valid_of)
    feat = jnp.concatenate([first[:edge], final[HALO:]], axis=0).astype(F32)
    atom_out = feat + mul(jnp.concatenate(contexts, axis=0), w_out_ref[...])
    atom_out = atom_out.astype(BF16)
    up = jnp.maximum(mul(atom_out, w_up_ref[...]), 0.0).astype(BF16)
    token = lax.broadcasted_iota(jnp.int32, (tok_rows, LANES), 0).astype(F32)
    name_first = atoms_ref[0, atom_count:, :].astype(F32)[:1]
    last_row = atom_count // LANES - 1
    name_final = atoms_ref[col_count - 1, atom_count:, :].astype(F32)[last_row : last_row + 1]
    name = jnp.where(lane_iota((1, LANES)) < edge, name_first, name_final)
    hot = jnp.where(name == token, 1.0, 0.0).astype(BF16)
    token_act = (total_ref[...] + mul(hot, up)) / count_ref[:, :1]
    center = jnp.sum(token_act, axis=-1, keepdims=True) * (1.0 / width)
    spread = jnp.sum(token_act * token_act, axis=-1, keepdims=True) * (1.0 / width)
    spread = spread - center * center
    normed = ((token_act - center) / jnp.sqrt(spread + EPS)).astype(BF16)
    normed_ref[...] = normed
    act_ref[...] = token_act
    for k in range(slices):
        mine_ref[k] = normed_ref[pl.ds(pl.multiple_of(place_ref[2 + k], share), share), :]
    out_share = act_out_ref.shape[0]
    start = pl.multiple_of(place_ref[6], out_share)
    normed_out_ref[...] = normed_ref[pl.ds(start, out_share), :]
    act_out_ref[...] = act_ref[pl.ds(start, out_share), :]
    inner = inner_ref[:atom_count, :]
    col = place_ref[0]
    my_ref[:edge, :] = jnp.where(col == 0, atom_out[:edge], inner[:edge])
    if atom_count > 2 * edge:
        my_ref[edge : atom_count - edge, :] = inner[edge : atom_count - edge]
    my_ref[atom_count - edge : atom_count, :] = jnp.where(
        col == col_count - 1, atom_out[edge:], inner[atom_count - edge :]
    )
    my_ref[atom_count:, :] = inner_ref[atom_count:, :]
    half = half_ref.shape[0]
    half_ref[...] = normed_ref[pl.ds(pl.multiple_of(place_ref[4], half), half), :]


def query_kernel(half_ref, normed_ref, w_query_ref, w_gate_hbm, query_ref, gate_ref, w_gate_ref, sem):
    load = pltpu.make_async_copy(w_gate_hbm, w_gate_ref, sem)
    load.start()
    query_ref[...] = mul(half_ref[...], w_query_ref[...]).astype(BF16)
    load.wait()
    gate_ref[...] = jax.nn.sigmoid(mul(normed_ref[...], w_gate_ref[...]))


def token_kernel(place_ref, query_ref, w_kv_ref, kept_ref, swapped_ref, *refs, row_count, groups):
    parts, refs = refs[:row_count], refs[row_count:]
    w_out_hbm, w_down_hbm, *refs = refs
    out_refs, refs = refs[:groups], refs[groups:]
    w_out_ref, w_down_ref, keys_ref, packet_ref, sems = refs
    loads = load_all((w_out_hbm, w_down_hbm), (w_out_ref, w_down_ref), sems)
    for k, part in enumerate(parts):
        for i in range(2):
            keys_ref[i, place_ref[8] ^ k] = part[i]
    heads, tok_rows, part_keys = kept_ref.shape
    key_count = 2 * part_keys
    width = query_ref.shape[1]
    head_size = width // heads
    share = out_refs[0].shape[0]
    keyvals = mul(keys_ref[...].reshape(key_count, width), w_kv_ref[...]).astype(BF16)
    stats = jnp.zeros((tok_rows, LANES), F32)
    lane = lane_iota((tok_rows, LANES))
    tiles = [jnp.zeros((tok_rows, LANES), F32)] * (width // LANES)
    tile_lane = lane_iota((tok_rows, LANES))
    windows = []
    scores = []
    for h in range(heads):
        low = h * head_size // LANES * LANES
        high = min(width, -(-(h + 1) * head_size // LANES) * LANES)
        windows.append((low, high))
        chan = lane_iota((tok_rows, high - low)) + low
        inside = (chan >= h * head_size) & (chan < (h + 1) * head_size)
        query = query_ref[:, low:high]
        query = jnp.where(inside, query, jnp.zeros_like(query))
        scores.append(mul(query, keyvals[:, low:high], NT))
    for h, (low, high) in enumerate(windows):
        score = scores[h] * (1.0 / head_size**0.5)
        score = score + jnp.concatenate([kept_ref[h], swapped_ref[h].astype(F32)], axis=1)
        top = jnp.max(score, axis=-1, keepdims=True)
        top_high = top.astype(BF16).astype(F32)
        top_low = (top - top_high).astype(BF16).astype(F32)
        expo = jnp.exp(score - (top_high + top_low))
        denom = jnp.sum(expo, axis=-1, keepdims=True)
        denom_high = denom.astype(BF16).astype(F32)
        stats = jnp.where(lane == h, top_high, stats)
        stats = jnp.where(lane == heads + h, top_low, stats)
        stats = jnp.where(lane == 2 * heads + h, denom_high, stats)
        stats = jnp.where(lane == 3 * heads + h, denom - denom_high, stats)
        mixed = mul(expo.astype(BF16), keyvals[:, width + low : width + high])
        for tile in range(low // LANES, high // LANES):
            chan = tile_lane + tile * LANES
            inside = (chan >= h * head_size) & (chan < (h + 1) * head_size)
            part = mixed[:, tile * LANES - low : (tile + 1) * LANES - low]
            tiles[tile] = jnp.where(inside, part, tiles[tile])
    for tile, values in enumerate(tiles):
        lanes = slice(tile * LANES, (tile + 1) * LANES)
        packet_ref[:, lanes] = values.astype(BF16)
    packet_ref[:, width:] = stats.astype(BF16)
    for k, out_ref in enumerate(out_refs):
        start = pl.multiple_of((place_ref[9] ^ k) * share, share)
        out_ref[...] = packet_ref[pl.ds(start, share), :]
    wait_all(loads)


def merge_kernel(*refs, heads, groups):
    part_refs = refs[:groups]
    gate_ref, act_ref, w_out_ref, w_down_ref, out_ref = refs[groups:]
    share = part_refs[0].shape[0]
    col_count = out_ref.shape[0]
    width = w_out_ref.shape[0]
    head_size = width // heads
    chan_share = width // col_count
    stats = jnp.stack([part[:, width:] for part in part_refs]).astype(F32)
    top = stats + pltpu.roll(stats, LANES - heads, 2)
    denom = pltpu.roll(stats, LANES - 2 * heads, 2) + pltpu.roll(stats, LANES - 3 * heads, 2)
    is_head = lane_iota(stats.shape) < heads
    highest = jnp.max(top, axis=0, keepdims=True)
    scale = jnp.where(is_head, jnp.exp(jnp.where(is_head, top - highest, 0.0)), 0.0)
    total = jnp.sum(scale * denom, axis=0, keepdims=True)
    factor = scale / jnp.where(is_head[:1], total, 1.0)
    factor = factor.reshape(groups * share, LANES)
    factor_high = factor.astype(BF16)
    factor_low = (factor - factor_high.astype(F32)).astype(BF16)
    chan_head = lane_iota((LANES, width)) // head_size
    spread = jnp.where(
        chan_head == lax.broadcasted_iota(jnp.int32, (LANES, width), 0), 1.0, 0.0
    ).astype(BF16)
    wide = mul(factor_high, spread) + mul(factor_low, spread)
    wide = wide.reshape(groups, share, width)
    context = sum(part[:, :width].astype(F32) * wide[k] for k, part in enumerate(part_refs))
    gated = (context * gate_ref[...]).astype(BF16)
    updated = act_ref[...] + mul(gated, w_out_ref[...])
    token_out = updated.astype(BF16)
    token_down = mul(token_out, w_down_ref[...]).astype(BF16)
    for c in range(col_count):
        out_ref[c, :, :LANES] = token_down
        out_ref[c, :, LANES : LANES + chan_share] = token_out[
            :, c * chan_share : (c + 1) * chan_share
        ]


def final_kernel(atoms_ref, last_ref, token_ref, atom_ref, *, chan_share):
    col_count, share, _ = last_ref.shape
    tok_rows = col_count * share
    atom_count = atom_ref.shape[0]
    order = sorted(range(col_count), key=lambda c: (c % 2, c // 2))
    last = jnp.concatenate([last_ref[c] for c in order], axis=0)
    token_ref[...] = last[:, LANES : LANES + chan_share].astype(F32).T.astype(BF16)
    names = atoms_ref[atom_count:, :].astype(F32)
    token = lane_iota((LANES, tok_rows)).astype(F32)
    for k in range(atom_count // LANES):
        name = jnp.broadcast_to(names[k : k + 1, :], (LANES, LANES)).T
        name = jnp.concatenate([name] * (tok_rows // LANES), axis=1)
        hot = jnp.where(name == token, 1.0, 0.0).astype(BF16)
        rows = slice(k * LANES, (k + 1) * LANES)
        moved = atoms_ref[rows, :].astype(F32) + mul(hot, last[:, :LANES])
        atom_ref[rows, :] = moved.astype(BF16)


def body(
    atom_feat,
    atom_token,
    w_atom_qkv,
    w_atom_out,
    w_atom_up,
    pair_repr,
    w_bias,
    w_query,
    w_kv,
    w_gate,
    w_out,
    w_down,
):
    row_count = lax.axis_size("row")
    col_count = lax.axis_size("col")
    row_index = lax.axis_index("row")
    col_index = lax.axis_index("col")
    atom_count, channels = atom_feat.shape
    tok_rows, _, share, pair_width = pair_repr.shape
    key_count = row_count * share
    heads = w_bias.shape[1]
    width = w_query.shape[0]
    chan_share = width // col_count
    all_atoms = atom_count * row_count * col_count
    half = tok_rows // 2
    col_groups = col_count // 2
    side, group = col_index & 1, col_index >> 1
    out_share = half // col_groups
    shares = [
        col_index * share,
        (col_index ^ 1) * share,
        side * half,
        (1 - side) * half,
        side * half + group * out_share,
        row_index & 1,
        row_index,
        group,
        col_index,
    ]
    place = jnp.stack([col_index, row_index * tok_rows] + shares).astype(jnp.int32)
    edge_place = jnp.stack([col_index, row_index * (atom_count * col_count)] + shares)
    edge_place = edge_place.astype(jnp.int32)
    smem = pl.BlockSpec(memory_space=pltpu.SMEM)
    vmem = pl.BlockSpec(memory_space=pltpu.VMEM)
    hbm = pl.BlockSpec(memory_space=pltpu.HBM)
    unread = pl.BlockSpec(memory_space=pl.ANY)

    def swap(x, axis, step):
        return lax.ppermute(x, axis, [(i, i ^ step) for i in range(lax.axis_size(axis))])

    top = col_count // 2
    far = swap(atom_feat, "col", top)
    far_tokens = swap(atom_token, "col", top)
    token_shape = (atom_count // LANES, LANES)
    tokens, far_tokens = atom_token.reshape(token_shape), far_tokens.reshape(token_shape)
    chunk = 16

    bias_shape = (heads, half, key_count)

    def pair_bias(place_of, after, weights):
        loads = len(weights)
        return call(
            functools.partial(bias_kernel, place=place_of, chunk=chunk, loads=loads),
            (shape_of(bias_shape, F32),) + tuple(shape_of(x.shape, x.dtype) for x in weights),
            12,
            in_specs=[smem, hbm, vmem, unread] + [hbm] * loads,
            out_specs=(vmem,) * (1 + loads),
            scratch_shapes=[
                pltpu.VMEM((half,) + pair_repr.shape[1:], BF16),
                pltpu.SemaphoreType.DMA((half // chunk,)),
                pltpu.SemaphoreType.DMA((loads,)),
            ],
        )(place, *in_hbm(pair_repr, w_bias.T), after, *in_hbm(*weights))

    kept, own, own_tokens = pair_bias(4, place, (atom_feat, tokens))
    packet = call(
        pack_kernel,
        shape_of((2, atom_count + PAD_ROWS, channels), BF16),
        2,
        in_specs=[smem] + [vmem] * 4 + [unread],
        out_specs=vmem,
    )(place, own, own_tokens, far, far_tokens, kept)
    packets = [packet] + [swap(packet, "col", k) for k in range(1, top)]
    other, *atom_weights = pair_bias(5, packet, (w_atom_qkv, w_atom_out, w_atom_up))
    sent, row_atoms, first, second = call(
        edge_kernel,
        (shape_of(bias_shape, BF16), shape_of((col_count, atom_count + PAD_ROWS, channels), BF16))
        + (shape_of((HALO, channels), BF16),) * 2,
        4,
        in_specs=[smem] + [vmem] * (1 + top),
        out_specs=(vmem,) * 4,
    )(place, other, *packets)
    swapped = swap(sent, "col", 1)
    first = swap(first, "row", 1)
    pairs = [(i, ((i + 1) ^ 1) - 1) for i in range(1, row_count - 1)]
    second = lax.ppermute(second, "row", pairs)
    total, counts, inner, w_query, w_kv = call(
        inner_kernel,
        (
            shape_of((tok_rows, width), F32),
            shape_of((tok_rows, LANES), F32),
            shape_of((atom_count + PAD_ROWS, channels), BF16),
            shape_of(w_query.shape, BF16),
            shape_of(w_kv.shape, BF16),
        ),
        16,
        in_specs=[smem] + [vmem] * 4 + [hbm] * 2,
        out_specs=(vmem,) * 5,
        scratch_shapes=[
            pltpu.VMEM((col_count * atom_count, 3 * channels), BF16),
            pltpu.VMEM((col_count * atom_count, channels), BF16),
            pltpu.VMEM((col_count * atom_count, width), BF16),
            pltpu.VMEM((tok_rows, col_count * atom_count), BF16),
            pltpu.SemaphoreType.DMA((2,)),
        ],
    )(place, row_atoms, *atom_weights, *in_hbm(w_query, w_kv))
    mine, half_normed, normed, act, my_atoms = call(
        functools.partial(pool_kernel, all_atoms=all_atoms),
        (
            shape_of((2, share, width), BF16),
            shape_of((half, width), BF16),
            shape_of((out_share, width), BF16),
            shape_of((out_share, width), F32),
            shape_of((atom_count + PAD_ROWS, channels), BF16),
        ),
        12,
        in_specs=[smem] + [vmem] * 9,
        out_specs=(vmem,) * 5,
        scratch_shapes=[
            pltpu.VMEM((tok_rows, width), F32),
            pltpu.VMEM((tok_rows, width), BF16),
        ],
    )(edge_place, row_atoms, total, counts, inner, first, second, *atom_weights)
    key_parts = [mine] + [
        lax.ppermute(mine, "row", [(i, i ^ k) for i in range(row_count)])
        for k in range(1, row_count)
    ]
    queries, gate = call(
        query_kernel,
        (shape_of((half, width), BF16), shape_of((out_share, width), F32)),
        6,
        in_specs=[vmem] * 3 + [hbm],
        out_specs=(vmem,) * 2,
        scratch_shapes=[pltpu.VMEM(w_gate.shape, BF16), pltpu.SemaphoreType.DMA],
    )(half_normed, normed, w_query, *in_hbm(w_gate))
    *parts, w_out, w_down = call(
        functools.partial(token_kernel, row_count=row_count, groups=col_groups),
        tuple(shape_of((out_share, width + LANES), BF16) for _ in range(col_groups))
        + (shape_of(w_out.shape, BF16), shape_of(w_down.shape, BF16)),
        14,
        in_specs=[smem] + [vmem] * (4 + row_count) + [hbm] * 2,
        out_specs=(vmem,) * (col_groups + 2),
        scratch_shapes=[
            pltpu.VMEM((2, row_count, share, width), BF16),
            pltpu.VMEM((half, width + LANES), BF16),
            pltpu.SemaphoreType.DMA((2,)),
        ],
    )(place, queries, w_kv, kept, swapped, *key_parts, *in_hbm(w_out, w_down))
    parts = parts[:1] + [
        lax.ppermute(part, "col", [(c, c ^ (2 * k)) for c in range(col_count)])
        for k, part in enumerate(parts)
        if k > 0
    ]
    last = call(
        functools.partial(merge_kernel, heads=heads, groups=col_groups),
        shape_of((col_count, out_share, 2 * LANES), BF16),
        8,
        in_specs=[vmem] * (col_groups + 4),
        out_specs=vmem,
    )(*parts, gate, act, w_out, w_down)
    last = lax.all_to_all(last, "col", 0, 0)
    token_share, atom_final = call(
        functools.partial(final_kernel, chan_share=chan_share),
        (shape_of((chan_share, tok_rows), BF16), shape_of((atom_count, channels), BF16)),
        4,
        in_specs=[vmem] * 2,
        out_specs=(vmem,) * 2,
    )(my_atoms, last)
    return (token_share.T, atom_final)


def solution(mesh):
    return jax.shard_map(
        body,
        mesh=mesh,
        in_specs=(
            P(("row", "col"), None),
            P(("row", "col")),
            P(),
            P(),
            P(),
            P("row", None, "col", None),
            P(),
            P(),
            P(),
            P(),
            P(),
            P(),
        ),
        out_specs=(P("row", "col"), P(("row", "col"), None)),
        check_vma=False,
    )
```

```python
import functools

import jax
import jax.numpy as jnp
from jax import lax
from jax.experimental import pallas as pl
from jax.experimental.pallas import tpu as pltpu
from jax.sharding import PartitionSpec as P

AHEADS = 4
QBLOCK = 32
KWIN = 128
HALO = 48
LANES = 128
AHEAD = 4
PAD_ROWS = 16
EDGE_BLOCKS = 2
EPS = 1e-05
LOG2_E = 1.4426950408889634
F32 = jnp.float32
BF16 = jnp.bfloat16
MIB = 1024 * 1024

NT = (((1,), (1,)), ((), ()))
NN = (((1,), (0,)), ((), ()))
TN = (((0,), (0,)), ((), ()))


def mul(a, b, dims=NN):
    return lax.dot_general(a, b, dims, preferred_element_type=F32)


def call(kernel, out_shape, vmem_mib, **kwargs):
    return pl.pallas_call(
        kernel,
        out_shape=out_shape,
        compiler_params=pltpu.CompilerParams(vmem_limit_bytes=vmem_mib * MIB),
        **kwargs,
    )


def shape_of(shape, dtype):
    return jax.ShapeDtypeStruct(shape, dtype)


def lane_iota(shape):
    return lax.broadcasted_iota(jnp.int32, shape, len(shape) - 1)


def in_hbm(*arrays):
    return tuple(pltpu.with_memory_space_constraint(x, pltpu.HBM) for x in arrays)


def load_all(sources, targets, sems):
    copies = [
        pltpu.make_async_copy(source, target, sems.at[i])
        for i, (source, target) in enumerate(zip(sources, targets))
    ]
    for copy in copies:
        copy.start()
    return copies


def wait_all(copies):
    for copy in copies:
        copy.wait()


def pack_kernel(place_ref, own_ref, token_ref, far_ref, far_token_ref, after_ref, out_ref):
    del after_ref
    atom_count = own_ref.shape[0]
    token_rows = token_ref.shape[0]
    blank = jnp.zeros((PAD_ROWS - token_rows, LANES), F32)
    for k, (feat, token) in enumerate(((own_ref, token_ref), (far_ref, far_token_ref))):
        out_ref[k, :atom_count, :] = feat[...]
        names = (token[...] - place_ref[1]).astype(F32)
        out_ref[k, atom_count:, :] = jnp.concatenate([names, blank], axis=0).astype(BF16)


def edge_kernel(place_ref, bias_ref, *refs):
    packets, (sent_ref, atoms_ref, first_ref, second_ref) = refs[:-4], refs[-4:]
    sent_ref[...] = bias_ref[...].astype(BF16)
    col_count, packet_rows, _ = atoms_ref.shape
    atom_count = packet_rows - PAD_ROWS
    for k, packet in enumerate(packets):
        for j in range(2):
            atoms_ref[place_ref[10] ^ (k + j * (col_count // 2))] = packet[j]
    tail = atoms_ref[col_count - 1, atom_count - HALO : atom_count, :]
    head = atoms_ref[0, :HALO, :]
    even = place_ref[7] == 0
    first_ref[...] = jnp.where(even, tail, head)
    second_ref[...] = jnp.where(even, head, tail)


def attend(query_of, union_of, blocks, valid_of=None):
    channels = query_of(0).shape[1]
    head_size = channels // AHEADS
    rows_of = AHEADS * QBLOCK
    head_of = lane_iota((QBLOCK, channels)) // head_size
    picks = [head_of == h for h in range(AHEADS)]
    scores = []
    for b in range(0, blocks, 2):
        stacked = []
        for query in (query_of(b), query_of(b + 1)):
            stacked += [jnp.where(pick, query, jnp.zeros_like(query)) for pick in picks]
        found = mul(union_of(b, 1), jnp.concatenate(stacked, axis=0), NT)
        scores += [found[:KWIN, :rows_of], found[QBLOCK:, rows_of:]]
    blank = jnp.zeros((KWIN, channels), BF16)
    row = lax.broadcasted_iota(jnp.int32, (PAD_ROWS, channels), 0)
    pair_rows = jnp.where(row < 2, 1.0, 0.0).astype(BF16)
    sum_rows = jnp.concatenate([blank[:PAD_ROWS], pair_rows], axis=1)
    contexts = []
    for b in range(blocks):
        score = scores[b]
        if valid_of is not None:
            score = jnp.where(valid_of(b, score.shape), score, -1e30)
        score = score - jnp.max(score, axis=0, keepdims=True)
        expo = jnp.exp2(score * (LOG2_E / head_size**0.5))
        denom = jnp.sum(expo, axis=0, keepdims=True)
        denom_high = denom.astype(BF16).astype(F32)
        sums = jnp.where(row == 0, denom_high, jnp.where(row == 1, denom - denom_high, 0.0))
        weights = jnp.concatenate([expo.astype(BF16), sums.astype(BF16)], axis=0)
        start = b % 2 * QBLOCK
        values = union_of(b - b % 2, 2)[start : start + KWIN]
        values = jnp.concatenate([values, blank], axis=1)
        mixed = mul(weights, jnp.concatenate([values, sum_rows], axis=0), TN)
        context = mixed[:QBLOCK]
        for h in range(1, AHEADS):
            pick = jnp.concatenate([picks[h]] * 2, axis=1)
            context = jnp.where(pick, mixed[h * QBLOCK : (h + 1) * QBLOCK], context)
        contexts.append((context[:, :channels] / context[:, channels:]).astype(BF16))
    return contexts


def inner_kernel(
    atoms_ref, w_qkv_ref, w_query_hbm, w_kv_hbm, ctx_ref, w_query_ref, w_kv_ref, proj_ref, sems
):
    loads = load_all((w_query_hbm, w_kv_hbm), (w_query_ref, w_kv_ref), sems)
    col_count, packet_rows, channels = atoms_ref.shape
    atom_count = packet_rows - PAD_ROWS
    row_atoms = col_count * atom_count
    blocks = row_atoms // QBLOCK - 2 * EDGE_BLOCKS
    step_blocks = max(n for n in range(2, 21, 2) if blocks % n == 0)
    edge = EDGE_BLOCKS * QBLOCK
    for c in range(col_count):
        proj = mul(atoms_ref[c, :atom_count, :], w_qkv_ref[...])
        proj_ref[c * atom_count : (c + 1) * atom_count, :] = proj.astype(BF16)
    ctx_ref[:edge, :] = jnp.zeros((edge, channels), BF16)
    ctx_ref[row_atoms - edge :, :] = jnp.zeros((edge, channels), BF16)

    def step(i, carry):
        first = i * (step_blocks * QBLOCK) + edge

        def query_of(b):
            start = pl.multiple_of(first + b * QBLOCK, QBLOCK)
            return proj_ref[pl.ds(start, QBLOCK), :channels]

        def union_of(b, part):
            start = pl.multiple_of(first + b * QBLOCK - HALO, PAD_ROWS)
            return proj_ref[
                pl.ds(start, KWIN + QBLOCK), part * channels : (part + 1) * channels
            ]

        for b, context in enumerate(attend(query_of, union_of, step_blocks)):
            ctx_ref[pl.ds(pl.multiple_of(first + b * QBLOCK, QBLOCK), QBLOCK), :] = context
        return carry

    lax.fori_loop(0, blocks // step_blocks, step, 0)
    wait_all(loads)


def bias_kernel(place_ref, pair_ref, w_ref, after_ref, *refs, place, offset, chunk, loads):
    del after_ref
    sources, out_ref, targets = refs[:loads], refs[loads], refs[loads + 1 : 2 * loads + 1]
    cells_ref, sems, load_sems = refs[2 * loads + 1 :]
    queries, rows, share, width = cells_ref.shape
    keys = rows * share
    heads = w_ref.shape[0]
    count = queries // chunk
    base = place_ref[place] + offset

    def load(i):
        start = pl.multiple_of(i * chunk, chunk)
        return pltpu.make_async_copy(
            pair_ref.at[pl.ds(base + start, chunk)],
            cells_ref.at[pl.ds(start, chunk)],
            sems.at[i],
        )

    for i in range(min(AHEAD, count)):
        load(i).start()
    extra = load_all(sources, targets, load_sems)
    weights = w_ref[...].astype(BF16)
    weight_sum = jnp.sum(weights.astype(F32), axis=1, keepdims=True)
    mean_of = jnp.full((heads, width), 1.0 / width, BF16)
    left = jnp.concatenate([weights, mean_of], axis=0)
    def step(i, carry):
        load(i).wait()

        @pl.when(i + AHEAD < count)
        def _():
            load(i + AHEAD).start()

        start = pl.multiple_of(i * chunk, chunk)
        for q in range(chunk):
            cells = cells_ref[start + q].reshape(keys, width).T
            values = cells.astype(F32)
            found = mul(left, cells)
            dots, center = found[:heads], found[heads:]
            spread = jnp.sum(values * values, axis=0, keepdims=True) * (1.0 / width)
            spread = spread - center * center
            bias = (dots - center * weight_sum) * lax.rsqrt(spread + EPS)
            out_ref[:, start + q, :] = bias.astype(BF16).astype(F32)
        return carry

    lax.fori_loop(0, count, step, 0)
    wait_all(extra)


def pool_kernel(
    place_ref,
    atoms_ref,
    ctx_ref,
    first_ref,
    second_ref,
    w_qkv_ref,
    w_out_ref,
    w_up_ref,
    mine_ref,
    half_ref,
    normed_out_ref,
    act_out_ref,
    my_ref,
    act_ref,
    atom_out_ref,
    *,
    all_atoms,
):
    col_count, packet_rows, channels = atoms_ref.shape
    atom_count = packet_rows - PAD_ROWS
    row_atoms = col_count * atom_count
    half, width = half_ref.shape
    slices, share = mine_ref.shape[:2]
    edge = EDGE_BLOCKS * QBLOCK
    near = edge + HALO
    begin = atoms_ref[0, :near, :]
    end = atoms_ref[col_count - 1, atom_count - near : atom_count, :]
    even = place_ref[7] == 0
    before = jnp.where(even, second_ref[...], first_ref[...])
    after = jnp.where(even, first_ref[...], second_ref[...])
    contexts = []
    for wide, base in (
        (jnp.concatenate([before, begin], axis=0), -HALO),
        (jnp.concatenate([end, after], axis=0), row_atoms - near),
    ):
        proj = mul(wide, w_qkv_ref[...]).astype(BF16)

        def query_of(b):
            return proj[HALO + b * QBLOCK : HALO + (b + 1) * QBLOCK, :channels]

        def union_of(b, part):
            return proj[
                b * QBLOCK : b * QBLOCK + KWIN + QBLOCK, part * channels : (part + 1) * channels
            ]

        def valid_of(b, shape):
            position = place_ref[1] + (base + b * QBLOCK)
            position = position + lax.broadcasted_iota(jnp.int32, shape, 0)
            return (position >= 0) & (position < all_atoms)

        contexts.append(jnp.concatenate(attend(query_of, union_of, EDGE_BLOCKS, valid_of), axis=0))
    rows = half + slices * share
    row = lax.broadcasted_iota(jnp.int32, (rows, LANES), 0)
    token = row + jnp.where(row < half, place_ref[4], place_ref[11] - half)
    token = token.astype(F32)
    counts = jnp.zeros((rows, LANES), F32)
    totals = jnp.zeros((rows, width), F32)
    for c in [*range(1, col_count - 1), 0, col_count - 1]:
        start = c * atom_count
        ctx = ctx_ref[start : start + atom_count, :]
        if c == 0:
            ctx = jnp.concatenate([contexts[0], ctx[edge:]], axis=0)
        if c == col_count - 1:
            ctx = jnp.concatenate([ctx[: atom_count - edge], contexts[1]], axis=0)
        atom_out = atoms_ref[c, :atom_count, :].astype(F32) + mul(ctx, w_out_ref[...])
        atom_out = atom_out.astype(BF16)
        atom_out_ref[c] = atom_out
        up = jnp.maximum(mul(atom_out, w_up_ref[...]), 0.0).astype(BF16)
        names = atoms_ref[c, atom_count:, :].astype(F32)
        hots = []
        for k in range(atom_count // LANES):
            hot = jnp.where(names[k : k + 1, :] == token, 1.0, 0.0)
            counts = counts + hot
            hots.append(hot.astype(BF16))
        totals = totals + mul(jnp.concatenate(hots, axis=1), up)
    token_act = totals / jnp.sum(counts, axis=-1, keepdims=True)
    center = jnp.sum(token_act, axis=-1, keepdims=True) * (1.0 / width)
    spread = jnp.sum(token_act * token_act, axis=-1, keepdims=True) * (1.0 / width)
    spread = spread - center * center
    normed = ((token_act - center) / jnp.sqrt(spread + EPS)).astype(BF16)
    side = place_ref[12]
    for k in range(slices):
        part = normed[half + k * share : half + (k + 1) * share]
        other = normed[half + (1 - k) * share : half + (2 - k) * share]
        mine_ref[k] = jnp.where(side == 0, part, other)
    half_ref[...] = normed[:half]
    act_ref[...] = token_act[:half]
    out_share = act_out_ref.shape[0]
    start = pl.multiple_of(place_ref[9] * out_share, out_share)
    normed_out_ref[...] = half_ref[pl.ds(start, out_share), :]
    act_out_ref[...] = act_ref[pl.ds(start, out_share), :]
    col = place_ref[10]
    my_ref[:atom_count, :] = atom_out_ref[col]
    my_ref[atom_count:, :] = atoms_ref[col, atom_count:, :]


def query_kernel(half_ref, normed_ref, w_query_ref, w_gate_hbm, query_ref, gate_ref, w_gate_ref, sem):
    load = pltpu.make_async_copy(w_gate_hbm, w_gate_ref, sem)
    load.start()
    query_ref[...] = mul(half_ref[...], w_query_ref[...]).astype(BF16)
    load.wait()
    gate_ref[...] = jax.nn.sigmoid(mul(normed_ref[...], w_gate_ref[...]))


def token_kernel(
    place_ref, query_ref, w_kv_ref, early_ref, late_ref, swapped_ref, *refs, row_count, groups
):
    parts, refs = refs[:row_count], refs[row_count:]
    w_out_hbm, w_down_hbm, *refs = refs
    out_refs, refs = refs[:groups], refs[groups:]
    w_out_ref, w_down_ref, keys_ref, packet_ref, sems = refs
    loads = load_all((w_out_hbm, w_down_hbm), (w_out_ref, w_down_ref), sems)
    for k, part in enumerate(parts):
        for i in range(2):
            keys_ref[i, place_ref[8] ^ k] = part[i]
    heads, tok_rows, part_keys = swapped_ref.shape
    key_count = 2 * part_keys
    width = query_ref.shape[1]
    head_size = width // heads
    share = out_refs[0].shape[0]
    keyvals = mul(keys_ref[...].reshape(key_count, width), w_kv_ref[...]).astype(BF16)
    stats = jnp.zeros((tok_rows, LANES), F32)
    lane = lane_iota((tok_rows, LANES))
    tiles = [jnp.zeros((tok_rows, LANES), F32)] * (width // LANES)
    tile_lane = lane_iota((tok_rows, LANES))
    windows = []
    scores = []
    for h in range(heads):
        low = h * head_size // LANES * LANES
        high = min(width, -(-(h + 1) * head_size // LANES) * LANES)
        windows.append((low, high))
        chan = lane_iota((tok_rows, high - low)) + low
        inside = (chan >= h * head_size) & (chan < (h + 1) * head_size)
        query = query_ref[:, low:high]
        query = jnp.where(inside, query, jnp.zeros_like(query))
        scores.append(mul(query, keyvals[:, low:high], NT))
    for h, (low, high) in enumerate(windows):
        score = scores[h] * (1.0 / head_size**0.5)
        kept = jnp.concatenate([early_ref[h], late_ref[h]], axis=0)
        score = score + jnp.concatenate([kept, swapped_ref[h].astype(F32)], axis=1)
        top = jnp.max(score, axis=-1, keepdims=True)
        top_high = top.astype(BF16).astype(F32)
        top_low = (top - top_high).astype(BF16).astype(F32)
        expo = jnp.exp(score - (top_high + top_low))
        denom = jnp.sum(expo, axis=-1, keepdims=True)
        denom_high = denom.astype(BF16).astype(F32)
        stats = jnp.where(lane == h, top_high, stats)
        stats = jnp.where(lane == heads + h, top_low, stats)
        stats = jnp.where(lane == 2 * heads + h, denom_high, stats)
        stats = jnp.where(lane == 3 * heads + h, denom - denom_high, stats)
        mixed = mul(expo.astype(BF16), keyvals[:, width + low : width + high])
        for tile in range(low // LANES, high // LANES):
            chan = tile_lane + tile * LANES
            inside = (chan >= h * head_size) & (chan < (h + 1) * head_size)
            part = mixed[:, tile * LANES - low : (tile + 1) * LANES - low]
            tiles[tile] = jnp.where(inside, part, tiles[tile])
    for tile, values in enumerate(tiles):
        lanes = slice(tile * LANES, (tile + 1) * LANES)
        packet_ref[:, lanes] = values.astype(BF16)
    packet_ref[:, width:] = stats.astype(BF16)
    for k, out_ref in enumerate(out_refs):
        start = pl.multiple_of((place_ref[9] ^ k) * share, share)
        out_ref[...] = packet_ref[pl.ds(start, share), :]
    wait_all(loads)


def merge_kernel(*refs, heads, groups):
    part_refs = refs[:groups]
    gate_ref, act_ref, w_out_ref, w_down_ref, out_ref = refs[groups:]
    share = part_refs[0].shape[0]
    col_count = out_ref.shape[0]
    width = w_out_ref.shape[0]
    head_size = width // heads
    chan_share = width // col_count
    stats = jnp.stack([part[:, width:] for part in part_refs]).astype(F32)
    top = stats + pltpu.roll(stats, LANES - heads, 2)
    denom = pltpu.roll(stats, LANES - 2 * heads, 2) + pltpu.roll(stats, LANES - 3 * heads, 2)
    is_head = lane_iota(stats.shape) < heads
    highest = jnp.max(top, axis=0, keepdims=True)
    scale = jnp.where(is_head, jnp.exp(jnp.where(is_head, top - highest, 0.0)), 0.0)
    total = jnp.sum(scale * denom, axis=0, keepdims=True)
    factor = scale / jnp.where(is_head[:1], total, 1.0)
    factor = factor.reshape(groups * share, LANES)
    factor_high = factor.astype(BF16)
    factor_low = (factor - factor_high.astype(F32)).astype(BF16)
    chan_head = lane_iota((LANES, width)) // head_size
    spread = jnp.where(
        chan_head == lax.broadcasted_iota(jnp.int32, (LANES, width), 0), 1.0, 0.0
    ).astype(BF16)
    wide = mul(factor_high, spread) + mul(factor_low, spread)
    wide = wide.reshape(groups, share, width)
    context = sum(part[:, :width].astype(F32) * wide[k] for k, part in enumerate(part_refs))
    gated = (context * gate_ref[...]).astype(BF16)
    updated = act_ref[...] + mul(gated, w_out_ref[...])
    token_out = updated.astype(BF16)
    token_down = mul(token_out, w_down_ref[...]).astype(BF16)
    for c in range(col_count):
        out_ref[c, :, :LANES] = token_down
        out_ref[c, :, LANES : LANES + chan_share] = token_out[
            :, c * chan_share : (c + 1) * chan_share
        ]


def final_kernel(atoms_ref, last_ref, token_ref, atom_ref, *, chan_share):
    col_count, share, _ = last_ref.shape
    tok_rows = col_count * share
    atom_count = atom_ref.shape[0]
    order = sorted(range(col_count), key=lambda c: (c % 2, c // 2))
    last = jnp.concatenate([last_ref[c] for c in order], axis=0)
    token_ref[...] = last[:, LANES : LANES + chan_share].astype(F32).T.astype(BF16)
    names = atoms_ref[atom_count:, :].astype(F32)
    token = lane_iota((LANES, tok_rows)).astype(F32)
    for k in range(atom_count // LANES):
        name = jnp.broadcast_to(names[k : k + 1, :], (LANES, LANES)).T
        name = jnp.concatenate([name] * (tok_rows // LANES), axis=1)
        hot = jnp.where(name == token, 1.0, 0.0).astype(BF16)
        rows = slice(k * LANES, (k + 1) * LANES)
        moved = atoms_ref[rows, :].astype(F32) + mul(hot, last[:, :LANES])
        atom_ref[rows, :] = moved.astype(BF16)


def body(
    atom_feat,
    atom_token,
    w_atom_qkv,
    w_atom_out,
    w_atom_up,
    pair_repr,
    w_bias,
    w_query,
    w_kv,
    w_gate,
    w_out,
    w_down,
):
    row_count = lax.axis_size("row")
    col_count = lax.axis_size("col")
    row_index = lax.axis_index("row")
    col_index = lax.axis_index("col")
    atom_count, channels = atom_feat.shape
    tok_rows, _, share, pair_width = pair_repr.shape
    key_count = row_count * share
    heads = w_bias.shape[1]
    width = w_query.shape[0]
    chan_share = width // col_count
    all_atoms = atom_count * row_count * col_count
    half = tok_rows // 2
    col_groups = col_count // 2
    side, group = col_index & 1, col_index >> 1
    out_share = half // col_groups
    shares = [
        col_index * share,
        (col_index ^ 1) * share,
        side * half,
        (1 - side) * half,
        side * half + group * out_share,
        row_index & 1,
        row_index,
        group,
        col_index,
        group * (2 * share),
        side,
    ]
    place = jnp.stack([col_index, row_index * tok_rows] + shares).astype(jnp.int32)
    edge_place = jnp.stack([col_index, row_index * (atom_count * col_count)] + shares)
    edge_place = edge_place.astype(jnp.int32)
    smem = pl.BlockSpec(memory_space=pltpu.SMEM)
    vmem = pl.BlockSpec(memory_space=pltpu.VMEM)
    hbm = pl.BlockSpec(memory_space=pltpu.HBM)
    unread = pl.BlockSpec(memory_space=pl.ANY)

    def swap(x, axis, step):
        return lax.ppermute(x, axis, [(i, i ^ step) for i in range(lax.axis_size(axis))])

    top = col_count // 2
    far = swap(atom_feat, "col", top)
    far_tokens = swap(atom_token, "col", top)
    token_shape = (atom_count // LANES, LANES)
    tokens, far_tokens = atom_token.reshape(token_shape), far_tokens.reshape(token_shape)

    def pair_bias(place_of, offset, rows, chunk, after, weights):
        loads = len(weights)
        return call(
            functools.partial(
                bias_kernel, place=place_of, offset=offset, chunk=chunk, loads=loads
            ),
            (shape_of((heads, rows, key_count), F32),)
            + tuple(shape_of(x.shape, x.dtype) for x in weights),
            12,
            in_specs=[smem, hbm, vmem, unread] + [hbm] * loads,
            out_specs=(vmem,) * (1 + loads),
            scratch_shapes=[
                pltpu.VMEM((rows,) + pair_repr.shape[1:], BF16),
                pltpu.SemaphoreType.DMA((rows // chunk,)),
                pltpu.SemaphoreType.DMA((max(loads, 1),)),
            ],
        )(place, *in_hbm(pair_repr, w_bias.T), after, *in_hbm(*weights))

    early = half * 5 // 8
    kept, own, own_tokens = pair_bias(4, 0, early, early // 2, place, (atom_feat, tokens))
    packet = call(
        pack_kernel,
        shape_of((2, atom_count + PAD_ROWS, channels), BF16),
        2,
        in_specs=[smem] + [vmem] * 4 + [unread],
        out_specs=vmem,
    )(place, own, own_tokens, far, far_tokens, kept)
    packets = [packet] + [swap(packet, "col", k) for k in range(1, top)]
    other, *atom_weights = pair_bias(
        5, 0, half, half // 4, packet, (w_atom_qkv, w_atom_out, w_atom_up)
    )
    sent, row_atoms, first, second = call(
        edge_kernel,
        (shape_of((heads, half, key_count), BF16), shape_of((col_count, atom_count + PAD_ROWS, channels), BF16))
        + (shape_of((HALO, channels), BF16),) * 2,
        4,
        in_specs=[smem] + [vmem] * (1 + top),
        out_specs=(vmem,) * 4,
    )(place, other, *packets)
    swapped = swap(sent, "col", 1)
    first = swap(first, "row", 1)
    pairs = [(i, ((i + 1) ^ 1) - 1) for i in range(1, row_count - 1)]
    second = lax.ppermute(second, "row", pairs)
    w_qkv, w_mix, w_up = atom_weights
    ctx, w_query, w_kv = call(
        inner_kernel,
        (
            shape_of((col_count * atom_count, channels), BF16),
            shape_of(w_query.shape, BF16),
            shape_of(w_kv.shape, BF16),
        ),
        12,
        in_specs=[vmem] * 2 + [hbm] * 2,
        out_specs=(vmem,) * 3,
        scratch_shapes=[
            pltpu.VMEM((col_count * atom_count, 3 * channels), BF16),
            pltpu.SemaphoreType.DMA((2,)),
        ],
    )(row_atoms, w_qkv, *in_hbm(w_query, w_kv))
    mine, half_normed, normed, act, my_atoms = call(
        functools.partial(pool_kernel, all_atoms=all_atoms),
        (
            shape_of((2, share, width), BF16),
            shape_of((half, width), BF16),
            shape_of((out_share, width), BF16),
            shape_of((out_share, width), F32),
            shape_of((atom_count + PAD_ROWS, channels), BF16),
        ),
        14,
        in_specs=[smem] + [vmem] * 7,
        out_specs=(vmem,) * 5,
        scratch_shapes=[
            pltpu.VMEM((half, width), F32),
            pltpu.VMEM((col_count, atom_count, channels), BF16),
        ],
    )(edge_place, row_atoms, ctx, first, second, w_qkv, w_mix, w_up)
    key_parts = [mine] + [swap(mine, "row", k) for k in range(1, row_count)]
    late = half - early
    (kept_late,) = pair_bias(4, early, late, late // 2, mine, ())
    queries, gate = call(
        query_kernel,
        (shape_of((half, width), BF16), shape_of((out_share, width), F32)),
        6,
        in_specs=[vmem] * 3 + [hbm],
        out_specs=(vmem,) * 2,
        scratch_shapes=[pltpu.VMEM(w_gate.shape, BF16), pltpu.SemaphoreType.DMA],
    )(half_normed, normed, w_query, *in_hbm(w_gate))
    *parts, w_out, w_down = call(
        functools.partial(token_kernel, row_count=row_count, groups=col_groups),
        tuple(shape_of((out_share, width + LANES), BF16) for _ in range(col_groups))
        + (shape_of(w_out.shape, BF16), shape_of(w_down.shape, BF16)),
        14,
        in_specs=[smem] + [vmem] * (5 + row_count) + [hbm] * 2,
        out_specs=(vmem,) * (col_groups + 2),
        scratch_shapes=[
            pltpu.VMEM((2, row_count, share, width), BF16),
            pltpu.VMEM((half, width + LANES), BF16),
            pltpu.SemaphoreType.DMA((2,)),
        ],
    )(place, queries, w_kv, kept, kept_late, swapped, *key_parts, *in_hbm(w_out, w_down))
    parts = parts[:1] + [
        lax.ppermute(part, "col", [(c, c ^ (2 * k)) for c in range(col_count)])
        for k, part in enumerate(parts)
        if k > 0
    ]
    last = call(
        functools.partial(merge_kernel, heads=heads, groups=col_groups),
        shape_of((col_count, out_share, 2 * LANES), BF16),
        8,
        in_specs=[vmem] * (col_groups + 4),
        out_specs=vmem,
    )(*parts, gate, act, w_out, w_down)
    last = lax.all_to_all(last, "col", 0, 0)
    token_share, atom_final = call(
        functools.partial(final_kernel, chan_share=chan_share),
        (shape_of((chan_share, tok_rows), BF16), shape_of((atom_count, channels), BF16)),
        4,
        in_specs=[vmem] * 2,
        out_specs=(vmem,) * 2,
    )(my_atoms, last)
    return (token_share.T, atom_final)


def solution(mesh):
    return jax.shard_map(
        body,
        mesh=mesh,
        in_specs=(
            P(("row", "col"), None),
            P(("row", "col")),
            P(),
            P(),
            P(),
            P("row", None, "col", None),
            P(),
            P(),
            P(),
            P(),
            P(),
            P(),
        ),
        out_specs=(P("row", "col"), P(("row", "col"), None)),
        check_vma=False,
    )
```

```python
import functools

import jax
import jax.numpy as jnp
from jax import lax
from jax.experimental import pallas as pl
from jax.experimental.pallas import tpu as pltpu
from jax.sharding import PartitionSpec as P

AHEADS = 4
QBLOCK = 32
KWIN = 128
HALO = 48
LANES = 128
AHEAD = 4
SUBLANES = 8
PAD_ROWS = 16
EDGE_BLOCKS = 2
EPS = 1e-05
LOG2_E = 1.4426950408889634
F32 = jnp.float32
BF16 = jnp.bfloat16
MIB = 1024 * 1024

NT = (((1,), (1,)), ((), ()))
NN = (((1,), (0,)), ((), ()))
TN = (((0,), (0,)), ((), ()))


def mul(a, b, dims=NN):
    return lax.dot_general(a, b, dims, preferred_element_type=F32)


def call(kernel, out_shape, vmem_mib, **kwargs):
    return pl.pallas_call(
        kernel,
        out_shape=out_shape,
        compiler_params=pltpu.CompilerParams(vmem_limit_bytes=vmem_mib * MIB),
        **kwargs,
    )


def shape_of(shape, dtype):
    return jax.ShapeDtypeStruct(shape, dtype)


def far_first(count):
    return [0] + list(range(count - 1, 0, -1))


def lane_iota(shape):
    return lax.broadcasted_iota(jnp.int32, shape, len(shape) - 1)


def in_hbm(*arrays):
    return tuple(pltpu.with_memory_space_constraint(x, pltpu.HBM) for x in arrays)


def load_all(sources, targets, sems):
    copies = [
        pltpu.make_async_copy(source, target, sems.at[i])
        for i, (source, target) in enumerate(zip(sources, targets))
    ]
    for copy in copies:
        copy.start()
    return copies


def wait_all(copies):
    for copy in copies:
        copy.wait()


def pack_kernel(place_ref, own_ref, token_ref, far_ref, far_token_ref, after_ref, out_ref):
    del after_ref
    atom_count = own_ref.shape[0]
    token_rows = token_ref.shape[0]
    blank = jnp.zeros((PAD_ROWS - token_rows, LANES), F32)
    for k, (feat, token) in enumerate(((own_ref, token_ref), (far_ref, far_token_ref))):
        out_ref[k, :atom_count, :] = feat[...]
        names = (token[...] - place_ref[1]).astype(F32)
        out_ref[k, atom_count:, :] = jnp.concatenate([names, blank], axis=0).astype(BF16)


def edge_kernel(place_ref, bias_ref, *refs):
    packets, (sent_ref, atoms_ref, first_ref, second_ref) = refs[:-4], refs[-4:]
    sent_ref[...] = bias_ref[...].astype(BF16)
    col_count, packet_rows, _ = atoms_ref.shape
    atom_count = packet_rows - PAD_ROWS
    for k, packet in enumerate(packets):
        for j in range(2):
            atoms_ref[place_ref[10] ^ (k + j * (col_count // 2))] = packet[j]
    tail = atoms_ref[col_count - 1, atom_count - HALO : atom_count, :]
    head = atoms_ref[0, :HALO, :]
    even = place_ref[7] == 0
    first_ref[...] = jnp.where(even, tail, head)
    second_ref[...] = jnp.where(even, head, tail)


def attend(query_of, union_of, blocks, valid_of=None):
    channels = query_of(0).shape[1]
    head_size = channels // AHEADS
    rows_of = AHEADS * QBLOCK
    head_of = lane_iota((QBLOCK, channels)) // head_size
    picks = [head_of == h for h in range(AHEADS)]
    scores = []
    for b in range(0, blocks, 2):
        stacked = []
        for query in (query_of(b), query_of(b + 1)):
            stacked += [jnp.where(pick, query, jnp.zeros_like(query)) for pick in picks]
        found = mul(union_of(b, 1), jnp.concatenate(stacked, axis=0), NT)
        scores += [found[:KWIN, :rows_of], found[QBLOCK:, rows_of:]]
    blank = jnp.zeros((KWIN, channels), BF16)
    row = lax.broadcasted_iota(jnp.int32, (PAD_ROWS, channels), 0)
    pair_rows = jnp.where(row < 2, 1.0, 0.0).astype(BF16)
    sum_rows = jnp.concatenate([blank[:PAD_ROWS], pair_rows], axis=1)
    contexts = []
    for b in range(blocks):
        score = scores[b]
        if valid_of is not None:
            score = jnp.where(valid_of(b, score.shape), score, -1e30)
        score = score - jnp.max(score, axis=0, keepdims=True)
        expo = jnp.exp2(score * (LOG2_E / head_size**0.5))
        denom = jnp.sum(expo, axis=0, keepdims=True)
        denom_high = denom.astype(BF16).astype(F32)
        sums = jnp.where(row == 0, denom_high, jnp.where(row == 1, denom - denom_high, 0.0))
        weights = jnp.concatenate([expo.astype(BF16), sums.astype(BF16)], axis=0)
        start = b % 2 * QBLOCK
        values = union_of(b - b % 2, 2)[start : start + KWIN]
        values = jnp.concatenate([values, blank], axis=1)
        mixed = mul(weights, jnp.concatenate([values, sum_rows], axis=0), TN)
        context = mixed[:QBLOCK]
        for h in range(1, AHEADS):
            pick = jnp.concatenate([picks[h]] * 2, axis=1)
            context = jnp.where(pick, mixed[h * QBLOCK : (h + 1) * QBLOCK], context)
        contexts.append((context[:, :channels] / context[:, channels:]).astype(BF16))
    return contexts


def inner_kernel(
    atoms_ref, w_qkv_ref, w_query_hbm, w_kv_hbm, ctx_ref, w_query_ref, w_kv_ref, proj_ref, sems
):
    loads = load_all((w_query_hbm, w_kv_hbm), (w_query_ref, w_kv_ref), sems)
    col_count, packet_rows, channels = atoms_ref.shape
    atom_count = packet_rows - PAD_ROWS
    row_atoms = col_count * atom_count
    blocks = row_atoms // QBLOCK - 2 * EDGE_BLOCKS
    step_blocks = max(n for n in range(2, 21, 2) if blocks % n == 0)
    edge = EDGE_BLOCKS * QBLOCK
    for c in range(col_count):
        proj = mul(atoms_ref[c, :atom_count, :], w_qkv_ref[...])
        proj_ref[c * atom_count : (c + 1) * atom_count, :] = proj.astype(BF16)
    ctx_ref[:edge, :] = jnp.zeros((edge, channels), BF16)
    ctx_ref[row_atoms - edge :, :] = jnp.zeros((edge, channels), BF16)

    def step(i, carry):
        first = i * (step_blocks * QBLOCK) + edge

        def query_of(b):
            start = pl.multiple_of(first + b * QBLOCK, QBLOCK)
            return proj_ref[pl.ds(start, QBLOCK), :channels]

        def union_of(b, part):
            start = pl.multiple_of(first + b * QBLOCK - HALO, PAD_ROWS)
            return proj_ref[
                pl.ds(start, KWIN + QBLOCK), part * channels : (part + 1) * channels
            ]

        for b, context in enumerate(attend(query_of, union_of, step_blocks)):
            ctx_ref[pl.ds(pl.multiple_of(first + b * QBLOCK, QBLOCK), QBLOCK), :] = context
        return carry

    lax.fori_loop(0, blocks // step_blocks, step, 0)
    wait_all(loads)


def bias_kernel(place_ref, pair_ref, w_ref, after_ref, *refs, place, offset, chunk, loads):
    del after_ref
    sources, out_ref, targets = refs[:loads], refs[loads], refs[loads + 1 : 2 * loads + 1]
    cells_ref, sems, load_sems = refs[2 * loads + 1 :]
    queries, rows, share, width = cells_ref.shape
    keys = rows * share
    heads = w_ref.shape[0]
    count = queries // chunk
    base = place_ref[place] + offset

    def load(i):
        start = pl.multiple_of(i * chunk, chunk)
        return pltpu.make_async_copy(
            pair_ref.at[pl.ds(base + start, chunk)],
            cells_ref.at[pl.ds(start, chunk)],
            sems.at[i],
        )

    for i in range(min(AHEAD, count)):
        load(i).start()
    extra = load_all(sources, targets, load_sems)
    weights = w_ref[...].astype(BF16)
    weight_sum = jnp.sum(weights.astype(F32), axis=1, keepdims=True)
    mean_of = jnp.full((heads, width), 1.0 / width, BF16)
    left = jnp.concatenate([weights, mean_of], axis=0)
    side = heads * SUBLANES
    to_row = lax.broadcasted_iota(jnp.int32, (side, side), 0)
    source = (to_row % SUBLANES) * heads + to_row // SUBLANES
    order = jnp.where(lane_iota((side, side)) == source, 1.0, 0.0).astype(BF16)
    def step(i, carry):
        load(i).wait()

        @pl.when(i + AHEAD < count)
        def _():
            load(i + AHEAD).start()

        start = pl.multiple_of(i * chunk, chunk)
        for q in range(0, chunk, SUBLANES):
            found_rows = []
            for k in range(SUBLANES):
                cells = cells_ref[start + q + k].reshape(keys, width).T
                values = cells.astype(F32)
                found = mul(left, cells)
                dots, center = found[:heads], found[heads:]
                spread = jnp.sum(values * values, axis=0, keepdims=True) * (1.0 / width)
                spread = spread - center * center
                bias = (dots - center * weight_sum) * lax.rsqrt(spread + EPS)
                found_rows.append(bias.astype(BF16))
            ordered = mul(order, jnp.concatenate(found_rows, axis=0))
            rows_at = pl.ds(pl.multiple_of(start + q, SUBLANES), SUBLANES)
            for h in range(heads):
                out_ref[h, rows_at, :] = ordered[h * SUBLANES : (h + 1) * SUBLANES]
        return carry

    lax.fori_loop(0, count, step, 0)
    wait_all(extra)


def pool_kernel(
    place_ref,
    atoms_ref,
    ctx_ref,
    first_ref,
    second_ref,
    w_qkv_ref,
    w_out_ref,
    w_up_ref,
    mine_ref,
    half_ref,
    normed_out_ref,
    act_out_ref,
    my_ref,
    act_ref,
    atom_out_ref,
    *,
    all_atoms,
):
    col_count, packet_rows, channels = atoms_ref.shape
    atom_count = packet_rows - PAD_ROWS
    row_atoms = col_count * atom_count
    half, width = half_ref.shape
    slices, share = mine_ref.shape[:2]
    edge = EDGE_BLOCKS * QBLOCK
    near = edge + HALO
    begin = atoms_ref[0, :near, :]
    end = atoms_ref[col_count - 1, atom_count - near : atom_count, :]
    even = place_ref[7] == 0
    before = jnp.where(even, second_ref[...], first_ref[...])
    after = jnp.where(even, first_ref[...], second_ref[...])
    contexts = []
    for wide, base in (
        (jnp.concatenate([before, begin], axis=0), -HALO),
        (jnp.concatenate([end, after], axis=0), row_atoms - near),
    ):
        proj = mul(wide, w_qkv_ref[...]).astype(BF16)

        def query_of(b):
            return proj[HALO + b * QBLOCK : HALO + (b + 1) * QBLOCK, :channels]

        def union_of(b, part):
            return proj[
                b * QBLOCK : b * QBLOCK + KWIN + QBLOCK, part * channels : (part + 1) * channels
            ]

        def valid_of(b, shape):
            position = place_ref[1] + (base + b * QBLOCK)
            position = position + lax.broadcasted_iota(jnp.int32, shape, 0)
            return (position >= 0) & (position < all_atoms)

        contexts.append(jnp.concatenate(attend(query_of, union_of, EDGE_BLOCKS, valid_of), axis=0))
    rows = half + slices * share
    row = lax.broadcasted_iota(jnp.int32, (rows, LANES), 0)
    token = row + jnp.where(row < half, place_ref[4], place_ref[11] - half)
    token = token.astype(F32)
    counts = jnp.zeros((rows, LANES), F32)
    totals = jnp.zeros((rows, width), F32)
    for c in [*range(1, col_count - 1), 0, col_count - 1]:
        start = c * atom_count
        ctx = ctx_ref[start : start + atom_count, :]
        if c == 0:
            ctx = jnp.concatenate([contexts[0], ctx[edge:]], axis=0)
        if c == col_count - 1:
            ctx = jnp.concatenate([ctx[: atom_count - edge], contexts[1]], axis=0)
        atom_out = atoms_ref[c, :atom_count, :].astype(F32) + mul(ctx, w_out_ref[...])
        atom_out = atom_out.astype(BF16)
        atom_out_ref[c] = atom_out
        up = jnp.maximum(mul(atom_out, w_up_ref[...]), 0.0).astype(BF16)
        names = atoms_ref[c, atom_count:, :].astype(F32)
        hots = []
        for k in range(atom_count // LANES):
            hot = jnp.where(names[k : k + 1, :] == token, 1.0, 0.0)
            counts = counts + hot
            hots.append(hot.astype(BF16))
        totals = totals + mul(jnp.concatenate(hots, axis=1), up)
    token_act = totals / jnp.sum(counts, axis=-1, keepdims=True)
    center = jnp.sum(token_act, axis=-1, keepdims=True) * (1.0 / width)
    spread = jnp.sum(token_act * token_act, axis=-1, keepdims=True) * (1.0 / width)
    spread = spread - center * center
    normed = ((token_act - center) / jnp.sqrt(spread + EPS)).astype(BF16)
    side = place_ref[12]
    for k in range(slices):
        part = normed[half + k * share : half + (k + 1) * share]
        other = normed[half + (1 - k) * share : half + (2 - k) * share]
        mine_ref[k] = jnp.where(side == 0, part, other)
    half_ref[...] = normed[:half]
    act_ref[...] = token_act[:half]
    out_share = act_out_ref.shape[0]
    start = pl.multiple_of(place_ref[9] * out_share, out_share)
    normed_out_ref[...] = half_ref[pl.ds(start, out_share), :]
    act_out_ref[...] = act_ref[pl.ds(start, out_share), :]
    col = place_ref[10]
    my_ref[:atom_count, :] = atom_out_ref[col]
    my_ref[atom_count:, :] = atoms_ref[col, atom_count:, :]


def query_kernel(half_ref, normed_ref, w_query_ref, w_gate_hbm, query_ref, gate_ref, w_gate_ref, sem):
    load = pltpu.make_async_copy(w_gate_hbm, w_gate_ref, sem)
    load.start()
    query_ref[...] = mul(half_ref[...], w_query_ref[...]).astype(BF16)
    load.wait()
    gate_ref[...] = jax.nn.sigmoid(mul(normed_ref[...], w_gate_ref[...]))


def token_kernel(
    place_ref, query_ref, w_kv_ref, early_ref, late_ref, swapped_ref, *refs, row_count, groups
):
    parts, refs = refs[:row_count], refs[row_count:]
    w_out_hbm, w_down_hbm, *refs = refs
    out_refs, refs = refs[:groups], refs[groups:]
    w_out_ref, w_down_ref, keys_ref, packet_ref, sems = refs
    loads = load_all((w_out_hbm, w_down_hbm), (w_out_ref, w_down_ref), sems)
    for k, part in enumerate(parts):
        for i in range(2):
            keys_ref[i, place_ref[8] ^ k] = part[i]
    heads, tok_rows, part_keys = swapped_ref.shape
    key_count = 2 * part_keys
    width = query_ref.shape[1]
    head_size = width // heads
    share = out_refs[0].shape[0]
    keyvals = mul(keys_ref[...].reshape(key_count, width), w_kv_ref[...]).astype(BF16)
    stats = jnp.zeros((tok_rows, LANES), F32)
    lane = lane_iota((tok_rows, LANES))
    tiles = [jnp.zeros((tok_rows, LANES), F32)] * (width // LANES)
    tile_lane = lane_iota((tok_rows, LANES))
    windows = []
    scores = []
    for h in range(heads):
        low = h * head_size // LANES * LANES
        high = min(width, -(-(h + 1) * head_size // LANES) * LANES)
        windows.append((low, high))
        chan = lane_iota((tok_rows, high - low)) + low
        inside = (chan >= h * head_size) & (chan < (h + 1) * head_size)
        query = query_ref[:, low:high]
        query = jnp.where(inside, query, jnp.zeros_like(query))
        scores.append(mul(query, keyvals[:, low:high], NT))
    for h, (low, high) in enumerate(windows):
        score = scores[h] * (1.0 / head_size**0.5)
        kept = jnp.concatenate([early_ref[h], late_ref[h]], axis=0)
        score = score + jnp.concatenate([kept, swapped_ref[h].astype(F32)], axis=1)
        top = jnp.max(score, axis=-1, keepdims=True)
        top_high = top.astype(BF16).astype(F32)
        top_low = (top - top_high).astype(BF16).astype(F32)
        expo = jnp.exp(score - (top_high + top_low))
        denom = jnp.sum(expo, axis=-1, keepdims=True)
        denom_high = denom.astype(BF16).astype(F32)
        stats = jnp.where(lane == h, top_high, stats)
        stats = jnp.where(lane == heads + h, top_low, stats)
        stats = jnp.where(lane == 2 * heads + h, denom_high, stats)
        stats = jnp.where(lane == 3 * heads + h, denom - denom_high, stats)
        mixed = mul(expo.astype(BF16), keyvals[:, width + low : width + high])
        for tile in range(low // LANES, high // LANES):
            chan = tile_lane + tile * LANES
            inside = (chan >= h * head_size) & (chan < (h + 1) * head_size)
            part = mixed[:, tile * LANES - low : (tile + 1) * LANES - low]
            tiles[tile] = jnp.where(inside, part, tiles[tile])
    for tile, values in enumerate(tiles):
        lanes = slice(tile * LANES, (tile + 1) * LANES)
        packet_ref[:, lanes] = values.astype(BF16)
    packet_ref[:, width:] = stats.astype(BF16)
    for k, out_ref in zip(far_first(groups), out_refs):
        start = pl.multiple_of((place_ref[9] ^ k) * share, share)
        out_ref[...] = packet_ref[pl.ds(start, share), :]
    wait_all(loads)


def merge_kernel(*refs, heads, groups):
    part_refs = refs[:groups]
    gate_ref, act_ref, w_out_ref, w_down_ref, out_ref = refs[groups:]
    share = part_refs[0].shape[0]
    col_count = out_ref.shape[0]
    width = w_out_ref.shape[0]
    head_size = width // heads
    chan_share = width // col_count
    stats = jnp.stack([part[:, width:] for part in part_refs]).astype(F32)
    top = stats + pltpu.roll(stats, LANES - heads, 2)
    denom = pltpu.roll(stats, LANES - 2 * heads, 2) + pltpu.roll(stats, LANES - 3 * heads, 2)
    is_head = lane_iota(stats.shape) < heads
    highest = jnp.max(top, axis=0, keepdims=True)
    scale = jnp.where(is_head, jnp.exp(jnp.where(is_head, top - highest, 0.0)), 0.0)
    total = jnp.sum(scale * denom, axis=0, keepdims=True)
    factor = scale / jnp.where(is_head[:1], total, 1.0)
    factor = factor.reshape(groups * share, LANES)
    factor_high = factor.astype(BF16)
    factor_low = (factor - factor_high.astype(F32)).astype(BF16)
    chan_head = lane_iota((LANES, width)) // head_size
    spread = jnp.where(
        chan_head == lax.broadcasted_iota(jnp.int32, (LANES, width), 0), 1.0, 0.0
    ).astype(BF16)
    wide = mul(factor_high, spread) + mul(factor_low, spread)
    wide = wide.reshape(groups, share, width)
    context = sum(part[:, :width].astype(F32) * wide[k] for k, part in enumerate(part_refs))
    gated = (context * gate_ref[...]).astype(BF16)
    updated = act_ref[...] + mul(gated, w_out_ref[...])
    token_out = updated.astype(BF16)
    token_down = mul(token_out, w_down_ref[...]).astype(BF16)
    for c in range(col_count):
        out_ref[c, :, :LANES] = token_down
        out_ref[c, :, LANES : LANES + chan_share] = token_out[
            :, c * chan_share : (c + 1) * chan_share
        ]


def final_kernel(atoms_ref, last_ref, token_ref, atom_ref, *, chan_share):
    col_count, share, _ = last_ref.shape
    tok_rows = col_count * share
    atom_count = atom_ref.shape[0]
    order = sorted(range(col_count), key=lambda c: (c % 2, c // 2))
    last = jnp.concatenate([last_ref[c] for c in order], axis=0)
    token_ref[...] = last[:, LANES : LANES + chan_share].astype(F32).T.astype(BF16)
    names = atoms_ref[atom_count:, :].astype(F32)
    token = lane_iota((LANES, tok_rows)).astype(F32)
    for k in range(atom_count // LANES):
        name = jnp.broadcast_to(names[k : k + 1, :], (LANES, LANES)).T
        name = jnp.concatenate([name] * (tok_rows // LANES), axis=1)
        hot = jnp.where(name == token, 1.0, 0.0).astype(BF16)
        rows = slice(k * LANES, (k + 1) * LANES)
        moved = atoms_ref[rows, :].astype(F32) + mul(hot, last[:, :LANES])
        atom_ref[rows, :] = moved.astype(BF16)


def body(
    atom_feat,
    atom_token,
    w_atom_qkv,
    w_atom_out,
    w_atom_up,
    pair_repr,
    w_bias,
    w_query,
    w_kv,
    w_gate,
    w_out,
    w_down,
):
    row_count = lax.axis_size("row")
    col_count = lax.axis_size("col")
    row_index = lax.axis_index("row")
    col_index = lax.axis_index("col")
    atom_count, channels = atom_feat.shape
    tok_rows, _, share, pair_width = pair_repr.shape
    key_count = row_count * share
    heads = w_bias.shape[1]
    width = w_query.shape[0]
    chan_share = width // col_count
    all_atoms = atom_count * row_count * col_count
    half = tok_rows // 2
    col_groups = col_count // 2
    side, group = col_index & 1, col_index >> 1
    out_share = half // col_groups
    shares = [
        col_index * share,
        (col_index ^ 1) * share,
        side * half,
        (1 - side) * half,
        side * half + group * out_share,
        row_index & 1,
        row_index,
        group,
        col_index,
        group * (2 * share),
        side,
    ]
    place = jnp.stack([col_index, row_index * tok_rows] + shares).astype(jnp.int32)
    edge_place = jnp.stack([col_index, row_index * (atom_count * col_count)] + shares)
    edge_place = edge_place.astype(jnp.int32)
    smem = pl.BlockSpec(memory_space=pltpu.SMEM)
    vmem = pl.BlockSpec(memory_space=pltpu.VMEM)
    hbm = pl.BlockSpec(memory_space=pltpu.HBM)
    unread = pl.BlockSpec(memory_space=pl.ANY)

    def swap(x, axis, step):
        return lax.ppermute(x, axis, [(i, i ^ step) for i in range(lax.axis_size(axis))])

    top = col_count // 2
    far = swap(atom_feat, "col", top)
    far_tokens = swap(atom_token, "col", top)
    token_shape = (atom_count // LANES, LANES)
    tokens, far_tokens = atom_token.reshape(token_shape), far_tokens.reshape(token_shape)

    def pair_bias(place_of, offset, rows, chunk, after, weights):
        loads = len(weights)
        return call(
            functools.partial(
                bias_kernel, place=place_of, offset=offset, chunk=chunk, loads=loads
            ),
            (shape_of((heads, rows, key_count), F32),)
            + tuple(shape_of(x.shape, x.dtype) for x in weights),
            12,
            in_specs=[smem, hbm, vmem, unread] + [hbm] * loads,
            out_specs=(vmem,) * (1 + loads),
            scratch_shapes=[
                pltpu.VMEM((rows,) + pair_repr.shape[1:], BF16),
                pltpu.SemaphoreType.DMA((rows // chunk,)),
                pltpu.SemaphoreType.DMA((max(loads, 1),)),
            ],
        )(place, *in_hbm(pair_repr, w_bias.T), after, *in_hbm(*weights))

    early = half * 3 // 4
    kept, own, own_tokens = pair_bias(4, 0, early, early // 3, place, (atom_feat, tokens))
    packet = call(
        pack_kernel,
        shape_of((2, atom_count + PAD_ROWS, channels), BF16),
        2,
        in_specs=[smem] + [vmem] * 4 + [unread],
        out_specs=vmem,
    )(place, own, own_tokens, far, far_tokens, kept)
    packets = [packet] + [swap(packet, "col", k) for k in range(1, top)]
    other, *atom_weights = pair_bias(
        5, 0, half, half // 4, packet, (w_atom_qkv, w_atom_out, w_atom_up)
    )
    sent, row_atoms, first, second = call(
        edge_kernel,
        (shape_of((heads, half, key_count), BF16), shape_of((col_count, atom_count + PAD_ROWS, channels), BF16))
        + (shape_of((HALO, channels), BF16),) * 2,
        4,
        in_specs=[smem] + [vmem] * (1 + top),
        out_specs=(vmem,) * 4,
    )(place, other, *packets)
    swapped = swap(sent, "col", 1)
    first = swap(first, "row", 1)
    pairs = [(i, ((i + 1) ^ 1) - 1) for i in range(1, row_count - 1)]
    second = lax.ppermute(second, "row", pairs)
    w_qkv, w_mix, w_up = atom_weights
    ctx, w_query, w_kv = call(
        inner_kernel,
        (
            shape_of((col_count * atom_count, channels), BF16),
            shape_of(w_query.shape, BF16),
            shape_of(w_kv.shape, BF16),
        ),
        12,
        in_specs=[vmem] * 2 + [hbm] * 2,
        out_specs=(vmem,) * 3,
        scratch_shapes=[
            pltpu.VMEM((col_count * atom_count, 3 * channels), BF16),
            pltpu.SemaphoreType.DMA((2,)),
        ],
    )(row_atoms, w_qkv, *in_hbm(w_query, w_kv))
    mine, half_normed, normed, act, my_atoms = call(
        functools.partial(pool_kernel, all_atoms=all_atoms),
        (
            shape_of((2, share, width), BF16),
            shape_of((half, width), BF16),
            shape_of((out_share, width), BF16),
            shape_of((out_share, width), F32),
            shape_of((atom_count + PAD_ROWS, channels), BF16),
        ),
        14,
        in_specs=[smem] + [vmem] * 7,
        out_specs=(vmem,) * 5,
        scratch_shapes=[
            pltpu.VMEM((half, width), F32),
            pltpu.VMEM((col_count, atom_count, channels), BF16),
        ],
    )(edge_place, row_atoms, ctx, first, second, w_qkv, w_mix, w_up)
    key_parts = [mine] + [swap(mine, "row", k) for k in range(1, row_count)]
    late = half - early
    (kept_late,) = pair_bias(4, early, late, late, mine, ())
    queries, gate = call(
        query_kernel,
        (shape_of((half, width), BF16), shape_of((out_share, width), F32)),
        6,
        in_specs=[vmem] * 3 + [hbm],
        out_specs=(vmem,) * 2,
        scratch_shapes=[pltpu.VMEM(w_gate.shape, BF16), pltpu.SemaphoreType.DMA],
    )(half_normed, normed, w_query, *in_hbm(w_gate))
    *parts, w_out, w_down = call(
        functools.partial(token_kernel, row_count=row_count, groups=col_groups),
        tuple(shape_of((out_share, width + LANES), BF16) for _ in range(col_groups))
        + (shape_of(w_out.shape, BF16), shape_of(w_down.shape, BF16)),
        14,
        in_specs=[smem] + [vmem] * (5 + row_count) + [hbm] * 2,
        out_specs=(vmem,) * (col_groups + 2),
        scratch_shapes=[
            pltpu.VMEM((2, row_count, share, width), BF16),
            pltpu.VMEM((half, width + LANES), BF16),
            pltpu.SemaphoreType.DMA((2,)),
        ],
    )(place, queries, w_kv, kept, kept_late, swapped, *key_parts, *in_hbm(w_out, w_down))
    parts = parts[:1] + [
        lax.ppermute(part, "col", [(c, c ^ (2 * k)) for c in range(col_count)])
        for k, part in zip(far_first(col_groups), parts)
        if k > 0
    ]
    last = call(
        functools.partial(merge_kernel, heads=heads, groups=col_groups),
        shape_of((col_count, out_share, 2 * LANES), BF16),
        8,
        in_specs=[vmem] * (col_groups + 4),
        out_specs=vmem,
    )(*parts, gate, act, w_out, w_down)
    last = lax.all_to_all(last, "col", 0, 0)
    token_share, atom_final = call(
        functools.partial(final_kernel, chan_share=chan_share),
        (shape_of((chan_share, tok_rows), BF16), shape_of((atom_count, channels), BF16)),
        4,
        in_specs=[vmem] * 2,
        out_specs=(vmem,) * 2,
    )(my_atoms, last)
    return (token_share.T, atom_final)


def solution(mesh):
    return jax.shard_map(
        body,
        mesh=mesh,
        in_specs=(
            P(("row", "col"), None),
            P(("row", "col")),
            P(),
            P(),
            P(),
            P("row", None, "col", None),
            P(),
            P(),
            P(),
            P(),
            P(),
            P(),
        ),
        out_specs=(P("row", "col"), P(("row", "col"), None)),
        check_vma=False,
    )
```

```python
import functools

import jax
import jax.numpy as jnp
from jax import lax
from jax.experimental import pallas as pl
from jax.experimental.pallas import tpu as pltpu
from jax.sharding import PartitionSpec as P

AHEADS = 4
QBLOCK = 32
KWIN = 128
HALO = 48
LANES = 128
AHEAD = 4
PAD_ROWS = 16
EDGE_BLOCKS = 2
EPS = 1e-05
LOG2_E = 1.4426950408889634
F32 = jnp.float32
BF16 = jnp.bfloat16
MIB = 1024 * 1024

NT = (((1,), (1,)), ((), ()))
NN = (((1,), (0,)), ((), ()))
TN = (((0,), (0,)), ((), ()))


def mul(a, b, dims=NN):
    return lax.dot_general(a, b, dims, preferred_element_type=F32)


def call(kernel, out_shape, vmem_mib, **kwargs):
    return pl.pallas_call(
        kernel,
        out_shape=out_shape,
        compiler_params=pltpu.CompilerParams(vmem_limit_bytes=vmem_mib * MIB),
        **kwargs,
    )


def shape_of(shape, dtype):
    return jax.ShapeDtypeStruct(shape, dtype)


def far_first(count):
    return [0] + list(range(count - 1, 0, -1))


def lane_iota(shape):
    return lax.broadcasted_iota(jnp.int32, shape, len(shape) - 1)


def in_hbm(*arrays):
    return tuple(pltpu.with_memory_space_constraint(x, pltpu.HBM) for x in arrays)


def load_all(sources, targets, sems):
    copies = [
        pltpu.make_async_copy(source, target, sems.at[i])
        for i, (source, target) in enumerate(zip(sources, targets))
    ]
    for copy in copies:
        copy.start()
    return copies


def wait_all(copies):
    for copy in copies:
        copy.wait()


def pack_kernel(place_ref, own_ref, token_ref, far_ref, far_token_ref, after_ref, out_ref):
    del after_ref
    atom_count = own_ref.shape[0]
    token_rows = token_ref.shape[0]
    blank = jnp.zeros((PAD_ROWS - token_rows, LANES), F32)
    for k, (feat, token) in enumerate(((own_ref, token_ref), (far_ref, far_token_ref))):
        out_ref[k, :atom_count, :] = feat[...]
        names = (token[...] - place_ref[1]).astype(F32)
        out_ref[k, atom_count:, :] = jnp.concatenate([names, blank], axis=0).astype(BF16)


def edge_kernel(place_ref, bias_ref, *refs):
    packets, (sent_ref, atoms_ref, first_ref, second_ref) = refs[:-4], refs[-4:]
    sent_ref[...] = bias_ref[...].astype(BF16)
    col_count, packet_rows, _ = atoms_ref.shape
    atom_count = packet_rows - PAD_ROWS
    for k, packet in enumerate(packets):
        for j in range(2):
            atoms_ref[place_ref[10] ^ (k + j * (col_count // 2))] = packet[j]
    tail = atoms_ref[col_count - 1, atom_count - HALO : atom_count, :]
    head = atoms_ref[0, :HALO, :]
    even = place_ref[7] == 0
    first_ref[...] = jnp.where(even, tail, head)
    second_ref[...] = jnp.where(even, head, tail)


def attend(query_of, union_of, blocks, valid_of=None):
    channels = query_of(0).shape[1]
    head_size = channels // AHEADS
    rows_of = AHEADS * QBLOCK
    head_of = lane_iota((QBLOCK, channels)) // head_size
    picks = [head_of == h for h in range(AHEADS)]
    scores = []
    for b in range(0, blocks, 2):
        stacked = []
        for query in (query_of(b), query_of(b + 1)):
            stacked += [jnp.where(pick, query, jnp.zeros_like(query)) for pick in picks]
        found = mul(union_of(b, 1), jnp.concatenate(stacked, axis=0), NT)
        scores += [found[:KWIN, :rows_of], found[QBLOCK:, rows_of:]]
    blank = jnp.zeros((KWIN, channels), BF16)
    row = lax.broadcasted_iota(jnp.int32, (PAD_ROWS, channels), 0)
    pair_rows = jnp.where(row < 2, 1.0, 0.0).astype(BF16)
    sum_rows = jnp.concatenate([blank[:PAD_ROWS], pair_rows], axis=1)
    contexts = []
    for b in range(blocks):
        score = scores[b]
        if valid_of is not None:
            score = jnp.where(valid_of(b, score.shape), score, -1e30)
        score = score - jnp.max(score, axis=0, keepdims=True)
        expo = jnp.exp2(score * (LOG2_E / head_size**0.5))
        denom = jnp.sum(expo, axis=0, keepdims=True)
        denom_high = denom.astype(BF16).astype(F32)
        sums = jnp.where(row == 0, denom_high, jnp.where(row == 1, denom - denom_high, 0.0))
        weights = jnp.concatenate([expo.astype(BF16), sums.astype(BF16)], axis=0)
        start = b % 2 * QBLOCK
        values = union_of(b - b % 2, 2)[start : start + KWIN]
        values = jnp.concatenate([values, blank], axis=1)
        mixed = mul(weights, jnp.concatenate([values, sum_rows], axis=0), TN)
        context = mixed[:QBLOCK]
        for h in range(1, AHEADS):
            pick = jnp.concatenate([picks[h]] * 2, axis=1)
            context = jnp.where(pick, mixed[h * QBLOCK : (h + 1) * QBLOCK], context)
        contexts.append((context[:, :channels] / context[:, channels:]).astype(BF16))
    return contexts


def inner_kernel(
    atoms_ref, w_qkv_ref, w_query_hbm, w_kv_hbm, ctx_ref, w_query_ref, w_kv_ref, proj_ref, sems
):
    loads = load_all((w_query_hbm, w_kv_hbm), (w_query_ref, w_kv_ref), sems)
    col_count, packet_rows, channels = atoms_ref.shape
    atom_count = packet_rows - PAD_ROWS
    row_atoms = col_count * atom_count
    blocks = row_atoms // QBLOCK - 2 * EDGE_BLOCKS
    step_blocks = max(n for n in range(2, 21, 2) if blocks % n == 0)
    edge = EDGE_BLOCKS * QBLOCK
    for c in range(col_count):
        proj = mul(atoms_ref[c, :atom_count, :], w_qkv_ref[...])
        proj_ref[c * atom_count : (c + 1) * atom_count, :] = proj.astype(BF16)
    ctx_ref[:edge, :] = jnp.zeros((edge, channels), BF16)
    ctx_ref[row_atoms - edge :, :] = jnp.zeros((edge, channels), BF16)

    def step(i, carry):
        first = i * (step_blocks * QBLOCK) + edge

        def query_of(b):
            start = pl.multiple_of(first + b * QBLOCK, QBLOCK)
            return proj_ref[pl.ds(start, QBLOCK), :channels]

        def union_of(b, part):
            start = pl.multiple_of(first + b * QBLOCK - HALO, PAD_ROWS)
            return proj_ref[
                pl.ds(start, KWIN + QBLOCK), part * channels : (part + 1) * channels
            ]

        for b, context in enumerate(attend(query_of, union_of, step_blocks)):
            ctx_ref[pl.ds(pl.multiple_of(first + b * QBLOCK, QBLOCK), QBLOCK), :] = context
        return carry

    lax.fori_loop(0, blocks // step_blocks, step, 0)
    wait_all(loads)


def bias_kernel(place_ref, pair_ref, w_ref, after_ref, *refs, place, offset, chunk, loads):
    del after_ref
    sources, out_ref, targets = refs[:loads], refs[loads], refs[loads + 1 : 2 * loads + 1]
    cells_ref, sems, load_sems = refs[2 * loads + 1 :]
    queries, rows, share, width = cells_ref.shape
    keys = rows * share
    heads = w_ref.shape[0]
    count = queries // chunk
    base = place_ref[place] + offset

    def load(i):
        start = pl.multiple_of(i * chunk, chunk)
        return pltpu.make_async_copy(
            pair_ref.at[pl.ds(base + start, chunk)],
            cells_ref.at[pl.ds(start, chunk)],
            sems.at[i],
        )

    for i in range(min(AHEAD, count)):
        load(i).start()
    extra = load_all(sources, targets, load_sems)
    weights = w_ref[...].astype(BF16)
    weight_sum = jnp.sum(weights.astype(F32), axis=1, keepdims=True)
    mean_of = jnp.full((heads, width), 1.0 / width, BF16)
    left = jnp.concatenate([weights, mean_of], axis=0)
    def step(i, carry):
        load(i).wait()

        @pl.when(i + AHEAD < count)
        def _():
            load(i + AHEAD).start()

        start = pl.multiple_of(i * chunk, chunk)
        for q in range(chunk):
            cells = cells_ref[start + q].reshape(keys, width).T
            values = cells.astype(F32)
            found = mul(left, cells)
            dots, center = found[:heads], found[heads:]
            spread = jnp.sum(values * values, axis=0, keepdims=True) * (1.0 / width)
            spread = spread - center * center
            bias = (dots - center * weight_sum) * lax.rsqrt(spread + EPS)
            out_ref[:, start + q, :] = bias.astype(BF16).astype(F32)
        return carry

    lax.fori_loop(0, count, step, 0)
    wait_all(extra)


def pool_kernel(
    place_ref,
    atoms_ref,
    ctx_ref,
    first_ref,
    second_ref,
    w_qkv_ref,
    w_out_ref,
    w_up_ref,
    mine_ref,
    half_ref,
    normed_out_ref,
    act_out_ref,
    my_ref,
    act_ref,
    atom_out_ref,
    *,
    all_atoms,
):
    col_count, packet_rows, channels = atoms_ref.shape
    atom_count = packet_rows - PAD_ROWS
    row_atoms = col_count * atom_count
    half, width = half_ref.shape
    slices, share = mine_ref.shape[:2]
    edge = EDGE_BLOCKS * QBLOCK
    near = edge + HALO
    begin = atoms_ref[0, :near, :]
    end = atoms_ref[col_count - 1, atom_count - near : atom_count, :]
    even = place_ref[7] == 0
    before = jnp.where(even, second_ref[...], first_ref[...])
    after = jnp.where(even, first_ref[...], second_ref[...])
    contexts = []
    for wide, base in (
        (jnp.concatenate([before, begin], axis=0), -HALO),
        (jnp.concatenate([end, after], axis=0), row_atoms - near),
    ):
        proj = mul(wide, w_qkv_ref[...]).astype(BF16)

        def query_of(b):
            return proj[HALO + b * QBLOCK : HALO + (b + 1) * QBLOCK, :channels]

        def union_of(b, part):
            return proj[
                b * QBLOCK : b * QBLOCK + KWIN + QBLOCK, part * channels : (part + 1) * channels
            ]

        def valid_of(b, shape):
            position = place_ref[1] + (base + b * QBLOCK)
            position = position + lax.broadcasted_iota(jnp.int32, shape, 0)
            return (position >= 0) & (position < all_atoms)

        contexts.append(jnp.concatenate(attend(query_of, union_of, EDGE_BLOCKS, valid_of), axis=0))
    rows = half + slices * share
    row = lax.broadcasted_iota(jnp.int32, (rows, LANES), 0)
    token = row + jnp.where(row < half, place_ref[4], place_ref[11] - half)
    token = token.astype(F32)
    counts = jnp.zeros((rows, LANES), F32)
    totals = jnp.zeros((rows, width), F32)
    for c in [*range(1, col_count - 1), 0, col_count - 1]:
        start = c * atom_count
        ctx = ctx_ref[start : start + atom_count, :]
        if c == 0:
            ctx = jnp.concatenate([contexts[0], ctx[edge:]], axis=0)
        if c == col_count - 1:
            ctx = jnp.concatenate([ctx[: atom_count - edge], contexts[1]], axis=0)
        atom_out = atoms_ref[c, :atom_count, :].astype(F32) + mul(ctx, w_out_ref[...])
        atom_out = atom_out.astype(BF16)
        atom_out_ref[c] = atom_out
        up = jnp.maximum(mul(atom_out, w_up_ref[...]), 0.0).astype(BF16)
        names = atoms_ref[c, atom_count:, :].astype(F32)
        hots = []
        for k in range(atom_count // LANES):
            hot = jnp.where(names[k : k + 1, :] == token, 1.0, 0.0)
            counts = counts + hot
            hots.append(hot.astype(BF16))
        totals = totals + mul(jnp.concatenate(hots, axis=1), up)
    token_act = totals / jnp.sum(counts, axis=-1, keepdims=True)
    center = jnp.sum(token_act, axis=-1, keepdims=True) * (1.0 / width)
    spread = jnp.sum(token_act * token_act, axis=-1, keepdims=True) * (1.0 / width)
    spread = spread - center * center
    normed = ((token_act - center) / jnp.sqrt(spread + EPS)).astype(BF16)
    side = place_ref[12]
    for k in range(slices):
        part = normed[half + k * share : half + (k + 1) * share]
        other = normed[half + (1 - k) * share : half + (2 - k) * share]
        mine_ref[k] = jnp.where(side == 0, part, other)
    half_ref[...] = normed[:half]
    act_ref[...] = token_act[:half]
    out_share = act_out_ref.shape[0]
    start = pl.multiple_of(place_ref[9] * out_share, out_share)
    normed_out_ref[...] = half_ref[pl.ds(start, out_share), :]
    act_out_ref[...] = act_ref[pl.ds(start, out_share), :]
    col = place_ref[10]
    my_ref[:atom_count, :] = atom_out_ref[col]
    my_ref[atom_count:, :] = atoms_ref[col, atom_count:, :]


def relay_kernel(after_ref, *refs):
    del after_ref
    count = len(refs) // 2
    for source, target in zip(refs[:count], refs[count:]):
        target[...] = source[...]


def query_kernel(half_ref, normed_ref, w_query_ref, w_gate_ref, after_ref, query_ref, gate_ref):
    del after_ref
    query_ref[...] = mul(half_ref[...], w_query_ref[...]).astype(BF16)
    gate_ref[...] = jax.nn.sigmoid(mul(normed_ref[...], w_gate_ref[...]))


def token_kernel(
    place_ref, query_ref, w_kv_ref, early_ref, late_ref, swapped_ref, *refs, row_count, groups
):
    parts, refs = refs[:row_count], refs[row_count:]
    w_out_hbm, w_down_hbm, *refs = refs
    out_refs, refs = refs[:groups], refs[groups:]
    w_out_ref, w_down_ref, keys_ref, packet_ref, sems = refs
    loads = load_all((w_out_hbm, w_down_hbm), (w_out_ref, w_down_ref), sems)
    for k, part in enumerate(parts):
        for i in range(2):
            keys_ref[i, place_ref[8] ^ k] = part[i]
    heads, tok_rows, part_keys = swapped_ref.shape
    key_count = 2 * part_keys
    width = query_ref.shape[1]
    head_size = width // heads
    share = out_refs[0].shape[0]
    keyvals = mul(keys_ref[...].reshape(key_count, width), w_kv_ref[...]).astype(BF16)
    stats = jnp.zeros((tok_rows, LANES), F32)
    lane = lane_iota((tok_rows, LANES))
    tiles = [jnp.zeros((tok_rows, LANES), F32)] * (width // LANES)
    tile_lane = lane_iota((tok_rows, LANES))
    windows = []
    scores = []
    for h in range(heads):
        low = h * head_size // LANES * LANES
        high = min(width, -(-(h + 1) * head_size // LANES) * LANES)
        windows.append((low, high))
        chan = lane_iota((tok_rows, high - low)) + low
        inside = (chan >= h * head_size) & (chan < (h + 1) * head_size)
        query = query_ref[:, low:high]
        query = jnp.where(inside, query, jnp.zeros_like(query))
        scores.append(mul(query, keyvals[:, low:high], NT))
    for h, (low, high) in enumerate(windows):
        score = scores[h] * (1.0 / head_size**0.5)
        kept = jnp.concatenate([early_ref[h], late_ref[h]], axis=0)
        score = score + jnp.concatenate([kept, swapped_ref[h].astype(F32)], axis=1)
        top = jnp.max(score, axis=-1, keepdims=True)
        top_high = top.astype(BF16).astype(F32)
        top_low = (top - top_high).astype(BF16).astype(F32)
        expo = jnp.exp(score - (top_high + top_low))
        denom = jnp.sum(expo, axis=-1, keepdims=True)
        denom_high = denom.astype(BF16).astype(F32)
        stats = jnp.where(lane == h, top_high, stats)
        stats = jnp.where(lane == heads + h, top_low, stats)
        stats = jnp.where(lane == 2 * heads + h, denom_high, stats)
        stats = jnp.where(lane == 3 * heads + h, denom - denom_high, stats)
        mixed = mul(expo.astype(BF16), keyvals[:, width + low : width + high])
        for tile in range(low // LANES, high // LANES):
            chan = tile_lane + tile * LANES
            inside = (chan >= h * head_size) & (chan < (h + 1) * head_size)
            part = mixed[:, tile * LANES - low : (tile + 1) * LANES - low]
            tiles[tile] = jnp.where(inside, part, tiles[tile])
    for tile, values in enumerate(tiles):
        lanes = slice(tile * LANES, (tile + 1) * LANES)
        packet_ref[:, lanes] = values.astype(BF16)
    packet_ref[:, width:] = stats.astype(BF16)
    for k, out_ref in zip(far_first(groups), out_refs):
        start = pl.multiple_of((place_ref[9] ^ k) * share, share)
        out_ref[...] = packet_ref[pl.ds(start, share), :]
    wait_all(loads)


def merge_kernel(*refs, heads, groups):
    part_refs = refs[:groups]
    gate_ref, act_ref, w_out_ref, w_down_ref, out_ref = refs[groups:]
    share = part_refs[0].shape[0]
    col_count = out_ref.shape[0]
    width = w_out_ref.shape[0]
    head_size = width // heads
    chan_share = width // col_count
    stats = jnp.stack([part[:, width:] for part in part_refs]).astype(F32)
    top = stats + pltpu.roll(stats, LANES - heads, 2)
    denom = pltpu.roll(stats, LANES - 2 * heads, 2) + pltpu.roll(stats, LANES - 3 * heads, 2)
    is_head = lane_iota(stats.shape) < heads
    highest = jnp.max(top, axis=0, keepdims=True)
    scale = jnp.where(is_head, jnp.exp(jnp.where(is_head, top - highest, 0.0)), 0.0)
    total = jnp.sum(scale * denom, axis=0, keepdims=True)
    factor = scale / jnp.where(is_head[:1], total, 1.0)
    factor = factor.reshape(groups * share, LANES)
    factor_high = factor.astype(BF16)
    factor_low = (factor - factor_high.astype(F32)).astype(BF16)
    chan_head = lane_iota((LANES, width)) // head_size
    spread = jnp.where(
        chan_head == lax.broadcasted_iota(jnp.int32, (LANES, width), 0), 1.0, 0.0
    ).astype(BF16)
    wide = mul(factor_high, spread) + mul(factor_low, spread)
    wide = wide.reshape(groups, share, width)
    context = sum(part[:, :width].astype(F32) * wide[k] for k, part in enumerate(part_refs))
    gated = (context * gate_ref[...]).astype(BF16)
    updated = act_ref[...] + mul(gated, w_out_ref[...])
    token_out = updated.astype(BF16)
    token_down = mul(token_out, w_down_ref[...]).astype(BF16)
    for c in range(col_count):
        out_ref[c, :, :LANES] = token_down
        out_ref[c, :, LANES : LANES + chan_share] = token_out[
            :, c * chan_share : (c + 1) * chan_share
        ]


def final_kernel(atoms_ref, last_ref, token_ref, atom_ref, *, chan_share):
    col_count, share, _ = last_ref.shape
    tok_rows = col_count * share
    atom_count = atom_ref.shape[0]
    order = sorted(range(col_count), key=lambda c: (c % 2, c // 2))
    last = jnp.concatenate([last_ref[c] for c in order], axis=0)
    token_ref[...] = last[:, LANES : LANES + chan_share].astype(F32).T.astype(BF16)
    names = atoms_ref[atom_count:, :].astype(F32)
    token = lane_iota((LANES, tok_rows)).astype(F32)
    for k in range(atom_count // LANES):
        name = jnp.broadcast_to(names[k : k + 1, :], (LANES, LANES)).T
        name = jnp.concatenate([name] * (tok_rows // LANES), axis=1)
        hot = jnp.where(name == token, 1.0, 0.0).astype(BF16)
        rows = slice(k * LANES, (k + 1) * LANES)
        moved = atoms_ref[rows, :].astype(F32) + mul(hot, last[:, :LANES])
        atom_ref[rows, :] = moved.astype(BF16)


def body(
    atom_feat,
    atom_token,
    w_atom_qkv,
    w_atom_out,
    w_atom_up,
    pair_repr,
    w_bias,
    w_query,
    w_kv,
    w_gate,
    w_out,
    w_down,
):
    row_count = lax.axis_size("row")
    col_count = lax.axis_size("col")
    row_index = lax.axis_index("row")
    col_index = lax.axis_index("col")
    atom_count, channels = atom_feat.shape
    tok_rows, _, share, pair_width = pair_repr.shape
    key_count = row_count * share
    heads = w_bias.shape[1]
    width = w_query.shape[0]
    chan_share = width // col_count
    all_atoms = atom_count * row_count * col_count
    half = tok_rows // 2
    col_groups = col_count // 2
    side, group = col_index & 1, col_index >> 1
    out_share = half // col_groups
    shares = [
        col_index * share,
        (col_index ^ 1) * share,
        side * half,
        (1 - side) * half,
        side * half + group * out_share,
        row_index & 1,
        row_index,
        group,
        col_index,
        group * (2 * share),
        side,
    ]
    place = jnp.stack([col_index, row_index * tok_rows] + shares).astype(jnp.int32)
    edge_place = jnp.stack([col_index, row_index * (atom_count * col_count)] + shares)
    edge_place = edge_place.astype(jnp.int32)
    smem = pl.BlockSpec(memory_space=pltpu.SMEM)
    vmem = pl.BlockSpec(memory_space=pltpu.VMEM)
    hbm = pl.BlockSpec(memory_space=pltpu.HBM)
    unread = pl.BlockSpec(memory_space=pl.ANY)

    def swap(x, axis, step):
        return lax.ppermute(x, axis, [(i, i ^ step) for i in range(lax.axis_size(axis))])

    top = col_count // 2
    far = swap(atom_feat, "col", top)
    far_tokens = swap(atom_token, "col", top)
    token_shape = (atom_count // LANES, LANES)
    tokens, far_tokens = atom_token.reshape(token_shape), far_tokens.reshape(token_shape)

    def pair_bias(place_of, offset, rows, chunk, after, weights):
        loads = len(weights)
        return call(
            functools.partial(
                bias_kernel, place=place_of, offset=offset, chunk=chunk, loads=loads
            ),
            (shape_of((heads, rows, key_count), F32),)
            + tuple(shape_of(x.shape, x.dtype) for x in weights),
            12,
            in_specs=[smem, hbm, vmem, unread] + [hbm] * loads,
            out_specs=(vmem,) * (1 + loads),
            scratch_shapes=[
                pltpu.VMEM((rows,) + pair_repr.shape[1:], BF16),
                pltpu.SemaphoreType.DMA((rows // chunk,)),
                pltpu.SemaphoreType.DMA((max(loads, 1),)),
            ],
        )(place, *in_hbm(pair_repr, w_bias.T), after, *in_hbm(*weights))

    early = half * 5 // 8
    kept, own, own_tokens = pair_bias(4, 0, early, early // 2, place, (atom_feat, tokens))
    packet = call(
        pack_kernel,
        shape_of((2, atom_count + PAD_ROWS, channels), BF16),
        2,
        in_specs=[smem] + [vmem] * 4 + [unread],
        out_specs=vmem,
    )(place, own, own_tokens, far, far_tokens, kept)
    packets = [packet] + [swap(packet, "col", k) for k in range(1, top)]
    other, *atom_weights = pair_bias(
        5, 0, half, half // 4, packet, (w_atom_qkv, w_atom_out, w_atom_up)
    )
    sent, row_atoms, first, second = call(
        edge_kernel,
        (shape_of((heads, half, key_count), BF16), shape_of((col_count, atom_count + PAD_ROWS, channels), BF16))
        + (shape_of((HALO, channels), BF16),) * 2,
        4,
        in_specs=[smem] + [vmem] * (1 + top),
        out_specs=(vmem,) * 4,
    )(place, other, *packets)
    swapped = swap(sent, "col", 1)
    first = swap(first, "row", 1)
    pairs = [(i, ((i + 1) ^ 1) - 1) for i in range(1, row_count - 1)]
    second = lax.ppermute(second, "row", pairs)
    w_qkv, w_mix, w_up = atom_weights
    ctx, w_query, w_kv = call(
        inner_kernel,
        (
            shape_of((col_count * atom_count, channels), BF16),
            shape_of(w_query.shape, BF16),
            shape_of(w_kv.shape, BF16),
        ),
        12,
        in_specs=[vmem] * 2 + [hbm] * 2,
        out_specs=(vmem,) * 3,
        scratch_shapes=[
            pltpu.VMEM((col_count * atom_count, 3 * channels), BF16),
            pltpu.SemaphoreType.DMA((2,)),
        ],
    )(row_atoms, w_qkv, *in_hbm(w_query, w_kv))
    mine, half_normed, normed, act, my_atoms = call(
        functools.partial(pool_kernel, all_atoms=all_atoms),
        (
            shape_of((2, share, width), BF16),
            shape_of((half, width), BF16),
            shape_of((out_share, width), BF16),
            shape_of((out_share, width), F32),
            shape_of((atom_count + PAD_ROWS, channels), BF16),
        ),
        14,
        in_specs=[smem] + [vmem] * 7,
        out_specs=(vmem,) * 5,
        scratch_shapes=[
            pltpu.VMEM((half, width), F32),
            pltpu.VMEM((col_count, atom_count, channels), BF16),
        ],
    )(edge_place, row_atoms, ctx, first, second, w_qkv, w_mix, w_up)
    far_parts = [swap(mine, "row", k) for k in range(2, row_count, 2)]
    near_part = swap(mine, "row", 1)
    late = half - early
    kept_late, w_gate = pair_bias(4, early, late, late // 2, mine, (w_gate,))
    relayed = call(
        relay_kernel,
        (shape_of(mine.shape, BF16),) * len(far_parts),
        4,
        in_specs=[unread] + [vmem] * len(far_parts),
        out_specs=(vmem,) * len(far_parts),
    )(kept_late, *far_parts)
    key_parts = [mine, near_part]
    for part in relayed:
        key_parts += [part, swap(part, "row", 1)]
    queries, gate = call(
        query_kernel,
        (shape_of((half, width), BF16), shape_of((out_share, width), F32)),
        6,
        in_specs=[vmem] * 4 + [unread],
        out_specs=(vmem,) * 2,
    )(half_normed, normed, w_query, w_gate, relayed[0])
    *parts, w_out, w_down = call(
        functools.partial(token_kernel, row_count=row_count, groups=col_groups),
        tuple(shape_of((out_share, width + LANES), BF16) for _ in range(col_groups))
        + (shape_of(w_out.shape, BF16), shape_of(w_down.shape, BF16)),
        14,
        in_specs=[smem] + [vmem] * (5 + row_count) + [hbm] * 2,
        out_specs=(vmem,) * (col_groups + 2),
        scratch_shapes=[
            pltpu.VMEM((2, row_count, share, width), BF16),
            pltpu.VMEM((half, width + LANES), BF16),
            pltpu.SemaphoreType.DMA((2,)),
        ],
    )(place, queries, w_kv, kept, kept_late, swapped, *key_parts, *in_hbm(w_out, w_down))
    parts = parts[:1] + [
        lax.ppermute(part, "col", [(c, c ^ (2 * k)) for c in range(col_count)])
        for k, part in zip(far_first(col_groups), parts)
        if k > 0
    ]
    last = call(
        functools.partial(merge_kernel, heads=heads, groups=col_groups),
        shape_of((col_count, out_share, 2 * LANES), BF16),
        8,
        in_specs=[vmem] * (col_groups + 4),
        out_specs=vmem,
    )(*parts, gate, act, w_out, w_down)
    last = lax.all_to_all(last, "col", 0, 0)
    token_share, atom_final = call(
        functools.partial(final_kernel, chan_share=chan_share),
        (shape_of((chan_share, tok_rows), BF16), shape_of((atom_count, channels), BF16)),
        4,
        in_specs=[vmem] * 2,
        out_specs=(vmem,) * 2,
    )(my_atoms, last)
    return (token_share.T, atom_final)


def solution(mesh):
    return jax.shard_map(
        body,
        mesh=mesh,
        in_specs=(
            P(("row", "col"), None),
            P(("row", "col")),
            P(),
            P(),
            P(),
            P("row", None, "col", None),
            P(),
            P(),
            P(),
            P(),
            P(),
            P(),
        ),
        out_specs=(P("row", "col"), P(("row", "col"), None)),
        check_vma=False,
    )
```

```python
import functools

import jax
import jax.numpy as jnp
from jax import lax
from jax.experimental import pallas as pl
from jax.experimental.pallas import tpu as pltpu
from jax.sharding import PartitionSpec as P

AHEADS = 4
QBLOCK = 32
KWIN = 128
HALO = 48
LANES = 128
PAD_ROWS = 16
EDGE_BLOCKS = 2
EPS = 1e-05
LOG2_E = 1.4426950408889634
F32 = jnp.float32
BF16 = jnp.bfloat16
MIB = 1024 * 1024

NT = (((1,), (1,)), ((), ()))
NN = (((1,), (0,)), ((), ()))
TN = (((0,), (0,)), ((), ()))


def mul(a, b, dims=NN):
    return lax.dot_general(a, b, dims, preferred_element_type=F32)


def call(kernel, out_shape, vmem_mib, **kwargs):
    return pl.pallas_call(
        kernel,
        out_shape=out_shape,
        compiler_params=pltpu.CompilerParams(vmem_limit_bytes=vmem_mib * MIB),
        **kwargs,
    )


def shape_of(shape, dtype):
    return jax.ShapeDtypeStruct(shape, dtype)


def far_first(count):
    return [0] + list(range(count - 1, 0, -1))


def lane_iota(shape):
    return lax.broadcasted_iota(jnp.int32, shape, len(shape) - 1)


def in_hbm(*arrays):
    return tuple(pltpu.with_memory_space_constraint(x, pltpu.HBM) for x in arrays)


def load_all(sources, targets, sems):
    copies = [
        pltpu.make_async_copy(source, target, sems.at[i])
        for i, (source, target) in enumerate(zip(sources, targets))
    ]
    for copy in copies:
        copy.start()
    return copies


def wait_all(copies):
    for copy in copies:
        copy.wait()


def pack_kernel(place_ref, own_ref, token_ref, far_ref, far_token_ref, after_ref, out_ref):
    del after_ref
    atom_count = own_ref.shape[0]
    token_rows = token_ref.shape[0]
    blank = jnp.zeros((PAD_ROWS - token_rows, LANES), F32)
    for k, (feat, token) in enumerate(((own_ref, token_ref), (far_ref, far_token_ref))):
        out_ref[k, :atom_count, :] = feat[...]
        names = (token[...] - place_ref[1]).astype(F32)
        out_ref[k, atom_count:, :] = jnp.concatenate([names, blank], axis=0).astype(BF16)


def edge_kernel(place_ref, bias_ref, *refs):
    packets, (sent_ref, atoms_ref, first_ref, second_ref) = refs[:-4], refs[-4:]
    sent_ref[...] = bias_ref[...].astype(BF16)
    col_count, packet_rows, _ = atoms_ref.shape
    atom_count = packet_rows - PAD_ROWS
    for k, packet in enumerate(packets):
        for j in range(2):
            atoms_ref[place_ref[10] ^ (k + j * (col_count // 2))] = packet[j]
    tail = atoms_ref[col_count - 1, atom_count - HALO : atom_count, :]
    head = atoms_ref[0, :HALO, :]
    even = place_ref[7] == 0
    first_ref[...] = jnp.where(even, tail, head)
    second_ref[...] = jnp.where(even, head, tail)


def attend(query_of, union_of, blocks, valid_of=None):
    channels = query_of(0).shape[1]
    head_size = channels // AHEADS
    rows_of = AHEADS * QBLOCK
    head_of = lane_iota((QBLOCK, channels)) // head_size
    picks = [head_of == h for h in range(AHEADS)]
    scores = []
    for b in range(0, blocks, 2):
        stacked = []
        for query in (query_of(b), query_of(b + 1)):
            stacked += [jnp.where(pick, query, jnp.zeros_like(query)) for pick in picks]
        found = mul(union_of(b, 1), jnp.concatenate(stacked, axis=0), NT)
        scores += [found[:KWIN, :rows_of], found[QBLOCK:, rows_of:]]
    blank = jnp.zeros((KWIN, channels), BF16)
    row = lax.broadcasted_iota(jnp.int32, (PAD_ROWS, channels), 0)
    pair_rows = jnp.where(row < 2, 1.0, 0.0).astype(BF16)
    sum_rows = jnp.concatenate([blank[:PAD_ROWS], pair_rows], axis=1)
    contexts = []
    for b in range(blocks):
        score = scores[b]
        if valid_of is not None:
            score = jnp.where(valid_of(b, score.shape), score, -1e30)
        score = score - jnp.max(score, axis=0, keepdims=True)
        expo = jnp.exp2(score * (LOG2_E / head_size**0.5))
        denom = jnp.sum(expo, axis=0, keepdims=True)
        denom_high = denom.astype(BF16).astype(F32)
        sums = jnp.where(row == 0, denom_high, jnp.where(row == 1, denom - denom_high, 0.0))
        weights = jnp.concatenate([expo.astype(BF16), sums.astype(BF16)], axis=0)
        start = b % 2 * QBLOCK
        values = union_of(b - b % 2, 2)[start : start + KWIN]
        values = jnp.concatenate([values, blank], axis=1)
        mixed = mul(weights, jnp.concatenate([values, sum_rows], axis=0), TN)
        context = mixed[:QBLOCK]
        for h in range(1, AHEADS):
            pick = jnp.concatenate([picks[h]] * 2, axis=1)
            context = jnp.where(pick, mixed[h * QBLOCK : (h + 1) * QBLOCK], context)
        contexts.append((context[:, :channels] / context[:, channels:]).astype(BF16))
    return contexts


def inner_kernel(
    atoms_ref, w_qkv_ref, w_query_hbm, w_kv_hbm, ctx_ref, w_query_ref, w_kv_ref, proj_ref, sems
):
    loads = load_all((w_query_hbm, w_kv_hbm), (w_query_ref, w_kv_ref), sems)
    col_count, packet_rows, channels = atoms_ref.shape
    atom_count = packet_rows - PAD_ROWS
    row_atoms = col_count * atom_count
    blocks = row_atoms // QBLOCK - 2 * EDGE_BLOCKS
    step_blocks = max(n for n in range(2, 21, 2) if blocks % n == 0)
    edge = EDGE_BLOCKS * QBLOCK
    for c in range(col_count):
        proj = mul(atoms_ref[c, :atom_count, :], w_qkv_ref[...])
        proj_ref[c * atom_count : (c + 1) * atom_count, :] = proj.astype(BF16)
    ctx_ref[:edge, :] = jnp.zeros((edge, channels), BF16)
    ctx_ref[row_atoms - edge :, :] = jnp.zeros((edge, channels), BF16)

    def step(i, carry):
        first = i * (step_blocks * QBLOCK) + edge

        def query_of(b):
            start = pl.multiple_of(first + b * QBLOCK, QBLOCK)
            return proj_ref[pl.ds(start, QBLOCK), :channels]

        def union_of(b, part):
            start = pl.multiple_of(first + b * QBLOCK - HALO, PAD_ROWS)
            return proj_ref[
                pl.ds(start, KWIN + QBLOCK), part * channels : (part + 1) * channels
            ]

        for b, context in enumerate(attend(query_of, union_of, step_blocks)):
            ctx_ref[pl.ds(pl.multiple_of(first + b * QBLOCK, QBLOCK), QBLOCK), :] = context
        return carry

    lax.fori_loop(0, blocks // step_blocks, step, 0)
    wait_all(loads)


def bias_kernel(place_ref, pair_ref, w_ref, after_ref, *refs, segments, loads):
    del after_ref
    parts = len(segments)
    sources, outs, targets = refs[:loads], refs[loads : loads + parts], refs[loads + parts :][:loads]
    refs = refs[2 * loads + parts :]
    cells_refs, sems, load_sems = refs[:parts], refs[parts : 2 * parts], refs[2 * parts]
    _, rows, share, width = cells_refs[0].shape
    keys = rows * share
    heads = w_ref.shape[0]

    def load(s, i):
        place, offset, _, chunk = segments[s]
        start = i * chunk
        return pltpu.make_async_copy(
            pair_ref.at[pl.ds(place_ref[place] + offset + start, chunk)],
            cells_refs[s].at[pl.ds(start, chunk)],
            sems[s].at[i],
        )

    def load_segment(s):
        for i in range(segments[s][2] // segments[s][3]):
            load(s, i).start()

    load_segment(0)
    extra = load_all(sources, targets, load_sems)
    weights = w_ref[...].astype(BF16)
    weight_sum = jnp.sum(weights.astype(F32), axis=1, keepdims=True)
    mean_of = jnp.full((heads, width), 1.0 / width, BF16)
    left = jnp.concatenate([weights, mean_of], axis=0)

    def run(s):
        chunk = segments[s][3]

        def step(i, carry):
            load(s, i).wait()
            if s + 1 < parts:

                @pl.when(i == 0)
                def _():
                    load_segment(s + 1)

            start = pl.multiple_of(i * chunk, chunk)
            for q in range(chunk):
                cells = cells_refs[s][start + q].reshape(keys, width).T
                values = cells.astype(F32)
                found = mul(left, cells)
                dots, center = found[:heads], found[heads:]
                spread = jnp.sum(values * values, axis=0, keepdims=True) * (1.0 / width)
                spread = spread - center * center
                bias = (dots - center * weight_sum) * lax.rsqrt(spread + EPS)
                outs[s][:, start + q, :] = bias.astype(BF16).astype(F32)
            return carry

        lax.fori_loop(0, segments[s][2] // chunk, step, 0)

    for s in range(parts):
        run(s)
    wait_all(extra)


def pool_kernel(
    place_ref,
    atoms_ref,
    ctx_ref,
    first_ref,
    second_ref,
    w_qkv_ref,
    w_out_ref,
    w_up_ref,
    w_gate_hbm,
    mine_ref,
    half_ref,
    normed_out_ref,
    act_out_ref,
    my_ref,
    w_gate_ref,
    act_ref,
    atom_out_ref,
    sem,
    *,
    all_atoms,
):
    load = pltpu.make_async_copy(w_gate_hbm, w_gate_ref, sem)
    load.start()
    col_count, packet_rows, channels = atoms_ref.shape
    atom_count = packet_rows - PAD_ROWS
    row_atoms = col_count * atom_count
    half, width = half_ref.shape
    slices, share = mine_ref.shape[:2]
    edge = EDGE_BLOCKS * QBLOCK
    near = edge + HALO
    begin = atoms_ref[0, :near, :]
    end = atoms_ref[col_count - 1, atom_count - near : atom_count, :]
    even = place_ref[7] == 0
    before = jnp.where(even, second_ref[...], first_ref[...])
    after = jnp.where(even, first_ref[...], second_ref[...])
    contexts = []
    for wide, base in (
        (jnp.concatenate([before, begin], axis=0), -HALO),
        (jnp.concatenate([end, after], axis=0), row_atoms - near),
    ):
        proj = mul(wide, w_qkv_ref[...]).astype(BF16)

        def query_of(b):
            return proj[HALO + b * QBLOCK : HALO + (b + 1) * QBLOCK, :channels]

        def union_of(b, part):
            return proj[
                b * QBLOCK : b * QBLOCK + KWIN + QBLOCK, part * channels : (part + 1) * channels
            ]

        def valid_of(b, shape):
            position = place_ref[1] + (base + b * QBLOCK)
            position = position + lax.broadcasted_iota(jnp.int32, shape, 0)
            return (position >= 0) & (position < all_atoms)

        contexts.append(jnp.concatenate(attend(query_of, union_of, EDGE_BLOCKS, valid_of), axis=0))
    rows = half + slices * share
    row = lax.broadcasted_iota(jnp.int32, (rows, LANES), 0)
    token = row + jnp.where(row < half, place_ref[4], place_ref[11] - half)
    token = token.astype(F32)
    counts = jnp.zeros((rows, LANES), F32)
    totals = jnp.zeros((rows, width), F32)
    for c in [*range(1, col_count - 1), 0, col_count - 1]:
        start = c * atom_count
        ctx = ctx_ref[start : start + atom_count, :]
        if c == 0:
            ctx = jnp.concatenate([contexts[0], ctx[edge:]], axis=0)
        if c == col_count - 1:
            ctx = jnp.concatenate([ctx[: atom_count - edge], contexts[1]], axis=0)
        atom_out = atoms_ref[c, :atom_count, :].astype(F32) + mul(ctx, w_out_ref[...])
        atom_out = atom_out.astype(BF16)
        atom_out_ref[c] = atom_out
        up = jnp.maximum(mul(atom_out, w_up_ref[...]), 0.0).astype(BF16)
        names = atoms_ref[c, atom_count:, :].astype(F32)
        hots = []
        for k in range(atom_count // LANES):
            hot = jnp.where(names[k : k + 1, :] == token, 1.0, 0.0)
            counts = counts + hot
            hots.append(hot.astype(BF16))
        totals = totals + mul(jnp.concatenate(hots, axis=1), up)
    token_act = totals / jnp.sum(counts, axis=-1, keepdims=True)
    center = jnp.sum(token_act, axis=-1, keepdims=True) * (1.0 / width)
    spread = jnp.sum(token_act * token_act, axis=-1, keepdims=True) * (1.0 / width)
    spread = spread - center * center
    normed = ((token_act - center) / jnp.sqrt(spread + EPS)).astype(BF16)
    side = place_ref[12]
    for k in range(slices):
        part = normed[half + k * share : half + (k + 1) * share]
        other = normed[half + (1 - k) * share : half + (2 - k) * share]
        mine_ref[k] = jnp.where(side == 0, part, other)
    half_ref[...] = normed[:half]
    act_ref[...] = token_act[:half]
    out_share = act_out_ref.shape[0]
    start = pl.multiple_of(place_ref[9] * out_share, out_share)
    normed_out_ref[...] = half_ref[pl.ds(start, out_share), :]
    act_out_ref[...] = act_ref[pl.ds(start, out_share), :]
    col = place_ref[10]
    my_ref[:atom_count, :] = atom_out_ref[col]
    my_ref[atom_count:, :] = atoms_ref[col, atom_count:, :]
    load.wait()


def relay_kernel(after_ref, *refs):
    del after_ref
    count = len(refs) // 2
    for source, target in zip(refs[:count], refs[count:]):
        target[...] = source[...]


def query_kernel(
    half_ref, normed_ref, mine_ref, near_ref, w_query_ref, w_gate_ref, w_kv_ref, *out_refs
):
    query_ref, gate_ref, near_kv_ref = out_refs
    query_ref[...] = mul(half_ref[...], w_query_ref[...]).astype(BF16)
    gate_ref[...] = jax.nn.sigmoid(mul(normed_ref[...], w_gate_ref[...]))
    project((mine_ref, near_ref), w_kv_ref, near_kv_ref)


def project(parts, w_kv_ref, out_ref):
    slices, share, width = parts[0].shape
    rows = [part[...].reshape(slices * share, width) for part in parts]
    found = mul(jnp.concatenate(rows, axis=0), w_kv_ref[...]).astype(BF16)
    out_ref[...] = found.reshape(len(parts), slices, share, found.shape[1])


def token_kernel(
    place_ref, query_ref, w_kv_ref, early_ref, late_ref, swapped_ref, *refs, row_count, groups
):
    near_kv_ref, parts, refs = refs[0], refs[1 : row_count - 1], refs[row_count - 1 :]
    w_out_hbm, w_down_hbm, *refs = refs
    out_refs, refs = refs[:groups], refs[groups:]
    w_out_ref, w_down_ref, keys_ref, far_kv_ref, packet_ref, sems = refs
    loads = load_all((w_out_hbm, w_down_hbm), (w_out_ref, w_down_ref), sems)
    project(parts, w_kv_ref, far_kv_ref)
    for k in range(row_count):
        found = near_kv_ref.at[k] if k < 2 else far_kv_ref.at[k - 2]
        for i in range(2):
            keys_ref[i, place_ref[8] ^ k] = found[i]
    heads, tok_rows, part_keys = swapped_ref.shape
    key_count = 2 * part_keys
    width = query_ref.shape[1]
    head_size = width // heads
    share = out_refs[0].shape[0]
    keyvals = keys_ref[...].reshape(key_count, 2 * width)
    stats = jnp.zeros((tok_rows, LANES), F32)
    lane = lane_iota((tok_rows, LANES))
    tiles = [jnp.zeros((tok_rows, LANES), F32)] * (width // LANES)
    tile_lane = lane_iota((tok_rows, LANES))
    windows = []
    scores = []
    for h in range(heads):
        low = h * head_size // LANES * LANES
        high = min(width, -(-(h + 1) * head_size // LANES) * LANES)
        windows.append((low, high))
        chan = lane_iota((tok_rows, high - low)) + low
        inside = (chan >= h * head_size) & (chan < (h + 1) * head_size)
        query = query_ref[:, low:high]
        query = jnp.where(inside, query, jnp.zeros_like(query))
        scores.append(mul(query, keyvals[:, low:high], NT))
    for h, (low, high) in enumerate(windows):
        score = scores[h] * (1.0 / head_size**0.5)
        kept = jnp.concatenate([early_ref[h], late_ref[h]], axis=0)
        score = score + jnp.concatenate([kept, swapped_ref[h].astype(F32)], axis=1)
        top = jnp.max(score, axis=-1, keepdims=True)
        top_high = top.astype(BF16).astype(F32)
        top_low = (top - top_high).astype(BF16).astype(F32)
        expo = jnp.exp(score - (top_high + top_low))
        denom = jnp.sum(expo, axis=-1, keepdims=True)
        denom_high = denom.astype(BF16).astype(F32)
        stats = jnp.where(lane == h, top_high, stats)
        stats = jnp.where(lane == heads + h, top_low, stats)
        stats = jnp.where(lane == 2 * heads + h, denom_high, stats)
        stats = jnp.where(lane == 3 * heads + h, denom - denom_high, stats)
        mixed = mul(expo.astype(BF16), keyvals[:, width + low : width + high])
        for tile in range(low // LANES, high // LANES):
            chan = tile_lane + tile * LANES
            inside = (chan >= h * head_size) & (chan < (h + 1) * head_size)
            part = mixed[:, tile * LANES - low : (tile + 1) * LANES - low]
            tiles[tile] = jnp.where(inside, part, tiles[tile])
    for tile, values in enumerate(tiles):
        lanes = slice(tile * LANES, (tile + 1) * LANES)
        packet_ref[:, lanes] = values.astype(BF16)
    packet_ref[:, width:] = stats.astype(BF16)
    for k, out_ref in zip(far_first(groups), out_refs):
        start = pl.multiple_of((place_ref[9] ^ k) * share, share)
        out_ref[...] = packet_ref[pl.ds(start, share), :]
    wait_all(loads)


def merge_kernel(*refs, heads, groups):
    part_refs = refs[:groups]
    gate_ref, act_ref, w_out_ref, w_down_ref, out_ref = refs[groups:]
    share = part_refs[0].shape[0]
    col_count = out_ref.shape[0]
    width = w_out_ref.shape[0]
    head_size = width // heads
    chan_share = width // col_count
    stats = jnp.stack([part[:, width:] for part in part_refs]).astype(F32)
    top = stats + pltpu.roll(stats, LANES - heads, 2)
    denom = pltpu.roll(stats, LANES - 2 * heads, 2) + pltpu.roll(stats, LANES - 3 * heads, 2)
    is_head = lane_iota(stats.shape) < heads
    highest = jnp.max(top, axis=0, keepdims=True)
    scale = jnp.where(is_head, jnp.exp(jnp.where(is_head, top - highest, 0.0)), 0.0)
    total = jnp.sum(scale * denom, axis=0, keepdims=True)
    factor = scale / jnp.where(is_head[:1], total, 1.0)
    factor = factor.reshape(groups * share, LANES)
    factor_high = factor.astype(BF16)
    factor_low = (factor - factor_high.astype(F32)).astype(BF16)
    chan_head = lane_iota((LANES, width)) // head_size
    spread = jnp.where(
        chan_head == lax.broadcasted_iota(jnp.int32, (LANES, width), 0), 1.0, 0.0
    ).astype(BF16)
    wide = mul(factor_high, spread) + mul(factor_low, spread)
    wide = wide.reshape(groups, share, width)
    context = sum(part[:, :width].astype(F32) * wide[k] for k, part in enumerate(part_refs))
    gated = (context * gate_ref[...]).astype(BF16)
    updated = act_ref[...] + mul(gated, w_out_ref[...])
    token_out = updated.astype(BF16)
    token_down = mul(token_out, w_down_ref[...]).astype(BF16)
    for c in range(col_count):
        out_ref[c, :, :LANES] = token_down
        out_ref[c, :, LANES : LANES + chan_share] = token_out[
            :, c * chan_share : (c + 1) * chan_share
        ]


def final_kernel(atoms_ref, last_ref, token_ref, atom_ref, *, chan_share):
    col_count, share, _ = last_ref.shape
    tok_rows = col_count * share
    atom_count = atom_ref.shape[0]
    order = sorted(range(col_count), key=lambda c: (c % 2, c // 2))
    last = jnp.concatenate([last_ref[c] for c in order], axis=0)
    token_ref[...] = last[:, LANES : LANES + chan_share].astype(F32).T.astype(BF16)
    names = atoms_ref[atom_count:, :].astype(F32)
    token = lane_iota((LANES, tok_rows)).astype(F32)
    for k in range(atom_count // LANES):
        name = jnp.broadcast_to(names[k : k + 1, :], (LANES, LANES)).T
        name = jnp.concatenate([name] * (tok_rows // LANES), axis=1)
        hot = jnp.where(name == token, 1.0, 0.0).astype(BF16)
        rows = slice(k * LANES, (k + 1) * LANES)
        moved = atoms_ref[rows, :].astype(F32) + mul(hot, last[:, :LANES])
        atom_ref[rows, :] = moved.astype(BF16)


def body(
    atom_feat,
    atom_token,
    w_atom_qkv,
    w_atom_out,
    w_atom_up,
    pair_repr,
    w_bias,
    w_query,
    w_kv,
    w_gate,
    w_out,
    w_down,
):
    row_count = lax.axis_size("row")
    col_count = lax.axis_size("col")
    row_index = lax.axis_index("row")
    col_index = lax.axis_index("col")
    atom_count, channels = atom_feat.shape
    tok_rows, _, share, pair_width = pair_repr.shape
    key_count = row_count * share
    heads = w_bias.shape[1]
    width = w_query.shape[0]
    chan_share = width // col_count
    all_atoms = atom_count * row_count * col_count
    half = tok_rows // 2
    col_groups = col_count // 2
    side, group = col_index & 1, col_index >> 1
    out_share = half // col_groups
    shares = [
        col_index * share,
        (col_index ^ 1) * share,
        side * half,
        (1 - side) * half,
        side * half + group * out_share,
        row_index & 1,
        row_index,
        group,
        col_index,
        group * (2 * share),
        side,
    ]
    place = jnp.stack([col_index, row_index * tok_rows] + shares).astype(jnp.int32)
    edge_place = jnp.stack([col_index, row_index * (atom_count * col_count)] + shares)
    edge_place = edge_place.astype(jnp.int32)
    smem = pl.BlockSpec(memory_space=pltpu.SMEM)
    vmem = pl.BlockSpec(memory_space=pltpu.VMEM)
    hbm = pl.BlockSpec(memory_space=pltpu.HBM)
    unread = pl.BlockSpec(memory_space=pl.ANY)

    def swap(x, axis, step):
        return lax.ppermute(x, axis, [(i, i ^ step) for i in range(lax.axis_size(axis))])

    top = col_count // 2
    far = swap(atom_feat, "col", top)
    far_tokens = swap(atom_token, "col", top)
    token_shape = (atom_count // LANES, LANES)
    tokens, far_tokens = atom_token.reshape(token_shape), far_tokens.reshape(token_shape)

    def pair_bias(segments, after, weights):
        loads, parts = len(weights), len(segments)
        return call(
            functools.partial(bias_kernel, segments=segments, loads=loads),
            tuple(shape_of((heads, rows, key_count), F32) for _, _, rows, _ in segments)
            + tuple(shape_of(x.shape, x.dtype) for x in weights),
            14,
            in_specs=[smem, hbm, vmem, unread] + [hbm] * loads,
            out_specs=(vmem,) * (parts + loads),
            scratch_shapes=[
                pltpu.VMEM((rows,) + pair_repr.shape[1:], BF16) for _, _, rows, _ in segments
            ]
            + [pltpu.SemaphoreType.DMA((rows // chunk,)) for _, _, rows, chunk in segments]
            + [pltpu.SemaphoreType.DMA((loads,))],
        )(place, *in_hbm(pair_repr, w_bias.T), after, *in_hbm(*weights))

    early = half * 5 // 8
    late = half - early
    kept, own, own_tokens = pair_bias([(4, 0, early, early // 2)], place, (atom_feat, tokens))
    packet = call(
        pack_kernel,
        shape_of((2, atom_count + PAD_ROWS, channels), BF16),
        2,
        in_specs=[smem] + [vmem] * 4 + [unread],
        out_specs=vmem,
    )(place, own, own_tokens, far, far_tokens, kept)
    packets = [packet] + [swap(packet, "col", k) for k in range(1, top)]
    other, kept_late, *atom_weights = pair_bias(
        [(5, 0, half, half // 4), (4, early, late, late // 2)],
        packet,
        (w_atom_qkv, w_atom_out, w_atom_up),
    )
    sent, row_atoms, first, second = call(
        edge_kernel,
        (shape_of((heads, half, key_count), BF16), shape_of((col_count, atom_count + PAD_ROWS, channels), BF16))
        + (shape_of((HALO, channels), BF16),) * 2,
        4,
        in_specs=[smem] + [vmem] * (1 + top),
        out_specs=(vmem,) * 4,
    )(place, other, *packets)
    swapped = swap(sent, "col", 1)
    first = swap(first, "row", 1)
    pairs = [(i, ((i + 1) ^ 1) - 1) for i in range(1, row_count - 1)]
    second = lax.ppermute(second, "row", pairs)
    w_qkv, w_mix, w_up = atom_weights
    ctx, w_query, w_kv = call(
        inner_kernel,
        (
            shape_of((col_count * atom_count, channels), BF16),
            shape_of(w_query.shape, BF16),
            shape_of(w_kv.shape, BF16),
        ),
        12,
        in_specs=[vmem] * 2 + [hbm] * 2,
        out_specs=(vmem,) * 3,
        scratch_shapes=[
            pltpu.VMEM((col_count * atom_count, 3 * channels), BF16),
            pltpu.SemaphoreType.DMA((2,)),
        ],
    )(row_atoms, w_qkv, *in_hbm(w_query, w_kv))
    mine, half_normed, normed, act, my_atoms, w_gate = call(
        functools.partial(pool_kernel, all_atoms=all_atoms),
        (
            shape_of((2, share, width), BF16),
            shape_of((half, width), BF16),
            shape_of((out_share, width), BF16),
            shape_of((out_share, width), F32),
            shape_of((atom_count + PAD_ROWS, channels), BF16),
            shape_of(w_gate.shape, BF16),
        ),
        14,
        in_specs=[smem] + [vmem] * 7 + [hbm],
        out_specs=(vmem,) * 6,
        scratch_shapes=[
            pltpu.VMEM((half, width), F32),
            pltpu.VMEM((col_count, atom_count, channels), BF16),
            pltpu.SemaphoreType.DMA,
        ],
    )(edge_place, row_atoms, ctx, first, second, w_qkv, w_mix, w_up, *in_hbm(w_gate))
    far_parts = [swap(mine, "row", k) for k in range(2, row_count, 2)]
    near_part = swap(mine, "row", 1)
    queries, gate, near_kv = call(
        query_kernel,
        (
            shape_of((half, width), BF16),
            shape_of((out_share, width), F32),
            shape_of((2, 2, share, 2 * width), BF16),
        ),
        8,
        in_specs=[vmem] * 7,
        out_specs=(vmem,) * 3,
    )(half_normed, normed, mine, near_part, w_query, w_gate, w_kv)
    relayed = call(
        relay_kernel,
        (shape_of(mine.shape, BF16),) * len(far_parts),
        4,
        in_specs=[unread] + [vmem] * len(far_parts),
        out_specs=(vmem,) * len(far_parts),
    )(queries, *far_parts)
    key_parts = []
    for part in relayed:
        key_parts += [part, swap(part, "row", 1)]
    *parts, w_out, w_down = call(
        functools.partial(token_kernel, row_count=row_count, groups=col_groups),
        tuple(shape_of((out_share, width + LANES), BF16) for _ in range(col_groups))
        + (shape_of(w_out.shape, BF16), shape_of(w_down.shape, BF16)),
        14,
        in_specs=[smem] + [vmem] * (4 + row_count) + [hbm] * 2,
        out_specs=(vmem,) * (col_groups + 2),
        scratch_shapes=[
            pltpu.VMEM((2, row_count, share, 2 * width), BF16),
            pltpu.VMEM((row_count - 2, 2, share, 2 * width), BF16),
            pltpu.VMEM((half, width + LANES), BF16),
            pltpu.SemaphoreType.DMA((2,)),
        ],
    )(place, queries, w_kv, kept, kept_late, swapped, near_kv, *key_parts, *in_hbm(w_out, w_down))
    parts = parts[:1] + [
        lax.ppermute(part, "col", [(c, c ^ (2 * k)) for c in range(col_count)])
        for k, part in zip(far_first(col_groups), parts)
        if k > 0
    ]
    last = call(
        functools.partial(merge_kernel, heads=heads, groups=col_groups),
        shape_of((col_count, out_share, 2 * LANES), BF16),
        8,
        in_specs=[vmem] * (col_groups + 4),
        out_specs=vmem,
    )(*parts, gate, act, w_out, w_down)
    last = lax.all_to_all(last, "col", 0, 0)
    token_share, atom_final = call(
        functools.partial(final_kernel, chan_share=chan_share),
        (shape_of((chan_share, tok_rows), BF16), shape_of((atom_count, channels), BF16)),
        4,
        in_specs=[vmem] * 2,
        out_specs=(vmem,) * 2,
    )(my_atoms, last)
    return (token_share.T, atom_final)


def solution(mesh):
    return jax.shard_map(
        body,
        mesh=mesh,
        in_specs=(
            P(("row", "col"), None),
            P(("row", "col")),
            P(),
            P(),
            P(),
            P("row", None, "col", None),
            P(),
            P(),
            P(),
            P(),
            P(),
            P(),
        ),
        out_specs=(P("row", "col"), P(("row", "col"), None)),
        check_vma=False,
    )
```

```python
import functools

import jax
import jax.numpy as jnp
from jax import lax
from jax.experimental import pallas as pl
from jax.experimental.pallas import tpu as pltpu
from jax.sharding import PartitionSpec as P

AHEADS = 4
QBLOCK = 32
KWIN = 128
HALO = 48
LANES = 128
PAD_ROWS = 16
EDGE_BLOCKS = 2
EPS = 1e-05
LOG2_E = 1.4426950408889634
F32 = jnp.float32
BF16 = jnp.bfloat16
MIB = 1024 * 1024

NT = (((1,), (1,)), ((), ()))
NN = (((1,), (0,)), ((), ()))
TN = (((0,), (0,)), ((), ()))


def mul(a, b, dims=NN):
    return lax.dot_general(a, b, dims, preferred_element_type=F32)


def call(kernel, out_shape, vmem_mib, **kwargs):
    return pl.pallas_call(
        kernel,
        out_shape=out_shape,
        compiler_params=pltpu.CompilerParams(vmem_limit_bytes=vmem_mib * MIB),
        **kwargs,
    )


def shape_of(shape, dtype):
    return jax.ShapeDtypeStruct(shape, dtype)


def far_first(count):
    return [0] + list(range(count - 1, 0, -1))


def lane_iota(shape):
    return lax.broadcasted_iota(jnp.int32, shape, len(shape) - 1)


def in_hbm(*arrays):
    return tuple(pltpu.with_memory_space_constraint(x, pltpu.HBM) for x in arrays)


def load_all(sources, targets, sems):
    copies = [
        pltpu.make_async_copy(source, target, sems.at[i])
        for i, (source, target) in enumerate(zip(sources, targets))
    ]
    for copy in copies:
        copy.start()
    return copies


def wait_all(copies):
    for copy in copies:
        copy.wait()


def pack_kernel(place_ref, own_ref, token_ref, far_ref, far_token_ref, after_ref, out_ref):
    del after_ref
    atom_count = own_ref.shape[0]
    token_rows = token_ref.shape[0]
    blank = jnp.zeros((PAD_ROWS - token_rows, LANES), F32)
    for k, (feat, token) in enumerate(((own_ref, token_ref), (far_ref, far_token_ref))):
        out_ref[k, :atom_count, :] = feat[...]
        names = (token[...] - place_ref[1]).astype(F32)
        out_ref[k, atom_count:, :] = jnp.concatenate([names, blank], axis=0).astype(BF16)


def edge_kernel(place_ref, bias_ref, *refs):
    packets, (sent_ref, atoms_ref, first_ref, second_ref) = refs[:-4], refs[-4:]
    sent_ref[...] = bias_ref[...].astype(BF16)
    col_count, packet_rows, _ = atoms_ref.shape
    atom_count = packet_rows - PAD_ROWS
    for k, packet in enumerate(packets):
        for j in range(2):
            atoms_ref[place_ref[10] ^ (k + j * (col_count // 2))] = packet[j]
    tail = atoms_ref[col_count - 1, atom_count - HALO : atom_count, :]
    head = atoms_ref[0, :HALO, :]
    even = place_ref[7] == 0
    first_ref[...] = jnp.where(even, tail, head)
    second_ref[...] = jnp.where(even, head, tail)


def attend(query_of, union_of, blocks, valid_of=None):
    channels = query_of(0).shape[1]
    head_size = channels // AHEADS
    rows_of = AHEADS * QBLOCK
    head_of = lane_iota((QBLOCK, channels)) // head_size
    picks = [head_of == h for h in range(AHEADS)]
    scores = []
    for b in range(0, blocks, 2):
        stacked = []
        for query in (query_of(b), query_of(b + 1)):
            stacked += [jnp.where(pick, query, jnp.zeros_like(query)) for pick in picks]
        found = mul(union_of(b, 1), jnp.concatenate(stacked, axis=0), NT)
        scores += [found[:KWIN, :rows_of], found[QBLOCK:, rows_of:]]
    blank = jnp.zeros((KWIN, channels), BF16)
    row = lax.broadcasted_iota(jnp.int32, (PAD_ROWS, channels), 0)
    pair_rows = jnp.where(row < 2, 1.0, 0.0).astype(BF16)
    sum_rows = jnp.concatenate([blank[:PAD_ROWS], pair_rows], axis=1)
    contexts = []
    for b in range(blocks):
        score = scores[b]
        if valid_of is not None:
            score = jnp.where(valid_of(b, score.shape), score, -1e30)
        score = score - jnp.max(score, axis=0, keepdims=True)
        expo = jnp.exp2(score * (LOG2_E / head_size**0.5))
        denom = jnp.sum(expo, axis=0, keepdims=True)
        denom_high = denom.astype(BF16).astype(F32)
        sums = jnp.where(row == 0, denom_high, jnp.where(row == 1, denom - denom_high, 0.0))
        weights = jnp.concatenate([expo.astype(BF16), sums.astype(BF16)], axis=0)
        start = b % 2 * QBLOCK
        values = union_of(b - b % 2, 2)[start : start + KWIN]
        values = jnp.concatenate([values, blank], axis=1)
        mixed = mul(weights, jnp.concatenate([values, sum_rows], axis=0), TN)
        context = mixed[:QBLOCK]
        for h in range(1, AHEADS):
            pick = jnp.concatenate([picks[h]] * 2, axis=1)
            context = jnp.where(pick, mixed[h * QBLOCK : (h + 1) * QBLOCK], context)
        contexts.append((context[:, :channels] / context[:, channels:]).astype(BF16))
    return contexts


def inner_kernel(
    atoms_ref, w_qkv_ref, w_query_hbm, w_kv_hbm, ctx_ref, w_query_ref, w_kv_ref, proj_ref, sems
):
    loads = load_all((w_query_hbm, w_kv_hbm), (w_query_ref, w_kv_ref), sems)
    col_count, packet_rows, channels = atoms_ref.shape
    atom_count = packet_rows - PAD_ROWS
    row_atoms = col_count * atom_count
    blocks = row_atoms // QBLOCK - 2 * EDGE_BLOCKS
    step_blocks = max(n for n in range(2, 21, 2) if blocks % n == 0)
    edge = EDGE_BLOCKS * QBLOCK
    for c in range(col_count):
        proj = mul(atoms_ref[c, :atom_count, :], w_qkv_ref[...])
        proj_ref[c * atom_count : (c + 1) * atom_count, :] = proj.astype(BF16)
    ctx_ref[:edge, :] = jnp.zeros((edge, channels), BF16)
    ctx_ref[row_atoms - edge :, :] = jnp.zeros((edge, channels), BF16)

    def step(i, carry):
        first = i * (step_blocks * QBLOCK) + edge

        def query_of(b):
            start = pl.multiple_of(first + b * QBLOCK, QBLOCK)
            return proj_ref[pl.ds(start, QBLOCK), :channels]

        def union_of(b, part):
            start = pl.multiple_of(first + b * QBLOCK - HALO, PAD_ROWS)
            return proj_ref[
                pl.ds(start, KWIN + QBLOCK), part * channels : (part + 1) * channels
            ]

        for b, context in enumerate(attend(query_of, union_of, step_blocks)):
            ctx_ref[pl.ds(pl.multiple_of(first + b * QBLOCK, QBLOCK), QBLOCK), :] = context
        return carry

    lax.fori_loop(0, blocks // step_blocks, step, 0)
    wait_all(loads)


def bias_kernel(place_ref, pair_ref, w_ref, after_ref, *refs, segments, loads):
    del after_ref
    parts = len(segments)
    sources, outs, targets = refs[:loads], refs[loads : loads + parts], refs[loads + parts :][:loads]
    refs = refs[2 * loads + parts :]
    cells_refs, sems, load_sems = refs[:parts], refs[parts : 2 * parts], refs[2 * parts]
    _, rows, share, width = cells_refs[0].shape
    keys = rows * share
    heads = w_ref.shape[0]

    def load(s, i):
        place, offset, _, chunk = segments[s]
        start = i * chunk
        return pltpu.make_async_copy(
            pair_ref.at[pl.ds(place_ref[place] + offset + start, chunk)],
            cells_refs[s].at[pl.ds(start, chunk)],
            sems[s].at[i],
        )

    def load_segment(s):
        for i in range(segments[s][2] // segments[s][3]):
            load(s, i).start()

    load_segment(0)
    extra = load_all(sources, targets, load_sems)
    weights = w_ref[...].astype(BF16)
    weight_sum = jnp.sum(weights.astype(F32), axis=1, keepdims=True)
    mean_of = jnp.full((heads, width), 1.0 / width, BF16)
    left = jnp.concatenate([weights, mean_of], axis=0)

    def run(s):
        chunk = segments[s][3]

        def step(i, carry):
            load(s, i).wait()
            if s + 1 < parts:

                @pl.when(i == 0)
                def _():
                    load_segment(s + 1)

            start = pl.multiple_of(i * chunk, chunk)
            for q in range(chunk):
                cells = cells_refs[s][start + q].reshape(keys, width).T
                values = cells.astype(F32)
                found = mul(left, cells)
                dots, center = found[:heads], found[heads:]
                spread = jnp.sum(values * values, axis=0, keepdims=True) * (1.0 / width)
                spread = spread - center * center
                bias = (dots - center * weight_sum) * lax.rsqrt(spread + EPS)
                outs[s][:, start + q, :] = bias.astype(BF16).astype(F32)
            return carry

        lax.fori_loop(0, segments[s][2] // chunk, step, 0)

    for s in range(parts):
        run(s)
    wait_all(extra)


def pool_kernel(
    place_ref,
    atoms_ref,
    ctx_ref,
    first_ref,
    second_ref,
    w_qkv_ref,
    w_out_ref,
    w_up_ref,
    mine_ref,
    half_ref,
    normed_out_ref,
    act_out_ref,
    my_ref,
    act_ref,
    atom_out_ref,
    *,
    all_atoms,
):
    col_count, packet_rows, channels = atoms_ref.shape
    atom_count = packet_rows - PAD_ROWS
    row_atoms = col_count * atom_count
    half, width = half_ref.shape
    slices, share = mine_ref.shape[:2]
    edge = EDGE_BLOCKS * QBLOCK
    near = edge + HALO
    begin = atoms_ref[0, :near, :]
    end = atoms_ref[col_count - 1, atom_count - near : atom_count, :]
    even = place_ref[7] == 0
    before = jnp.where(even, second_ref[...], first_ref[...])
    after = jnp.where(even, first_ref[...], second_ref[...])
    contexts = []
    for wide, base in (
        (jnp.concatenate([before, begin], axis=0), -HALO),
        (jnp.concatenate([end, after], axis=0), row_atoms - near),
    ):
        proj = mul(wide, w_qkv_ref[...]).astype(BF16)

        def query_of(b):
            return proj[HALO + b * QBLOCK : HALO + (b + 1) * QBLOCK, :channels]

        def union_of(b, part):
            return proj[
                b * QBLOCK : b * QBLOCK + KWIN + QBLOCK, part * channels : (part + 1) * channels
            ]

        def valid_of(b, shape):
            position = place_ref[1] + (base + b * QBLOCK)
            position = position + lax.broadcasted_iota(jnp.int32, shape, 0)
            return (position >= 0) & (position < all_atoms)

        contexts.append(jnp.concatenate(attend(query_of, union_of, EDGE_BLOCKS, valid_of), axis=0))
    rows = half + slices * share
    row = lax.broadcasted_iota(jnp.int32, (rows, LANES), 0)
    token = row + jnp.where(row < half, place_ref[4], place_ref[11] - half)
    token = token.astype(F32)
    counts = jnp.zeros((rows, LANES), F32)
    totals = jnp.zeros((rows, width), F32)
    for c in [*range(1, col_count - 1), 0, col_count - 1]:
        start = c * atom_count
        ctx = ctx_ref[start : start + atom_count, :]
        if c == 0:
            ctx = jnp.concatenate([contexts[0], ctx[edge:]], axis=0)
        if c == col_count - 1:
            ctx = jnp.concatenate([ctx[: atom_count - edge], contexts[1]], axis=0)
        atom_out = atoms_ref[c, :atom_count, :].astype(F32) + mul(ctx, w_out_ref[...])
        atom_out = atom_out.astype(BF16)
        atom_out_ref[c] = atom_out
        up = jnp.maximum(mul(atom_out, w_up_ref[...]), 0.0).astype(BF16)
        names = atoms_ref[c, atom_count:, :].astype(F32)
        hots = []
        for k in range(atom_count // LANES):
            hot = jnp.where(names[k : k + 1, :] == token, 1.0, 0.0)
            counts = counts + hot
            hots.append(hot.astype(BF16))
        totals = totals + mul(jnp.concatenate(hots, axis=1), up)
    token_act = totals / jnp.sum(counts, axis=-1, keepdims=True)
    center = jnp.sum(token_act, axis=-1, keepdims=True) * (1.0 / width)
    spread = jnp.sum(token_act * token_act, axis=-1, keepdims=True) * (1.0 / width)
    spread = spread - center * center
    normed = ((token_act - center) / jnp.sqrt(spread + EPS)).astype(BF16)
    side = place_ref[12]
    for k in range(slices):
        part = normed[half + k * share : half + (k + 1) * share]
        other = normed[half + (1 - k) * share : half + (2 - k) * share]
        mine_ref[k] = jnp.where(side == 0, part, other)
    half_ref[...] = normed[:half]
    act_ref[...] = token_act[:half]
    out_share = act_out_ref.shape[0]
    start = pl.multiple_of(place_ref[9] * out_share, out_share)
    normed_out_ref[...] = half_ref[pl.ds(start, out_share), :]
    act_out_ref[...] = act_ref[pl.ds(start, out_share), :]
    col = place_ref[10]
    my_ref[:atom_count, :] = atom_out_ref[col]
    my_ref[atom_count:, :] = atoms_ref[col, atom_count:, :]


def relay_kernel(after_ref, *refs):
    del after_ref
    count = len(refs) // 2
    for source, target in zip(refs[:count], refs[count:]):
        target[...] = source[...]


def query_kernel(
    half_ref, normed_ref, mine_ref, w_query_ref, w_kv_ref, w_gate_hbm, *refs
):
    query_ref, gate_ref, own_kv_ref, w_gate_ref, sem = refs
    load = pltpu.make_async_copy(w_gate_hbm, w_gate_ref, sem)
    load.start()
    query_ref[...] = mul(half_ref[...], w_query_ref[...]).astype(BF16)
    project((mine_ref,), w_kv_ref, own_kv_ref)
    load.wait()
    gate_ref[...] = jax.nn.sigmoid(mul(normed_ref[...], w_gate_ref[...]))


def project(parts, w_kv_ref, out_ref):
    slices, share, width = parts[0].shape
    rows = [part[...].reshape(slices * share, width) for part in parts]
    found = mul(jnp.concatenate(rows, axis=0), w_kv_ref[...]).astype(BF16)
    out_ref[...] = found.reshape(len(parts), slices, share, found.shape[1])


def token_kernel(
    place_ref, query_ref, w_kv_ref, early_ref, late_ref, swapped_ref, *refs, row_count, groups
):
    own_kv_ref, parts, refs = refs[0], refs[1:row_count], refs[row_count:]
    w_out_hbm, w_down_hbm, *refs = refs
    out_refs, refs = refs[:groups], refs[groups:]
    w_out_ref, w_down_ref, keys_ref, other_kv_ref, packet_ref, sems = refs
    loads = load_all((w_out_hbm, w_down_hbm), (w_out_ref, w_down_ref), sems)
    project(parts, w_kv_ref, other_kv_ref)
    for k in range(row_count):
        found = other_kv_ref.at[k - 1] if k else own_kv_ref.at[k]
        for i in range(2):
            keys_ref[i, place_ref[8] ^ k] = found[i]
    heads, tok_rows, part_keys = swapped_ref.shape
    key_count = 2 * part_keys
    width = query_ref.shape[1]
    head_size = width // heads
    share = out_refs[0].shape[0]
    keyvals = keys_ref[...].reshape(key_count, 2 * width)
    stats = jnp.zeros((tok_rows, LANES), F32)
    lane = lane_iota((tok_rows, LANES))
    tiles = [jnp.zeros((tok_rows, LANES), F32)] * (width // LANES)
    tile_lane = lane_iota((tok_rows, LANES))
    windows = []
    scores = []
    for h in range(heads):
        low = h * head_size // LANES * LANES
        high = min(width, -(-(h + 1) * head_size // LANES) * LANES)
        windows.append((low, high))
        chan = lane_iota((tok_rows, high - low)) + low
        inside = (chan >= h * head_size) & (chan < (h + 1) * head_size)
        query = query_ref[:, low:high]
        query = jnp.where(inside, query, jnp.zeros_like(query))
        scores.append(mul(query, keyvals[:, low:high], NT))
    for h, (low, high) in enumerate(windows):
        score = scores[h] * (1.0 / head_size**0.5)
        kept = jnp.concatenate([early_ref[h], late_ref[h]], axis=0)
        score = score + jnp.concatenate([kept, swapped_ref[h].astype(F32)], axis=1)
        top = jnp.max(score, axis=-1, keepdims=True)
        top_high = top.astype(BF16).astype(F32)
        top_low = (top - top_high).astype(BF16).astype(F32)
        expo = jnp.exp(score - (top_high + top_low))
        denom = jnp.sum(expo, axis=-1, keepdims=True)
        denom_high = denom.astype(BF16).astype(F32)
        stats = jnp.where(lane == h, top_high, stats)
        stats = jnp.where(lane == heads + h, top_low, stats)
        stats = jnp.where(lane == 2 * heads + h, denom_high, stats)
        stats = jnp.where(lane == 3 * heads + h, denom - denom_high, stats)
        mixed = mul(expo.astype(BF16), keyvals[:, width + low : width + high])
        for tile in range(low // LANES, high // LANES):
            chan = tile_lane + tile * LANES
            inside = (chan >= h * head_size) & (chan < (h + 1) * head_size)
            part = mixed[:, tile * LANES - low : (tile + 1) * LANES - low]
            tiles[tile] = jnp.where(inside, part, tiles[tile])
    for tile, values in enumerate(tiles):
        lanes = slice(tile * LANES, (tile + 1) * LANES)
        packet_ref[:, lanes] = values.astype(BF16)
    packet_ref[:, width:] = stats.astype(BF16)
    for k, out_ref in zip(far_first(groups), out_refs):
        start = pl.multiple_of((place_ref[9] ^ k) * share, share)
        out_ref[...] = packet_ref[pl.ds(start, share), :]
    wait_all(loads)


def merge_kernel(*refs, heads, groups):
    part_refs = refs[:groups]
    gate_ref, act_ref, w_out_ref, w_down_ref, out_ref = refs[groups:]
    share = part_refs[0].shape[0]
    col_count = out_ref.shape[0]
    width = w_out_ref.shape[0]
    head_size = width // heads
    chan_share = width // col_count
    stats = jnp.stack([part[:, width:] for part in part_refs]).astype(F32)
    top = stats + pltpu.roll(stats, LANES - heads, 2)
    denom = pltpu.roll(stats, LANES - 2 * heads, 2) + pltpu.roll(stats, LANES - 3 * heads, 2)
    is_head = lane_iota(stats.shape) < heads
    highest = jnp.max(top, axis=0, keepdims=True)
    scale = jnp.where(is_head, jnp.exp(jnp.where(is_head, top - highest, 0.0)), 0.0)
    total = jnp.sum(scale * denom, axis=0, keepdims=True)
    factor = scale / jnp.where(is_head[:1], total, 1.0)
    factor = factor.reshape(groups * share, LANES)
    factor_high = factor.astype(BF16)
    factor_low = (factor - factor_high.astype(F32)).astype(BF16)
    chan_head = lane_iota((LANES, width)) // head_size
    spread = jnp.where(
        chan_head == lax.broadcasted_iota(jnp.int32, (LANES, width), 0), 1.0, 0.0
    ).astype(BF16)
    wide = mul(factor_high, spread) + mul(factor_low, spread)
    wide = wide.reshape(groups, share, width)
    context = sum(part[:, :width].astype(F32) * wide[k] for k, part in enumerate(part_refs))
    gated = (context * gate_ref[...]).astype(BF16)
    updated = act_ref[...] + mul(gated, w_out_ref[...])
    token_out = updated.astype(BF16)
    token_down = mul(token_out, w_down_ref[...]).astype(BF16)
    for c in range(col_count):
        out_ref[c, :, :LANES] = token_down
        out_ref[c, :, LANES : LANES + chan_share] = token_out[
            :, c * chan_share : (c + 1) * chan_share
        ]


def final_kernel(atoms_ref, last_ref, token_ref, atom_ref, *, chan_share):
    col_count, share, _ = last_ref.shape
    tok_rows = col_count * share
    atom_count = atom_ref.shape[0]
    order = sorted(range(col_count), key=lambda c: (c % 2, c // 2))
    last = jnp.concatenate([last_ref[c] for c in order], axis=0)
    token_ref[...] = last[:, LANES : LANES + chan_share].astype(F32).T.astype(BF16)
    names = atoms_ref[atom_count:, :].astype(F32)
    token = lane_iota((LANES, tok_rows)).astype(F32)
    for k in range(atom_count // LANES):
        name = jnp.broadcast_to(names[k : k + 1, :], (LANES, LANES)).T
        name = jnp.concatenate([name] * (tok_rows // LANES), axis=1)
        hot = jnp.where(name == token, 1.0, 0.0).astype(BF16)
        rows = slice(k * LANES, (k + 1) * LANES)
        moved = atoms_ref[rows, :].astype(F32) + mul(hot, last[:, :LANES])
        atom_ref[rows, :] = moved.astype(BF16)


def body(
    atom_feat,
    atom_token,
    w_atom_qkv,
    w_atom_out,
    w_atom_up,
    pair_repr,
    w_bias,
    w_query,
    w_kv,
    w_gate,
    w_out,
    w_down,
):
    row_count = lax.axis_size("row")
    col_count = lax.axis_size("col")
    row_index = lax.axis_index("row")
    col_index = lax.axis_index("col")
    atom_count, channels = atom_feat.shape
    tok_rows, _, share, pair_width = pair_repr.shape
    key_count = row_count * share
    heads = w_bias.shape[1]
    width = w_query.shape[0]
    chan_share = width // col_count
    all_atoms = atom_count * row_count * col_count
    half = tok_rows // 2
    col_groups = col_count // 2
    side, group = col_index & 1, col_index >> 1
    out_share = half // col_groups
    shares = [
        col_index * share,
        (col_index ^ 1) * share,
        side * half,
        (1 - side) * half,
        side * half + group * out_share,
        row_index & 1,
        row_index,
        group,
        col_index,
        group * (2 * share),
        side,
    ]
    place = jnp.stack([col_index, row_index * tok_rows] + shares).astype(jnp.int32)
    edge_place = jnp.stack([col_index, row_index * (atom_count * col_count)] + shares)
    edge_place = edge_place.astype(jnp.int32)
    smem = pl.BlockSpec(memory_space=pltpu.SMEM)
    vmem = pl.BlockSpec(memory_space=pltpu.VMEM)
    hbm = pl.BlockSpec(memory_space=pltpu.HBM)
    unread = pl.BlockSpec(memory_space=pl.ANY)

    def swap(x, axis, step):
        return lax.ppermute(x, axis, [(i, i ^ step) for i in range(lax.axis_size(axis))])

    top = col_count // 2
    far = swap(atom_feat, "col", top)
    far_tokens = swap(atom_token, "col", top)
    token_shape = (atom_count // LANES, LANES)
    tokens, far_tokens = atom_token.reshape(token_shape), far_tokens.reshape(token_shape)

    def pair_bias(segments, after, weights):
        loads, parts = len(weights), len(segments)
        return call(
            functools.partial(bias_kernel, segments=segments, loads=loads),
            tuple(shape_of((heads, rows, key_count), F32) for _, _, rows, _ in segments)
            + tuple(shape_of(x.shape, x.dtype) for x in weights),
            14,
            in_specs=[smem, hbm, vmem, unread] + [hbm] * loads,
            out_specs=(vmem,) * (parts + loads),
            scratch_shapes=[
                pltpu.VMEM((rows,) + pair_repr.shape[1:], BF16) for _, _, rows, _ in segments
            ]
            + [pltpu.SemaphoreType.DMA((rows // chunk,)) for _, _, rows, chunk in segments]
            + [pltpu.SemaphoreType.DMA((loads,))],
        )(place, *in_hbm(pair_repr, w_bias.T), after, *in_hbm(*weights))

    early = half * 5 // 8
    late = half - early
    kept, own, own_tokens = pair_bias([(4, 0, early, early // 2)], place, (atom_feat, tokens))
    packet = call(
        pack_kernel,
        shape_of((2, atom_count + PAD_ROWS, channels), BF16),
        2,
        in_specs=[smem] + [vmem] * 4 + [unread],
        out_specs=vmem,
    )(place, own, own_tokens, far, far_tokens, kept)
    packets = [packet] + [swap(packet, "col", k) for k in range(1, top)]
    other, kept_late, *atom_weights = pair_bias(
        [(5, 0, half, half // 4), (4, early, late, late // 2)],
        packet,
        (w_atom_qkv, w_atom_out, w_atom_up),
    )
    sent, row_atoms, first, second = call(
        edge_kernel,
        (shape_of((heads, half, key_count), BF16), shape_of((col_count, atom_count + PAD_ROWS, channels), BF16))
        + (shape_of((HALO, channels), BF16),) * 2,
        4,
        in_specs=[smem] + [vmem] * (1 + top),
        out_specs=(vmem,) * 4,
    )(place, other, *packets)
    swapped = swap(sent, "col", 1)
    first = swap(first, "row", 1)
    pairs = [(i, ((i + 1) ^ 1) - 1) for i in range(1, row_count - 1)]
    second = lax.ppermute(second, "row", pairs)
    w_qkv, w_mix, w_up = atom_weights
    ctx, w_query, w_kv = call(
        inner_kernel,
        (
            shape_of((col_count * atom_count, channels), BF16),
            shape_of(w_query.shape, BF16),
            shape_of(w_kv.shape, BF16),
        ),
        12,
        in_specs=[vmem] * 2 + [hbm] * 2,
        out_specs=(vmem,) * 3,
        scratch_shapes=[
            pltpu.VMEM((col_count * atom_count, 3 * channels), BF16),
            pltpu.SemaphoreType.DMA((2,)),
        ],
    )(row_atoms, w_qkv, *in_hbm(w_query, w_kv))
    mine, half_normed, normed, act, my_atoms = call(
        functools.partial(pool_kernel, all_atoms=all_atoms),
        (
            shape_of((2, share, width), BF16),
            shape_of((half, width), BF16),
            shape_of((out_share, width), BF16),
            shape_of((out_share, width), F32),
            shape_of((atom_count + PAD_ROWS, channels), BF16),
        ),
        14,
        in_specs=[smem] + [vmem] * 7,
        out_specs=(vmem,) * 5,
        scratch_shapes=[
            pltpu.VMEM((half, width), F32),
            pltpu.VMEM((col_count, atom_count, channels), BF16),
        ],
    )(edge_place, row_atoms, ctx, first, second, w_qkv, w_mix, w_up)
    far_parts = [swap(mine, "row", k) for k in range(2, row_count, 2)]
    near_part = swap(mine, "row", 1)
    queries, gate, own_kv = call(
        query_kernel,
        (
            shape_of((half, width), BF16),
            shape_of((out_share, width), F32),
            shape_of((1, 2, share, 2 * width), BF16),
        ),
        8,
        in_specs=[vmem] * 5 + [hbm],
        out_specs=(vmem,) * 3,
        scratch_shapes=[pltpu.VMEM(w_gate.shape, BF16), pltpu.SemaphoreType.DMA],
    )(half_normed, normed, mine, w_query, w_kv, *in_hbm(w_gate))
    relayed = call(
        relay_kernel,
        (shape_of(mine.shape, BF16),) * len(far_parts),
        4,
        in_specs=[unread] + [vmem] * len(far_parts),
        out_specs=(vmem,) * len(far_parts),
    )(queries, *far_parts)
    key_parts = [near_part]
    for part in relayed:
        key_parts += [part, swap(part, "row", 1)]
    *parts, w_out, w_down = call(
        functools.partial(token_kernel, row_count=row_count, groups=col_groups),
        tuple(shape_of((out_share, width + LANES), BF16) for _ in range(col_groups))
        + (shape_of(w_out.shape, BF16), shape_of(w_down.shape, BF16)),
        14,
        in_specs=[smem] + [vmem] * (5 + row_count) + [hbm] * 2,
        out_specs=(vmem,) * (col_groups + 2),
        scratch_shapes=[
            pltpu.VMEM((2, row_count, share, 2 * width), BF16),
            pltpu.VMEM((row_count - 1, 2, share, 2 * width), BF16),
            pltpu.VMEM((half, width + LANES), BF16),
            pltpu.SemaphoreType.DMA((2,)),
        ],
    )(place, queries, w_kv, kept, kept_late, swapped, own_kv, *key_parts, *in_hbm(w_out, w_down))
    parts = parts[:1] + [
        lax.ppermute(part, "col", [(c, c ^ (2 * k)) for c in range(col_count)])
        for k, part in zip(far_first(col_groups), parts)
        if k > 0
    ]
    last = call(
        functools.partial(merge_kernel, heads=heads, groups=col_groups),
        shape_of((col_count, out_share, 2 * LANES), BF16),
        8,
        in_specs=[vmem] * (col_groups + 4),
        out_specs=vmem,
    )(*parts, gate, act, w_out, w_down)
    last = lax.all_to_all(last, "col", 0, 0)
    token_share, atom_final = call(
        functools.partial(final_kernel, chan_share=chan_share),
        (shape_of((chan_share, tok_rows), BF16), shape_of((atom_count, channels), BF16)),
        4,
        in_specs=[vmem] * 2,
        out_specs=(vmem,) * 2,
    )(my_atoms, last)
    return (token_share.T, atom_final)


def solution(mesh):
    return jax.shard_map(
        body,
        mesh=mesh,
        in_specs=(
            P(("row", "col"), None),
            P(("row", "col")),
            P(),
            P(),
            P(),
            P("row", None, "col", None),
            P(),
            P(),
            P(),
            P(),
            P(),
            P(),
        ),
        out_specs=(P("row", "col"), P(("row", "col"), None)),
        check_vma=False,
    )
```

```python
import functools

import jax
import jax.numpy as jnp
from jax import lax
from jax.experimental import pallas as pl
from jax.experimental.pallas import tpu as pltpu
from jax.sharding import PartitionSpec as P

AHEADS = 4
QBLOCK = 32
KWIN = 128
HALO = 48
LANES = 128
PAD_ROWS = 16
EDGE_BLOCKS = 2
EPS = 1e-05
LOG2_E = 1.4426950408889634
F32 = jnp.float32
BF16 = jnp.bfloat16
MIB = 1024 * 1024

NT = (((1,), (1,)), ((), ()))
NN = (((1,), (0,)), ((), ()))
TN = (((0,), (0,)), ((), ()))


def mul(a, b, dims=NN):
    return lax.dot_general(a, b, dims, preferred_element_type=F32)


def call(kernel, out_shape, vmem_mib, **kwargs):
    return pl.pallas_call(
        kernel,
        out_shape=out_shape,
        compiler_params=pltpu.CompilerParams(vmem_limit_bytes=vmem_mib * MIB),
        **kwargs,
    )


def shape_of(shape, dtype):
    return jax.ShapeDtypeStruct(shape, dtype)


def far_first(count):
    return [0] + list(range(count - 1, 0, -1))


def lane_iota(shape):
    return lax.broadcasted_iota(jnp.int32, shape, len(shape) - 1)


def in_hbm(*arrays):
    return tuple(pltpu.with_memory_space_constraint(x, pltpu.HBM) for x in arrays)


def load_all(sources, targets, sems):
    copies = [
        pltpu.make_async_copy(source, target, sems.at[i])
        for i, (source, target) in enumerate(zip(sources, targets))
    ]
    for copy in copies:
        copy.start()
    return copies


def wait_all(copies):
    for copy in copies:
        copy.wait()


def own_kernel(place_ref, feat_ref, token_ref, out_ref, names_ref, sems):
    atom_count = feat_ref.shape[0]
    loads = [
        pltpu.make_async_copy(token_ref, names_ref, sems.at[0]),
        pltpu.make_async_copy(feat_ref, out_ref.at[pl.ds(0, atom_count)], sems.at[1]),
    ]
    for copy in loads:
        copy.start()
    wait_all(loads)
    names = (names_ref[...] - place_ref[1]).astype(F32)
    blank = jnp.zeros((PAD_ROWS - names.shape[0], LANES), F32)
    out_ref[atom_count:, :] = jnp.concatenate([names, blank], axis=0).astype(BF16)


def pack_kernel(own_ref, far_ref, after_ref, out_ref):
    del after_ref
    out_ref[0] = own_ref[...]
    out_ref[1] = far_ref[...]


def edge_kernel(place_ref, bias_ref, *refs):
    packets, (sent_ref, atoms_ref, first_ref, second_ref) = refs[:-4], refs[-4:]
    sent_ref[...] = bias_ref[...].astype(BF16)
    col_count, packet_rows, _ = atoms_ref.shape
    atom_count = packet_rows - PAD_ROWS
    for k, packet in enumerate(packets):
        for j in range(2):
            atoms_ref[place_ref[10] ^ (k + j * (col_count // 2))] = packet[j]
    tail = atoms_ref[col_count - 1, atom_count - HALO : atom_count, :]
    head = atoms_ref[0, :HALO, :]
    even = place_ref[7] == 0
    first_ref[...] = jnp.where(even, tail, head)
    second_ref[...] = jnp.where(even, head, tail)


def attend(query_of, union_of, blocks, valid_of=None):
    channels = query_of(0).shape[1]
    head_size = channels // AHEADS
    rows_of = AHEADS * QBLOCK
    head_of = lane_iota((QBLOCK, channels)) // head_size
    picks = [head_of == h for h in range(AHEADS)]
    scores = []
    for b in range(0, blocks, 2):
        stacked = []
        for query in (query_of(b), query_of(b + 1)):
            stacked += [jnp.where(pick, query, jnp.zeros_like(query)) for pick in picks]
        found = mul(union_of(b, 1), jnp.concatenate(stacked, axis=0), NT)
        scores += [found[:KWIN, :rows_of], found[QBLOCK:, rows_of:]]
    blank = jnp.zeros((KWIN, channels), BF16)
    row = lax.broadcasted_iota(jnp.int32, (PAD_ROWS, channels), 0)
    pair_rows = jnp.where(row < 2, 1.0, 0.0).astype(BF16)
    sum_rows = jnp.concatenate([blank[:PAD_ROWS], pair_rows], axis=1)
    contexts = []
    for b in range(blocks):
        score = scores[b]
        if valid_of is not None:
            score = jnp.where(valid_of(b, score.shape), score, -1e30)
        score = score - jnp.max(score, axis=0, keepdims=True)
        expo = jnp.exp2(score * (LOG2_E / head_size**0.5))
        denom = jnp.sum(expo, axis=0, keepdims=True)
        denom_high = denom.astype(BF16).astype(F32)
        sums = jnp.where(row == 0, denom_high, jnp.where(row == 1, denom - denom_high, 0.0))
        weights = jnp.concatenate([expo.astype(BF16), sums.astype(BF16)], axis=0)
        start = b % 2 * QBLOCK
        values = union_of(b - b % 2, 2)[start : start + KWIN]
        values = jnp.concatenate([values, blank], axis=1)
        mixed = mul(weights, jnp.concatenate([values, sum_rows], axis=0), TN)
        context = mixed[:QBLOCK]
        for h in range(1, AHEADS):
            pick = jnp.concatenate([picks[h]] * 2, axis=1)
            context = jnp.where(pick, mixed[h * QBLOCK : (h + 1) * QBLOCK], context)
        contexts.append((context[:, :channels] / context[:, channels:]).astype(BF16))
    return contexts


def inner_kernel(
    atoms_ref, w_qkv_ref, w_query_hbm, w_kv_hbm, ctx_ref, w_query_ref, w_kv_ref, proj_ref, sems
):
    loads = load_all((w_query_hbm, w_kv_hbm), (w_query_ref, w_kv_ref), sems)
    col_count, packet_rows, channels = atoms_ref.shape
    atom_count = packet_rows - PAD_ROWS
    row_atoms = col_count * atom_count
    blocks = row_atoms // QBLOCK - 2 * EDGE_BLOCKS
    step_blocks = max(n for n in range(2, 31, 2) if blocks % n == 0)
    edge = EDGE_BLOCKS * QBLOCK
    for c in range(col_count):
        proj = mul(atoms_ref[c, :atom_count, :], w_qkv_ref[...])
        proj_ref[c * atom_count : (c + 1) * atom_count, :] = proj.astype(BF16)
    ctx_ref[:edge, :] = jnp.zeros((edge, channels), BF16)
    ctx_ref[row_atoms - edge :, :] = jnp.zeros((edge, channels), BF16)

    def step(i, carry):
        first = i * (step_blocks * QBLOCK) + edge

        def query_of(b):
            start = pl.multiple_of(first + b * QBLOCK, QBLOCK)
            return proj_ref[pl.ds(start, QBLOCK), :channels]

        def union_of(b, part):
            start = pl.multiple_of(first + b * QBLOCK - HALO, PAD_ROWS)
            return proj_ref[
                pl.ds(start, KWIN + QBLOCK), part * channels : (part + 1) * channels
            ]

        for b, context in enumerate(attend(query_of, union_of, step_blocks)):
            ctx_ref[pl.ds(pl.multiple_of(first + b * QBLOCK, QBLOCK), QBLOCK), :] = context
        return carry

    lax.fori_loop(0, blocks // step_blocks, step, 0)
    wait_all(loads)


def bias_kernel(place_ref, pair_ref, w_ref, after_ref, *refs, segments, loads):
    del after_ref
    parts = len(segments)
    sources, outs, targets = refs[:loads], refs[loads : loads + parts], refs[loads + parts :][:loads]
    refs = refs[2 * loads + parts :]
    cells_refs, sems, load_sems = refs[:parts], refs[parts : 2 * parts], refs[2 * parts]
    _, rows, share, width = cells_refs[0].shape
    keys = rows * share
    heads = w_ref.shape[0]

    def load(s, i):
        place, offset, _, chunk = segments[s]
        start = i * chunk
        return pltpu.make_async_copy(
            pair_ref.at[pl.ds(place_ref[place] + offset + start, chunk)],
            cells_refs[s].at[pl.ds(start, chunk)],
            sems[s].at[i],
        )

    def load_segment(s):
        for i in range(segments[s][2] // segments[s][3]):
            load(s, i).start()

    load_segment(0)
    extra = load_all(sources, targets, load_sems)
    weights = w_ref[...].astype(BF16)
    weight_sum = jnp.sum(weights.astype(F32), axis=1, keepdims=True)
    mean_of = jnp.full((heads, width), 1.0 / width, BF16)
    left = jnp.concatenate([weights, mean_of], axis=0)

    def run(s):
        chunk = segments[s][3]

        def step(i, carry):
            load(s, i).wait()
            if s + 1 < parts:

                @pl.when(i == 0)
                def _():
                    load_segment(s + 1)

            start = pl.multiple_of(i * chunk, chunk)
            for q in range(chunk):
                cells = cells_refs[s][start + q].reshape(keys, width).T
                values = cells.astype(F32)
                found = mul(left, cells)
                dots, center = found[:heads], found[heads:]
                spread = jnp.sum(values * values, axis=0, keepdims=True) * (1.0 / width)
                spread = spread - center * center
                bias = (dots - center * weight_sum) * lax.rsqrt(spread + EPS)
                outs[s][:, start + q, :] = bias.astype(BF16).astype(F32)
            return carry

        lax.fori_loop(0, segments[s][2] // chunk, step, 0)

    for s in range(parts):
        run(s)
    wait_all(extra)


def pool_kernel(
    place_ref,
    atoms_ref,
    ctx_ref,
    first_ref,
    second_ref,
    w_qkv_ref,
    w_out_ref,
    w_up_ref,
    mine_ref,
    half_ref,
    normed_out_ref,
    act_out_ref,
    my_ref,
    act_ref,
    atom_out_ref,
    *,
    all_atoms,
):
    col_count, packet_rows, channels = atoms_ref.shape
    atom_count = packet_rows - PAD_ROWS
    row_atoms = col_count * atom_count
    half, width = half_ref.shape
    slices, share = mine_ref.shape[:2]
    edge = EDGE_BLOCKS * QBLOCK
    near = edge + HALO
    begin = atoms_ref[0, :near, :]
    end = atoms_ref[col_count - 1, atom_count - near : atom_count, :]
    even = place_ref[7] == 0
    before = jnp.where(even, second_ref[...], first_ref[...])
    after = jnp.where(even, first_ref[...], second_ref[...])
    contexts = []
    for wide, base in (
        (jnp.concatenate([before, begin], axis=0), -HALO),
        (jnp.concatenate([end, after], axis=0), row_atoms - near),
    ):
        proj = mul(wide, w_qkv_ref[...]).astype(BF16)

        def query_of(b):
            return proj[HALO + b * QBLOCK : HALO + (b + 1) * QBLOCK, :channels]

        def union_of(b, part):
            return proj[
                b * QBLOCK : b * QBLOCK + KWIN + QBLOCK, part * channels : (part + 1) * channels
            ]

        def valid_of(b, shape):
            position = place_ref[1] + (base + b * QBLOCK)
            position = position + lax.broadcasted_iota(jnp.int32, shape, 0)
            return (position >= 0) & (position < all_atoms)

        contexts.append(jnp.concatenate(attend(query_of, union_of, EDGE_BLOCKS, valid_of), axis=0))
    rows = half + slices * share
    row = lax.broadcasted_iota(jnp.int32, (rows, LANES), 0)
    token = row + jnp.where(row < half, place_ref[4], place_ref[11] - half)
    token = token.astype(F32)
    counts = jnp.zeros((rows, LANES), F32)
    totals = jnp.zeros((rows, width), F32)
    for c in [*range(1, col_count - 1), 0, col_count - 1]:
        start = c * atom_count
        ctx = ctx_ref[start : start + atom_count, :]
        if c == 0:
            ctx = jnp.concatenate([contexts[0], ctx[edge:]], axis=0)
        if c == col_count - 1:
            ctx = jnp.concatenate([ctx[: atom_count - edge], contexts[1]], axis=0)
        atom_out = atoms_ref[c, :atom_count, :].astype(F32) + mul(ctx, w_out_ref[...])
        atom_out = atom_out.astype(BF16)
        atom_out_ref[c] = atom_out
        up = jnp.maximum(mul(atom_out, w_up_ref[...]), 0.0).astype(BF16)
        names = atoms_ref[c, atom_count:, :].astype(F32)
        hots = []
        for k in range(atom_count // LANES):
            hot = jnp.where(names[k : k + 1, :] == token, 1.0, 0.0)
            counts = counts + hot
            hots.append(hot.astype(BF16))
        totals = totals + mul(jnp.concatenate(hots, axis=1), up)
    token_act = totals / jnp.sum(counts, axis=-1, keepdims=True)
    center = jnp.sum(token_act, axis=-1, keepdims=True) * (1.0 / width)
    spread = jnp.sum(token_act * token_act, axis=-1, keepdims=True) * (1.0 / width)
    spread = spread - center * center
    normed = ((token_act - center) / jnp.sqrt(spread + EPS)).astype(BF16)
    side = place_ref[12]
    for k in range(slices):
        part = normed[half + k * share : half + (k + 1) * share]
        other = normed[half + (1 - k) * share : half + (2 - k) * share]
        mine_ref[k] = jnp.where(side == 0, part, other)
    half_ref[...] = normed[:half]
    act_ref[...] = token_act[:half]
    out_share = act_out_ref.shape[0]
    start = pl.multiple_of(place_ref[9] * out_share, out_share)
    normed_out_ref[...] = half_ref[pl.ds(start, out_share), :]
    act_out_ref[...] = act_ref[pl.ds(start, out_share), :]
    col = place_ref[10]
    my_ref[:atom_count, :] = atom_out_ref[col]
    my_ref[atom_count:, :] = atoms_ref[col, atom_count:, :]


def relay_kernel(after_ref, *refs):
    del after_ref
    count = len(refs) // 2
    for source, target in zip(refs[:count], refs[count:]):
        target[...] = source[...]


def query_kernel(
    half_ref, normed_ref, mine_ref, w_query_ref, w_kv_ref, w_gate_hbm, *refs
):
    query_ref, gate_ref, own_kv_ref, w_gate_ref, sem = refs
    load = pltpu.make_async_copy(w_gate_hbm, w_gate_ref, sem)
    load.start()
    query_ref[...] = mul(half_ref[...], w_query_ref[...]).astype(BF16)
    project((mine_ref,), w_kv_ref, own_kv_ref)
    load.wait()
    gate_ref[...] = jax.nn.sigmoid(mul(normed_ref[...], w_gate_ref[...]))


def project(parts, w_kv_ref, out_ref):
    slices, share, width = parts[0].shape
    rows = [part[...].reshape(slices * share, width) for part in parts]
    found = mul(jnp.concatenate(rows, axis=0), w_kv_ref[...]).astype(BF16)
    out_ref[...] = found.reshape(len(parts), slices, share, found.shape[1])


def token_kernel(
    place_ref, query_ref, w_kv_ref, early_ref, late_ref, swapped_ref, *refs, row_count, groups
):
    own_kv_ref, parts, refs = refs[0], refs[1:row_count], refs[row_count:]
    w_out_hbm, w_down_hbm, *refs = refs
    out_refs, refs = refs[:groups], refs[groups:]
    w_out_ref, w_down_ref, keys_ref, other_kv_ref, packet_ref, sems = refs
    loads = load_all((w_out_hbm, w_down_hbm), (w_out_ref, w_down_ref), sems)
    project(parts, w_kv_ref, other_kv_ref)
    for k in range(row_count):
        found = other_kv_ref.at[k - 1] if k else own_kv_ref.at[k]
        for i in range(2):
            keys_ref[i, place_ref[8] ^ k] = found[i]
    heads, tok_rows, part_keys = swapped_ref.shape
    key_count = 2 * part_keys
    width = query_ref.shape[1]
    head_size = width // heads
    share = out_refs[0].shape[0]
    keyvals = keys_ref[...].reshape(key_count, 2 * width)
    stats = jnp.zeros((tok_rows, LANES), F32)
    lane = lane_iota((tok_rows, LANES))
    tiles = [jnp.zeros((tok_rows, LANES), F32)] * (width // LANES)
    tile_lane = lane_iota((tok_rows, LANES))
    windows = []
    scores = []
    for h in range(heads):
        low = h * head_size // LANES * LANES
        high = min(width, -(-(h + 1) * head_size // LANES) * LANES)
        windows.append((low, high))
        chan = lane_iota((tok_rows, high - low)) + low
        inside = (chan >= h * head_size) & (chan < (h + 1) * head_size)
        query = query_ref[:, low:high]
        query = jnp.where(inside, query, jnp.zeros_like(query))
        scores.append(mul(query, keyvals[:, low:high], NT))
    for h, (low, high) in enumerate(windows):
        score = scores[h] * (1.0 / head_size**0.5)
        kept = jnp.concatenate([early_ref[h], late_ref[h]], axis=0)
        score = score + jnp.concatenate([kept, swapped_ref[h].astype(F32)], axis=1)
        top = jnp.max(score, axis=-1, keepdims=True)
        top_high = top.astype(BF16).astype(F32)
        top_low = (top - top_high).astype(BF16).astype(F32)
        expo = jnp.exp(score - (top_high + top_low))
        denom = jnp.sum(expo, axis=-1, keepdims=True)
        denom_high = denom.astype(BF16).astype(F32)
        stats = jnp.where(lane == h, top_high, stats)
        stats = jnp.where(lane == heads + h, top_low, stats)
        stats = jnp.where(lane == 2 * heads + h, denom_high, stats)
        stats = jnp.where(lane == 3 * heads + h, denom - denom_high, stats)
        mixed = mul(expo.astype(BF16), keyvals[:, width + low : width + high])
        for tile in range(low // LANES, high // LANES):
            chan = tile_lane + tile * LANES
            inside = (chan >= h * head_size) & (chan < (h + 1) * head_size)
            part = mixed[:, tile * LANES - low : (tile + 1) * LANES - low]
            tiles[tile] = jnp.where(inside, part, tiles[tile])
    for tile, values in enumerate(tiles):
        lanes = slice(tile * LANES, (tile + 1) * LANES)
        packet_ref[:, lanes] = values.astype(BF16)
    packet_ref[:, width:] = stats.astype(BF16)
    for k, out_ref in zip(far_first(groups), out_refs):
        start = pl.multiple_of((place_ref[9] ^ k) * share, share)
        out_ref[...] = packet_ref[pl.ds(start, share), :]
    wait_all(loads)


def merge_kernel(*refs, heads, groups):
    part_refs = refs[:groups]
    gate_ref, act_ref, w_out_ref, w_down_ref, out_ref = refs[groups:]
    share = part_refs[0].shape[0]
    col_count = out_ref.shape[0]
    width = w_out_ref.shape[0]
    head_size = width // heads
    chan_share = width // col_count
    stats = jnp.stack([part[:, width:] for part in part_refs]).astype(F32)
    top = stats + pltpu.roll(stats, LANES - heads, 2)
    denom = pltpu.roll(stats, LANES - 2 * heads, 2) + pltpu.roll(stats, LANES - 3 * heads, 2)
    is_head = lane_iota(stats.shape) < heads
    highest = jnp.max(top, axis=0, keepdims=True)
    scale = jnp.where(is_head, jnp.exp(jnp.where(is_head, top - highest, 0.0)), 0.0)
    total = jnp.sum(scale * denom, axis=0, keepdims=True)
    factor = scale / jnp.where(is_head[:1], total, 1.0)
    factor = factor.reshape(groups * share, LANES)
    factor_high = factor.astype(BF16)
    factor_low = (factor - factor_high.astype(F32)).astype(BF16)
    chan_head = lane_iota((LANES, width)) // head_size
    spread = jnp.where(
        chan_head == lax.broadcasted_iota(jnp.int32, (LANES, width), 0), 1.0, 0.0
    ).astype(BF16)
    wide = mul(factor_high, spread) + mul(factor_low, spread)
    wide = wide.reshape(groups, share, width)
    context = sum(part[:, :width].astype(F32) * wide[k] for k, part in enumerate(part_refs))
    gated = (context * gate_ref[...]).astype(BF16)
    updated = act_ref[...] + mul(gated, w_out_ref[...])
    token_out = updated.astype(BF16)
    token_down = mul(token_out, w_down_ref[...]).astype(BF16)
    for c in range(col_count):
        out_ref[c, :, :LANES] = token_down
        out_ref[c, :, LANES : LANES + chan_share] = token_out[
            :, c * chan_share : (c + 1) * chan_share
        ]


def final_kernel(atoms_ref, last_ref, token_ref, atom_ref, *, chan_share):
    col_count, share, _ = last_ref.shape
    tok_rows = col_count * share
    atom_count = atom_ref.shape[0]
    order = sorted(range(col_count), key=lambda c: (c % 2, c // 2))
    last = jnp.concatenate([last_ref[c] for c in order], axis=0)
    token_ref[...] = last[:, LANES : LANES + chan_share].astype(F32).T.astype(BF16)
    names = atoms_ref[atom_count:, :].astype(F32)
    token = lane_iota((LANES, tok_rows)).astype(F32)
    for k in range(atom_count // LANES):
        name = jnp.broadcast_to(names[k : k + 1, :], (LANES, LANES)).T
        name = jnp.concatenate([name] * (tok_rows // LANES), axis=1)
        hot = jnp.where(name == token, 1.0, 0.0).astype(BF16)
        rows = slice(k * LANES, (k + 1) * LANES)
        moved = atoms_ref[rows, :].astype(F32) + mul(hot, last[:, :LANES])
        atom_ref[rows, :] = moved.astype(BF16)


def body(
    atom_feat,
    atom_token,
    w_atom_qkv,
    w_atom_out,
    w_atom_up,
    pair_repr,
    w_bias,
    w_query,
    w_kv,
    w_gate,
    w_out,
    w_down,
):
    row_count = lax.axis_size("row")
    col_count = lax.axis_size("col")
    row_index = lax.axis_index("row")
    col_index = lax.axis_index("col")
    atom_count, channels = atom_feat.shape
    tok_rows, _, share, pair_width = pair_repr.shape
    key_count = row_count * share
    heads = w_bias.shape[1]
    width = w_query.shape[0]
    chan_share = width // col_count
    all_atoms = atom_count * row_count * col_count
    half = tok_rows // 2
    col_groups = col_count // 2
    side, group = col_index & 1, col_index >> 1
    out_share = half // col_groups
    shares = [
        col_index * share,
        (col_index ^ 1) * share,
        side * half,
        (1 - side) * half,
        side * half + group * out_share,
        row_index & 1,
        row_index,
        group,
        col_index,
        group * (2 * share),
        side,
    ]
    place = jnp.stack([col_index, row_index * tok_rows] + shares).astype(jnp.int32)
    edge_place = jnp.stack([col_index, row_index * (atom_count * col_count)] + shares)
    edge_place = edge_place.astype(jnp.int32)
    smem = pl.BlockSpec(memory_space=pltpu.SMEM)
    vmem = pl.BlockSpec(memory_space=pltpu.VMEM)
    hbm = pl.BlockSpec(memory_space=pltpu.HBM)
    unread = pl.BlockSpec(memory_space=pl.ANY)

    def swap(x, axis, step):
        return lax.ppermute(x, axis, [(i, i ^ step) for i in range(lax.axis_size(axis))])

    top = col_count // 2
    tokens = atom_token.reshape(atom_count // LANES, LANES)
    own = call(
        own_kernel,
        shape_of((atom_count + PAD_ROWS, channels), BF16),
        2,
        in_specs=[smem] + [hbm] * 2,
        out_specs=vmem,
        scratch_shapes=[
            pltpu.VMEM(tokens.shape, jnp.int32),
            pltpu.SemaphoreType.DMA((2,)),
        ],
    )(place, *in_hbm(atom_feat, tokens))
    far = swap(own, "col", top)

    def pair_bias(segments, after, weights):
        loads, parts = len(weights), len(segments)
        return call(
            functools.partial(bias_kernel, segments=segments, loads=loads),
            tuple(shape_of((heads, rows, key_count), F32) for _, _, rows, _ in segments)
            + tuple(shape_of(x.shape, x.dtype) for x in weights),
            14,
            in_specs=[smem, hbm, vmem, unread] + [hbm] * loads,
            out_specs=(vmem,) * (parts + loads),
            scratch_shapes=[
                pltpu.VMEM((rows,) + pair_repr.shape[1:], BF16) for _, _, rows, _ in segments
            ]
            + [pltpu.SemaphoreType.DMA((rows // chunk,)) for _, _, rows, chunk in segments]
            + [pltpu.SemaphoreType.DMA((max(loads, 1),))],
        )(place, *in_hbm(pair_repr, w_bias.T), after, *in_hbm(*weights))

    early = half * 5 // 8
    late = half - early
    (kept,) = pair_bias([(4, 0, early, early // 2)], own, ())
    packet = call(
        pack_kernel,
        shape_of((2, atom_count + PAD_ROWS, channels), BF16),
        2,
        in_specs=[vmem] * 2 + [unread],
        out_specs=vmem,
    )(own, far, kept)
    packets = [packet] + [swap(packet, "col", k) for k in range(1, top)]
    other, kept_late, *atom_weights = pair_bias(
        [(5, 0, half, half // 4), (4, early, late, late // 2)],
        packet,
        (w_atom_qkv, w_atom_out, w_atom_up),
    )
    sent, row_atoms, first, second = call(
        edge_kernel,
        (shape_of((heads, half, key_count), BF16), shape_of((col_count, atom_count + PAD_ROWS, channels), BF16))
        + (shape_of((HALO, channels), BF16),) * 2,
        4,
        in_specs=[smem] + [vmem] * (1 + top),
        out_specs=(vmem,) * 4,
    )(place, other, *packets)
    swapped = swap(sent, "col", 1)
    first = swap(first, "row", 1)
    pairs = [(i, ((i + 1) ^ 1) - 1) for i in range(1, row_count - 1)]
    second = lax.ppermute(second, "row", pairs)
    w_qkv, w_mix, w_up = atom_weights
    ctx, w_query, w_kv = call(
        inner_kernel,
        (
            shape_of((col_count * atom_count, channels), BF16),
            shape_of(w_query.shape, BF16),
            shape_of(w_kv.shape, BF16),
        ),
        12,
        in_specs=[vmem] * 2 + [hbm] * 2,
        out_specs=(vmem,) * 3,
        scratch_shapes=[
            pltpu.VMEM((col_count * atom_count, 3 * channels), BF16),
            pltpu.SemaphoreType.DMA((2,)),
        ],
    )(row_atoms, w_qkv, *in_hbm(w_query, w_kv))
    mine, half_normed, normed, act, my_atoms = call(
        functools.partial(pool_kernel, all_atoms=all_atoms),
        (
            shape_of((2, share, width), BF16),
            shape_of((half, width), BF16),
            shape_of((out_share, width), BF16),
            shape_of((out_share, width), F32),
            shape_of((atom_count + PAD_ROWS, channels), BF16),
        ),
        14,
        in_specs=[smem] + [vmem] * 7,
        out_specs=(vmem,) * 5,
        scratch_shapes=[
            pltpu.VMEM((half, width), F32),
            pltpu.VMEM((col_count, atom_count, channels), BF16),
        ],
    )(edge_place, row_atoms, ctx, first, second, w_qkv, w_mix, w_up)
    far_parts = [swap(mine, "row", k) for k in range(2, row_count, 2)]
    near_part = swap(mine, "row", 1)
    queries, gate, own_kv = call(
        query_kernel,
        (
            shape_of((half, width), BF16),
            shape_of((out_share, width), F32),
            shape_of((1, 2, share, 2 * width), BF16),
        ),
        8,
        in_specs=[vmem] * 5 + [hbm],
        out_specs=(vmem,) * 3,
        scratch_shapes=[pltpu.VMEM(w_gate.shape, BF16), pltpu.SemaphoreType.DMA],
    )(half_normed, normed, mine, w_query, w_kv, *in_hbm(w_gate))
    relayed = call(
        relay_kernel,
        (shape_of(mine.shape, BF16),) * len(far_parts),
        4,
        in_specs=[unread] + [vmem] * len(far_parts),
        out_specs=(vmem,) * len(far_parts),
    )(queries, *far_parts)
    key_parts = [near_part]
    for part in relayed:
        key_parts += [part, swap(part, "row", 1)]
    *parts, w_out, w_down = call(
        functools.partial(token_kernel, row_count=row_count, groups=col_groups),
        tuple(shape_of((out_share, width + LANES), BF16) for _ in range(col_groups))
        + (shape_of(w_out.shape, BF16), shape_of(w_down.shape, BF16)),
        14,
        in_specs=[smem] + [vmem] * (5 + row_count) + [hbm] * 2,
        out_specs=(vmem,) * (col_groups + 2),
        scratch_shapes=[
            pltpu.VMEM((2, row_count, share, 2 * width), BF16),
            pltpu.VMEM((row_count - 1, 2, share, 2 * width), BF16),
            pltpu.VMEM((half, width + LANES), BF16),
            pltpu.SemaphoreType.DMA((2,)),
        ],
    )(place, queries, w_kv, kept, kept_late, swapped, own_kv, *key_parts, *in_hbm(w_out, w_down))
    parts = parts[:1] + [
        lax.ppermute(part, "col", [(c, c ^ (2 * k)) for c in range(col_count)])
        for k, part in zip(far_first(col_groups), parts)
        if k > 0
    ]
    last = call(
        functools.partial(merge_kernel, heads=heads, groups=col_groups),
        shape_of((col_count, out_share, 2 * LANES), BF16),
        8,
        in_specs=[vmem] * (col_groups + 4),
        out_specs=vmem,
    )(*parts, gate, act, w_out, w_down)
    last = lax.all_to_all(last, "col", 0, 0)
    token_share, atom_final = call(
        functools.partial(final_kernel, chan_share=chan_share),
        (shape_of((chan_share, tok_rows), BF16), shape_of((atom_count, channels), BF16)),
        4,
        in_specs=[vmem] * 2,
        out_specs=(vmem,) * 2,
    )(my_atoms, last)
    return (token_share.T, atom_final)


def solution(mesh):
    return jax.shard_map(
        body,
        mesh=mesh,
        in_specs=(
            P(("row", "col"), None),
            P(("row", "col")),
            P(),
            P(),
            P(),
            P("row", None, "col", None),
            P(),
            P(),
            P(),
            P(),
            P(),
            P(),
        ),
        out_specs=(P("row", "col"), P(("row", "col"), None)),
        check_vma=False,
    )
```

```python
import functools

import jax
import jax.numpy as jnp
from jax import lax
from jax.experimental import pallas as pl
from jax.experimental.pallas import tpu as pltpu
from jax.sharding import PartitionSpec as P

AHEADS = 4
QBLOCK = 32
KWIN = 128
HALO = 48
LANES = 128
PAD_ROWS = 16
EDGE_BLOCKS = 2
EPS = 1e-05
LOG2_E = 1.4426950408889634
F32 = jnp.float32
BF16 = jnp.bfloat16
MIB = 1024 * 1024

NT = (((1,), (1,)), ((), ()))
NN = (((1,), (0,)), ((), ()))
TN = (((0,), (0,)), ((), ()))


def mul(a, b, dims=NN):
    return lax.dot_general(a, b, dims, preferred_element_type=F32)


def call(kernel, out_shape, vmem_mib, **kwargs):
    return pl.pallas_call(
        kernel,
        out_shape=out_shape,
        compiler_params=pltpu.CompilerParams(vmem_limit_bytes=vmem_mib * MIB),
        **kwargs,
    )


def shape_of(shape, dtype):
    return jax.ShapeDtypeStruct(shape, dtype)


def far_first(count):
    return [0] + list(range(count - 1, 0, -1))


def lane_iota(shape):
    return lax.broadcasted_iota(jnp.int32, shape, len(shape) - 1)


def in_hbm(*arrays):
    return tuple(pltpu.with_memory_space_constraint(x, pltpu.HBM) for x in arrays)


def load_all(sources, targets, sems):
    copies = [
        pltpu.make_async_copy(source, target, sems.at[i])
        for i, (source, target) in enumerate(zip(sources, targets))
    ]
    for copy in copies:
        copy.start()
    return copies


def wait_all(copies):
    for copy in copies:
        copy.wait()


def pack_kernel(place_ref, own_ref, token_ref, far_ref, far_token_ref, after_ref, out_ref):
    del after_ref
    atom_count = own_ref.shape[0]
    token_rows = token_ref.shape[0]
    blank = jnp.zeros((PAD_ROWS - token_rows, LANES), F32)
    for k, (feat, token) in enumerate(((own_ref, token_ref), (far_ref, far_token_ref))):
        out_ref[k, :atom_count, :] = feat[...]
        names = (token[...] - place_ref[1]).astype(F32)
        out_ref[k, atom_count:, :] = jnp.concatenate([names, blank], axis=0).astype(BF16)


def edge_kernel(place_ref, bias_ref, *refs):
    packets, (sent_ref, atoms_ref, first_ref, second_ref) = refs[:-4], refs[-4:]
    sent_ref[...] = bias_ref[...].astype(BF16)
    col_count, packet_rows, _ = atoms_ref.shape
    atom_count = packet_rows - PAD_ROWS
    for k, packet in enumerate(packets):
        for j in range(2):
            atoms_ref[place_ref[10] ^ (k + j * (col_count // 2))] = packet[j]
    tail = atoms_ref[col_count - 1, atom_count - HALO : atom_count, :]
    head = atoms_ref[0, :HALO, :]
    even = place_ref[7] == 0
    first_ref[...] = jnp.where(even, tail, head)
    second_ref[...] = jnp.where(even, head, tail)


def attend(query_of, union_of, blocks, valid_of=None):
    channels = query_of(0).shape[1]
    head_size = channels // AHEADS
    rows_of = AHEADS * QBLOCK
    head_of = lane_iota((QBLOCK, channels)) // head_size
    picks = [head_of == h for h in range(AHEADS)]
    scores = []
    for b in range(0, blocks, 2):
        stacked = []
        for query in (query_of(b), query_of(b + 1)):
            stacked += [jnp.where(pick, query, jnp.zeros_like(query)) for pick in picks]
        found = mul(union_of(b, 1), jnp.concatenate(stacked, axis=0), NT)
        scores += [found[:KWIN, :rows_of], found[QBLOCK:, rows_of:]]
    blank = jnp.zeros((KWIN, channels), BF16)
    row = lax.broadcasted_iota(jnp.int32, (PAD_ROWS, channels), 0)
    pair_rows = jnp.where(row < 2, 1.0, 0.0).astype(BF16)
    sum_rows = jnp.concatenate([blank[:PAD_ROWS], pair_rows], axis=1)
    contexts = []
    for b in range(blocks):
        score = scores[b]
        if valid_of is not None:
            score = jnp.where(valid_of(b, score.shape), score, -1e30)
        score = score - jnp.max(score, axis=0, keepdims=True)
        expo = jnp.exp2(score * (LOG2_E / head_size**0.5))
        denom = jnp.sum(expo, axis=0, keepdims=True)
        denom_high = denom.astype(BF16).astype(F32)
        sums = jnp.where(row == 0, denom_high, jnp.where(row == 1, denom - denom_high, 0.0))
        weights = jnp.concatenate([expo.astype(BF16), sums.astype(BF16)], axis=0)
        start = b % 2 * QBLOCK
        values = union_of(b - b % 2, 2)[start : start + KWIN]
        values = jnp.concatenate([values, blank], axis=1)
        mixed = mul(weights, jnp.concatenate([values, sum_rows], axis=0), TN)
        context = mixed[:QBLOCK]
        for h in range(1, AHEADS):
            pick = jnp.concatenate([picks[h]] * 2, axis=1)
            context = jnp.where(pick, mixed[h * QBLOCK : (h + 1) * QBLOCK], context)
        contexts.append((context[:, :channels] / context[:, channels:]).astype(BF16))
    return contexts


def inner_kernel(
    atoms_ref, w_qkv_ref, w_query_hbm, w_kv_hbm, ctx_ref, w_query_ref, w_kv_ref, proj_ref, sems
):
    loads = load_all((w_query_hbm, w_kv_hbm), (w_query_ref, w_kv_ref), sems)
    col_count, packet_rows, channels = atoms_ref.shape
    atom_count = packet_rows - PAD_ROWS
    row_atoms = col_count * atom_count
    blocks = row_atoms // QBLOCK - 2 * EDGE_BLOCKS
    step_blocks = max(n for n in range(2, 31, 2) if blocks % n == 0)
    edge = EDGE_BLOCKS * QBLOCK
    for c in range(col_count):
        proj = mul(atoms_ref[c, :atom_count, :], w_qkv_ref[...])
        proj_ref[c * atom_count : (c + 1) * atom_count, :] = proj.astype(BF16)
    ctx_ref[:edge, :] = jnp.zeros((edge, channels), BF16)
    ctx_ref[row_atoms - edge :, :] = jnp.zeros((edge, channels), BF16)

    def step(i, carry):
        first = i * (step_blocks * QBLOCK) + edge

        def query_of(b):
            start = pl.multiple_of(first + b * QBLOCK, QBLOCK)
            return proj_ref[pl.ds(start, QBLOCK), :channels]

        def union_of(b, part):
            start = pl.multiple_of(first + b * QBLOCK - HALO, PAD_ROWS)
            return proj_ref[
                pl.ds(start, KWIN + QBLOCK), part * channels : (part + 1) * channels
            ]

        for b, context in enumerate(attend(query_of, union_of, step_blocks)):
            ctx_ref[pl.ds(pl.multiple_of(first + b * QBLOCK, QBLOCK), QBLOCK), :] = context
        return carry

    lax.fori_loop(0, blocks // step_blocks, step, 0)
    wait_all(loads)


def bias_kernel(place_ref, pair_ref, w_ref, after_ref, *refs, segments, loads):
    del after_ref
    parts = len(segments)
    sources, outs, targets = refs[:loads], refs[loads : loads + parts], refs[loads + parts :][:loads]
    refs = refs[2 * loads + parts :]
    cells_refs, sems, load_sems = refs[:parts], refs[parts : 2 * parts], refs[2 * parts]
    _, rows, share, width = cells_refs[0].shape
    keys = rows * share
    heads = w_ref.shape[0]

    def load(s, i):
        place, offset, _, chunk = segments[s]
        start = i * chunk
        return pltpu.make_async_copy(
            pair_ref.at[pl.ds(place_ref[place] + offset + start, chunk)],
            cells_refs[s].at[pl.ds(start, chunk)],
            sems[s].at[i],
        )

    def load_segment(s):
        for i in range(segments[s][2] // segments[s][3]):
            load(s, i).start()

    load_segment(0)
    extra = load_all(sources, targets, load_sems)
    weights = w_ref[...].astype(BF16)
    weight_sum = jnp.sum(weights.astype(F32), axis=1, keepdims=True)
    mean_of = jnp.full((heads, width), 1.0 / width, BF16)
    left = jnp.concatenate([weights, mean_of], axis=0)

    def run(s):
        chunk = segments[s][3]

        def step(i, carry):
            load(s, i).wait()
            if s + 1 < parts:

                @pl.when(i == 0)
                def _():
                    load_segment(s + 1)

            start = pl.multiple_of(i * chunk, chunk)
            for q in range(chunk):
                cells = cells_refs[s][start + q].reshape(keys, width).T
                values = cells.astype(F32)
                found = mul(left, cells)
                dots, center = found[:heads], found[heads:]
                spread = jnp.sum(values * values, axis=0, keepdims=True) * (1.0 / width)
                spread = spread - center * center
                bias = (dots - center * weight_sum) * lax.rsqrt(spread + EPS)
                outs[s][:, start + q, :] = bias.astype(BF16).astype(F32)
            return carry

        lax.fori_loop(0, segments[s][2] // chunk, step, 0)

    for s in range(parts):
        run(s)
    wait_all(extra)


def pool_kernel(
    place_ref,
    atoms_ref,
    ctx_ref,
    first_ref,
    second_ref,
    w_qkv_ref,
    w_out_ref,
    w_up_ref,
    mine_ref,
    half_ref,
    normed_out_ref,
    act_out_ref,
    my_ref,
    act_ref,
    atom_out_ref,
    *,
    all_atoms,
):
    col_count, packet_rows, channels = atoms_ref.shape
    atom_count = packet_rows - PAD_ROWS
    row_atoms = col_count * atom_count
    half, width = half_ref.shape
    slices, share = mine_ref.shape[:2]
    edge = EDGE_BLOCKS * QBLOCK
    near = edge + HALO
    begin = atoms_ref[0, :near, :]
    end = atoms_ref[col_count - 1, atom_count - near : atom_count, :]
    even = place_ref[7] == 0
    before = jnp.where(even, second_ref[...], first_ref[...])
    after = jnp.where(even, first_ref[...], second_ref[...])
    contexts = []
    for wide, base in (
        (jnp.concatenate([before, begin], axis=0), -HALO),
        (jnp.concatenate([end, after], axis=0), row_atoms - near),
    ):
        proj = mul(wide, w_qkv_ref[...]).astype(BF16)

        def query_of(b):
            return proj[HALO + b * QBLOCK : HALO + (b + 1) * QBLOCK, :channels]

        def union_of(b, part):
            return proj[
                b * QBLOCK : b * QBLOCK + KWIN + QBLOCK, part * channels : (part + 1) * channels
            ]

        def valid_of(b, shape):
            position = place_ref[1] + (base + b * QBLOCK)
            position = position + lax.broadcasted_iota(jnp.int32, shape, 0)
            return (position >= 0) & (position < all_atoms)

        contexts.append(jnp.concatenate(attend(query_of, union_of, EDGE_BLOCKS, valid_of), axis=0))
    rows = half + slices * share
    row = lax.broadcasted_iota(jnp.int32, (rows, LANES), 0)
    token = row + jnp.where(row < half, place_ref[4], place_ref[11] - half)
    token = token.astype(F32)
    counts = jnp.zeros((rows, LANES), F32)
    totals = jnp.zeros((rows, width), F32)
    for c in [*range(1, col_count - 1), 0, col_count - 1]:
        start = c * atom_count
        ctx = ctx_ref[start : start + atom_count, :]
        if c == 0:
            ctx = jnp.concatenate([contexts[0], ctx[edge:]], axis=0)
        if c == col_count - 1:
            ctx = jnp.concatenate([ctx[: atom_count - edge], contexts[1]], axis=0)
        atom_out = atoms_ref[c, :atom_count, :].astype(F32) + mul(ctx, w_out_ref[...])
        atom_out = atom_out.astype(BF16)
        atom_out_ref[c] = atom_out
        up = jnp.maximum(mul(atom_out, w_up_ref[...]), 0.0).astype(BF16)
        names = atoms_ref[c, atom_count:, :].astype(F32)
        hots = []
        for k in range(atom_count // LANES):
            hot = jnp.where(names[k : k + 1, :] == token, 1.0, 0.0)
            counts = counts + hot
            hots.append(hot.astype(BF16))
        totals = totals + mul(jnp.concatenate(hots, axis=1), up)
    token_act = totals / jnp.sum(counts, axis=-1, keepdims=True)
    center = jnp.sum(token_act, axis=-1, keepdims=True) * (1.0 / width)
    spread = jnp.sum(token_act * token_act, axis=-1, keepdims=True) * (1.0 / width)
    spread = spread - center * center
    normed = ((token_act - center) / jnp.sqrt(spread + EPS)).astype(BF16)
    side = place_ref[12]
    for k in range(slices):
        part = normed[half + k * share : half + (k + 1) * share]
        other = normed[half + (1 - k) * share : half + (2 - k) * share]
        mine_ref[k] = jnp.where(side == 0, part, other)
    half_ref[...] = normed[:half]
    act_ref[...] = token_act[:half]
    out_share = act_out_ref.shape[0]
    start = pl.multiple_of(place_ref[9] * out_share, out_share)
    normed_out_ref[...] = half_ref[pl.ds(start, out_share), :]
    act_out_ref[...] = act_ref[pl.ds(start, out_share), :]
    col = place_ref[10]
    my_ref[:atom_count, :] = atom_out_ref[col]
    my_ref[atom_count:, :] = atoms_ref[col, atom_count:, :]


def relay_kernel(after_ref, *refs):
    del after_ref
    count = len(refs) // 2
    for source, target in zip(refs[:count], refs[count:]):
        target[...] = source[...]


def query_kernel(
    half_ref, normed_ref, mine_ref, w_query_ref, w_kv_ref, w_gate_hbm, *refs
):
    query_ref, gate_ref, own_kv_ref, w_gate_ref, sem = refs
    load = pltpu.make_async_copy(w_gate_hbm, w_gate_ref, sem)
    load.start()
    query_ref[...] = mul(half_ref[...], w_query_ref[...]).astype(BF16)
    project((mine_ref,), w_kv_ref, own_kv_ref)
    load.wait()
    gate_ref[...] = jax.nn.sigmoid(mul(normed_ref[...], w_gate_ref[...]))


def project(parts, w_kv_ref, out_ref):
    slices, share, width = parts[0].shape
    rows = [part[...].reshape(slices * share, width) for part in parts]
    found = mul(jnp.concatenate(rows, axis=0), w_kv_ref[...]).astype(BF16)
    out_ref[...] = found.reshape(len(parts), slices, share, found.shape[1])


def token_kernel(
    place_ref, query_ref, w_kv_ref, early_ref, late_ref, swapped_ref, *refs, row_count, groups
):
    own_kv_ref, parts, refs = refs[0], refs[1:row_count], refs[row_count:]
    w_out_hbm, w_down_hbm, *refs = refs
    out_refs, refs = refs[:groups], refs[groups:]
    w_out_ref, w_down_ref, keys_ref, other_kv_ref, packet_ref, sems = refs
    loads = load_all((w_out_hbm, w_down_hbm), (w_out_ref, w_down_ref), sems)
    project(parts, w_kv_ref, other_kv_ref)
    for k in range(row_count):
        found = other_kv_ref.at[k - 1] if k else own_kv_ref.at[k]
        for i in range(2):
            keys_ref[i, place_ref[8] ^ k] = found[i]
    heads, tok_rows, part_keys = swapped_ref.shape
    key_count = 2 * part_keys
    width = query_ref.shape[1]
    head_size = width // heads
    share = out_refs[0].shape[0]
    keyvals = keys_ref[...].reshape(key_count, 2 * width)
    stats = jnp.zeros((tok_rows, LANES), F32)
    lane = lane_iota((tok_rows, LANES))
    tiles = [jnp.zeros((tok_rows, LANES), F32)] * (width // LANES)
    tile_lane = lane_iota((tok_rows, LANES))
    windows = []
    scores = []
    for h in range(heads):
        low = h * head_size // LANES * LANES
        high = min(width, -(-(h + 1) * head_size // LANES) * LANES)
        windows.append((low, high))
        chan = lane_iota((tok_rows, high - low)) + low
        inside = (chan >= h * head_size) & (chan < (h + 1) * head_size)
        query = query_ref[:, low:high]
        query = jnp.where(inside, query, jnp.zeros_like(query))
        scores.append(mul(query, keyvals[:, low:high], NT))
    for h, (low, high) in enumerate(windows):
        score = scores[h] * (1.0 / head_size**0.5)
        kept = jnp.concatenate([early_ref[h], late_ref[h]], axis=0)
        score = score + jnp.concatenate([kept, swapped_ref[h].astype(F32)], axis=1)
        top = jnp.max(score, axis=-1, keepdims=True)
        top_high = top.astype(BF16).astype(F32)
        top_low = (top - top_high).astype(BF16).astype(F32)
        expo = jnp.exp(score - (top_high + top_low))
        denom = jnp.sum(expo, axis=-1, keepdims=True)
        denom_high = denom.astype(BF16).astype(F32)
        stats = jnp.where(lane == h, top_high, stats)
        stats = jnp.where(lane == heads + h, top_low, stats)
        stats = jnp.where(lane == 2 * heads + h, denom_high, stats)
        stats = jnp.where(lane == 3 * heads + h, denom - denom_high, stats)
        mixed = mul(expo.astype(BF16), keyvals[:, width + low : width + high])
        for tile in range(low // LANES, high // LANES):
            chan = tile_lane + tile * LANES
            inside = (chan >= h * head_size) & (chan < (h + 1) * head_size)
            part = mixed[:, tile * LANES - low : (tile + 1) * LANES - low]
            tiles[tile] = jnp.where(inside, part, tiles[tile])
    for tile, values in enumerate(tiles):
        lanes = slice(tile * LANES, (tile + 1) * LANES)
        packet_ref[:, lanes] = values.astype(BF16)
    packet_ref[:, width:] = stats.astype(BF16)
    for k, out_ref in zip(far_first(groups), out_refs):
        start = pl.multiple_of((place_ref[9] ^ k) * share, share)
        out_ref[...] = packet_ref[pl.ds(start, share), :]
    wait_all(loads)


def merge_kernel(*refs, heads, groups):
    part_refs = refs[:groups]
    gate_ref, act_ref, w_out_ref, w_down_ref, out_ref = refs[groups:]
    share = part_refs[0].shape[0]
    col_count = out_ref.shape[0]
    width = w_out_ref.shape[0]
    head_size = width // heads
    chan_share = width // col_count
    stats = jnp.stack([part[:, width:] for part in part_refs]).astype(F32)
    top = stats + pltpu.roll(stats, LANES - heads, 2)
    denom = pltpu.roll(stats, LANES - 2 * heads, 2) + pltpu.roll(stats, LANES - 3 * heads, 2)
    is_head = lane_iota(stats.shape) < heads
    highest = jnp.max(top, axis=0, keepdims=True)
    scale = jnp.where(is_head, jnp.exp(jnp.where(is_head, top - highest, 0.0)), 0.0)
    total = jnp.sum(scale * denom, axis=0, keepdims=True)
    factor = scale / jnp.where(is_head[:1], total, 1.0)
    factor = factor.reshape(groups * share, LANES)
    factor_high = factor.astype(BF16)
    factor_low = (factor - factor_high.astype(F32)).astype(BF16)
    chan_head = lane_iota((LANES, width)) // head_size
    spread = jnp.where(
        chan_head == lax.broadcasted_iota(jnp.int32, (LANES, width), 0), 1.0, 0.0
    ).astype(BF16)
    wide = mul(factor_high, spread) + mul(factor_low, spread)
    wide = wide.reshape(groups, share, width)
    context = sum(part[:, :width].astype(F32) * wide[k] for k, part in enumerate(part_refs))
    gated = (context * gate_ref[...]).astype(BF16)
    updated = act_ref[...] + mul(gated, w_out_ref[...])
    token_out = updated.astype(BF16)
    token_down = mul(token_out, w_down_ref[...]).astype(BF16)
    for c in range(col_count):
        out_ref[c, :, :LANES] = token_down
        out_ref[c, :, LANES : LANES + chan_share] = token_out[
            :, c * chan_share : (c + 1) * chan_share
        ]


def final_kernel(atoms_ref, last_ref, token_ref, atom_ref, *, chan_share):
    col_count, share, _ = last_ref.shape
    tok_rows = col_count * share
    atom_count = atom_ref.shape[0]
    order = sorted(range(col_count), key=lambda c: (c % 2, c // 2))
    last = jnp.concatenate([last_ref[c] for c in order], axis=0)
    token_ref[...] = last[:, LANES : LANES + chan_share].astype(F32).T.astype(BF16)
    names = atoms_ref[atom_count:, :].astype(F32)
    token = lane_iota((LANES, tok_rows)).astype(F32)
    for k in range(atom_count // LANES):
        name = jnp.broadcast_to(names[k : k + 1, :], (LANES, LANES)).T
        name = jnp.concatenate([name] * (tok_rows // LANES), axis=1)
        hot = jnp.where(name == token, 1.0, 0.0).astype(BF16)
        rows = slice(k * LANES, (k + 1) * LANES)
        moved = atoms_ref[rows, :].astype(F32) + mul(hot, last[:, :LANES])
        atom_ref[rows, :] = moved.astype(BF16)


def body(
    atom_feat,
    atom_token,
    w_atom_qkv,
    w_atom_out,
    w_atom_up,
    pair_repr,
    w_bias,
    w_query,
    w_kv,
    w_gate,
    w_out,
    w_down,
):
    row_count = lax.axis_size("row")
    col_count = lax.axis_size("col")
    row_index = lax.axis_index("row")
    col_index = lax.axis_index("col")
    atom_count, channels = atom_feat.shape
    tok_rows, _, share, pair_width = pair_repr.shape
    key_count = row_count * share
    heads = w_bias.shape[1]
    width = w_query.shape[0]
    chan_share = width // col_count
    all_atoms = atom_count * row_count * col_count
    half = tok_rows // 2
    col_groups = col_count // 2
    side, group = col_index & 1, col_index >> 1
    out_share = half // col_groups
    shares = [
        col_index * share,
        (col_index ^ 1) * share,
        side * half,
        (1 - side) * half,
        side * half + group * out_share,
        row_index & 1,
        row_index,
        group,
        col_index,
        group * (2 * share),
        side,
    ]
    place = jnp.stack([col_index, row_index * tok_rows] + shares).astype(jnp.int32)
    edge_place = jnp.stack([col_index, row_index * (atom_count * col_count)] + shares)
    edge_place = edge_place.astype(jnp.int32)
    smem = pl.BlockSpec(memory_space=pltpu.SMEM)
    vmem = pl.BlockSpec(memory_space=pltpu.VMEM)
    hbm = pl.BlockSpec(memory_space=pltpu.HBM)
    unread = pl.BlockSpec(memory_space=pl.ANY)

    def swap(x, axis, step):
        return lax.ppermute(x, axis, [(i, i ^ step) for i in range(lax.axis_size(axis))])

    top = col_count // 2
    far = swap(atom_feat, "col", top)
    far_tokens = swap(atom_token, "col", top)
    token_shape = (atom_count // LANES, LANES)
    tokens, far_tokens = atom_token.reshape(token_shape), far_tokens.reshape(token_shape)

    def pair_bias(segments, after, weights):
        loads, parts = len(weights), len(segments)
        return call(
            functools.partial(bias_kernel, segments=segments, loads=loads),
            tuple(shape_of((heads, rows, key_count), F32) for _, _, rows, _ in segments)
            + tuple(shape_of(x.shape, x.dtype) for x in weights),
            14,
            in_specs=[smem, hbm, vmem, unread] + [hbm] * loads,
            out_specs=(vmem,) * (parts + loads),
            scratch_shapes=[
                pltpu.VMEM((rows,) + pair_repr.shape[1:], BF16) for _, _, rows, _ in segments
            ]
            + [pltpu.SemaphoreType.DMA((rows // chunk,)) for _, _, rows, chunk in segments]
            + [pltpu.SemaphoreType.DMA((loads,))],
        )(place, *in_hbm(pair_repr, w_bias.T), after, *in_hbm(*weights))

    early = half * 5 // 8
    late = half - early
    kept, own, own_tokens = pair_bias([(4, 0, early, early // 2)], place, (atom_feat, tokens))
    packet = call(
        pack_kernel,
        shape_of((2, atom_count + PAD_ROWS, channels), BF16),
        2,
        in_specs=[smem] + [vmem] * 4 + [unread],
        out_specs=vmem,
    )(place, own, own_tokens, far, far_tokens, kept)
    packets = [packet] + [swap(packet, "col", k) for k in range(1, top)]
    other, kept_late, *atom_weights = pair_bias(
        [(5, 0, half, half // 4), (4, early, late, late // 2)],
        packet,
        (w_atom_qkv, w_atom_out, w_atom_up),
    )
    sent, row_atoms, first, second = call(
        edge_kernel,
        (shape_of((heads, half, key_count), BF16), shape_of((col_count, atom_count + PAD_ROWS, channels), BF16))
        + (shape_of((HALO, channels), BF16),) * 2,
        4,
        in_specs=[smem] + [vmem] * (1 + top),
        out_specs=(vmem,) * 4,
    )(place, other, *packets)
    swapped = swap(sent, "col", 1)
    first = swap(first, "row", 1)
    pairs = [(i, ((i + 1) ^ 1) - 1) for i in range(1, row_count - 1)]
    second = lax.ppermute(second, "row", pairs)
    w_qkv, w_mix, w_up = atom_weights
    ctx, w_query, w_kv = call(
        inner_kernel,
        (
            shape_of((col_count * atom_count, channels), BF16),
            shape_of(w_query.shape, BF16),
            shape_of(w_kv.shape, BF16),
        ),
        12,
        in_specs=[vmem] * 2 + [hbm] * 2,
        out_specs=(vmem,) * 3,
        scratch_shapes=[
            pltpu.VMEM((col_count * atom_count, 3 * channels), BF16),
            pltpu.SemaphoreType.DMA((2,)),
        ],
    )(row_atoms, w_qkv, *in_hbm(w_query, w_kv))
    mine, half_normed, normed, act, my_atoms = call(
        functools.partial(pool_kernel, all_atoms=all_atoms),
        (
            shape_of((2, share, width), BF16),
            shape_of((half, width), BF16),
            shape_of((out_share, width), BF16),
            shape_of((out_share, width), F32),
            shape_of((atom_count + PAD_ROWS, channels), BF16),
        ),
        14,
        in_specs=[smem] + [vmem] * 7,
        out_specs=(vmem,) * 5,
        scratch_shapes=[
            pltpu.VMEM((half, width), F32),
            pltpu.VMEM((col_count, atom_count, channels), BF16),
        ],
    )(edge_place, row_atoms, ctx, first, second, w_qkv, w_mix, w_up)
    far_parts = [swap(mine, "row", k) for k in range(2, row_count, 2)]
    near_part = swap(mine, "row", 1)
    queries, gate, own_kv = call(
        query_kernel,
        (
            shape_of((half, width), BF16),
            shape_of((out_share, width), F32),
            shape_of((1, 2, share, 2 * width), BF16),
        ),
        8,
        in_specs=[vmem] * 5 + [hbm],
        out_specs=(vmem,) * 3,
        scratch_shapes=[pltpu.VMEM(w_gate.shape, BF16), pltpu.SemaphoreType.DMA],
    )(half_normed, normed, mine, w_query, w_kv, *in_hbm(w_gate))
    relayed = call(
        relay_kernel,
        (shape_of(mine.shape, BF16),) * len(far_parts),
        4,
        in_specs=[unread] + [vmem] * len(far_parts),
        out_specs=(vmem,) * len(far_parts),
    )(queries, *far_parts)
    key_parts = [near_part]
    for part in relayed:
        key_parts += [part, swap(part, "row", 1)]
    *parts, w_out, w_down = call(
        functools.partial(token_kernel, row_count=row_count, groups=col_groups),
        tuple(shape_of((out_share, width + LANES), BF16) for _ in range(col_groups))
        + (shape_of(w_out.shape, BF16), shape_of(w_down.shape, BF16)),
        14,
        in_specs=[smem] + [vmem] * (5 + row_count) + [hbm] * 2,
        out_specs=(vmem,) * (col_groups + 2),
        scratch_shapes=[
            pltpu.VMEM((2, row_count, share, 2 * width), BF16),
            pltpu.VMEM((row_count - 1, 2, share, 2 * width), BF16),
            pltpu.VMEM((half, width + LANES), BF16),
            pltpu.SemaphoreType.DMA((2,)),
        ],
    )(place, queries, w_kv, kept, kept_late, swapped, own_kv, *key_parts, *in_hbm(w_out, w_down))
    parts = parts[:1] + [
        lax.ppermute(part, "col", [(c, c ^ (2 * k)) for c in range(col_count)])
        for k, part in zip(far_first(col_groups), parts)
        if k > 0
    ]
    last = call(
        functools.partial(merge_kernel, heads=heads, groups=col_groups),
        shape_of((col_count, out_share, 2 * LANES), BF16),
        8,
        in_specs=[vmem] * (col_groups + 4),
        out_specs=vmem,
    )(*parts, gate, act, w_out, w_down)
    last = lax.all_to_all(last, "col", 0, 0)
    token_share, atom_final = call(
        functools.partial(final_kernel, chan_share=chan_share),
        (shape_of((chan_share, tok_rows), BF16), shape_of((atom_count, channels), BF16)),
        4,
        in_specs=[vmem] * 2,
        out_specs=(vmem,) * 2,
    )(my_atoms, last)
    return (token_share.T, atom_final)


def solution(mesh):
    return jax.shard_map(
        body,
        mesh=mesh,
        in_specs=(
            P(("row", "col"), None),
            P(("row", "col")),
            P(),
            P(),
            P(),
            P("row", None, "col", None),
            P(),
            P(),
            P(),
            P(),
            P(),
            P(),
        ),
        out_specs=(P("row", "col"), P(("row", "col"), None)),
        check_vma=False,
    )
```
